256 devices in a mesh: cols: 32 (over y, x, core), rows: 8 (over z).
Axes of the slice: x: 4, y: 4, z: 8, core: 2. Of those that a mesh axis runs over, the one named last changes fastest.
Arguments:
- latent: bfloat16 [64, 2048, 256], P('rows', 'cols'), may hold values from -6 to 6
- cotangent: bfloat16 [128, 4096, 256], P('rows', 'cols'), may hold values from -12 to 12
- pixel_mask: int32 [128, 4096], P('rows', 'cols'), may hold values 0 or 1
- res_kernels: bfloat16 [6, 3, 3, 256, 256], replicated, may hold values from -0.125 to 0.125
- up_kernel: bfloat16 [3, 3, 256, 256], replicated, may hold values from -0.125 to 0.125
Outputs:
- latent_grad: float32 [64, 2048, 256], P('rows', 'cols')
The draws below stay inside these ranges and needn't reach their ends.
All inputs are finite; a program needn't handle non-finite values. No bound on the sum of `pixel_mask` on one device may be relied on, other than what follows from the above.
Results may differ from the reference program's by a relative error of at most 0.014.
Values may be sent and summed in bfloat16 or wider, within the bound.
A program may use at most 128 MiB of HBM per device.

```python
import math
import jax
import jax.numpy as jnp
from jax import lax

CHANNELS = 256
GROUPS = 32
LAYERS = 3
LAT_H = 64
LAT_W = 2048


def draw_latent(key, part):
    key = jax.random.fold_in(key, 11)
    keys = jax.random.split(key, 8)
    row_pos = jnp.arange(LAT_H, dtype=jnp.float32) / max(LAT_H - 1, 1)
    col_pos = jnp.arange(LAT_W, dtype=jnp.float32) / max(LAT_W - 1, 1)
    channel_scale = jnp.exp(jax.random.uniform(keys[1], (CHANNELS,), jnp.float32, -math.log(2.0), math.log(2.0)))
    channel_shift = jax.random.uniform(keys[2], (CHANNELS,), jnp.float32, -1.0, 1.0)
    loading = jax.random.uniform(keys[5], (CHANNELS,), jnp.float32, 0.5, 1.5)
    phases = jax.random.uniform(keys[6], (3,), jnp.float32, 0.0, 2.0 * math.pi)
    row_wave = jnp.cos(2.0 * math.pi * 1.5 * row_pos + phases[0])
    col_wave = jnp.cos(2.0 * math.pi * 3.0 * col_pos + phases[1]) + 0.5 * jnp.cos(2.0 * math.pi * 7.0 * col_pos + phases[2])
    base = jax.random.normal(keys[0], (LAT_H, LAT_W, CHANNELS), jnp.float32)
    row_scale = 1.0 + row_pos
    col_scale = 1.0 + 2.0 * col_pos
    common_rough = jnp.clip(jax.random.normal(keys[7], (LAT_H, LAT_W), jnp.float32), -6.0, 6.0)
    smooth = 0.45 * row_wave[:, None] * col_wave[None, :]
    amplitude = 0.12
    values = amplitude * base * row_scale[:, None, None] * col_scale[None, :, None] * channel_scale[None, None, :]
    values = values + 0.15 * channel_shift[None, None, :] * (2.0 * col_pos[None, :, None] - 1.0)
    values = values + loading[None, None, :] * (0.3 * common_rough + smooth)[:, :, None]
    return jnp.clip(values, -6.0, 6.0).astype(jnp.bfloat16)


def draw_cotangent(key, part):
    key = jax.random.fold_in(key, 23)
    keys = jax.random.split(key, 2)
    fine_rows = 2 * LAT_H
    fine_cols = 2 * LAT_W
    col_pos = jnp.arange(fine_cols, dtype=jnp.float32) / max(fine_cols - 1, 1)
    level = jax.random.uniform(keys[1], (CHANNELS,), jnp.float32, -1.0, 1.0)
    ramp = 0.5 + 1.5 * col_pos
    noise = jnp.clip(jax.random.normal(keys[0], (fine_rows, fine_cols, CHANNELS), jnp.float32), -6.0, 6.0)
    offset = level[None, None, :] * ramp[None, :, None] * jnp.ones((fine_rows, 1, 1), jnp.float32)
    return jnp.clip(noise + offset, -12.0, 12.0).astype(jnp.bfloat16)


def set_ends(values, rng, least, largest):
    longest = values.shape.index(max(values.shape))
    spots = []
    for shift in (0, 1):
        where = [jax.random.randint(jax.random.fold_in(rng, axis), (), 0, length) for axis, length in enumerate(values.shape)]
        where[longest] = (where[longest] + shift) % values.shape[longest]
        spots.append(tuple(where))
    return values.at[spots[0]].set(least).at[spots[1]].set(largest)


def scatter_about(rng, extent, deviation, most, kind=jnp.bfloat16):
    drawn = jax.random.normal(rng, extent, jnp.float32) * deviation
    return jnp.minimum(jnp.maximum(drawn, -most), most).astype(kind)


def setup_inputs(seed: int = 0) -> dict:
    splits = jax.random.split(jax.random.key(seed), 6)
    latent = draw_latent(jax.random.fold_in(splits[5], 71), 0)
    cotangent = draw_cotangent(jax.random.fold_in(splits[5], 71), 0)
    pixel_mask = set_ends((jax.random.randint(splits[2], (2 * LAT_H, 2 * LAT_W), 0, 2) < 1).astype(jnp.int32), jax.random.fold_in(splits[2], 1), 0, 1)
    res_kernels = scatter_about(splits[3], (2 * LAYERS, 3, 3, CHANNELS, CHANNELS), (9 * CHANNELS) ** -0.5, 0.125)
    up_kernel = scatter_about(splits[4], (3, 3, CHANNELS, CHANNELS), (9 * CHANNELS) ** -0.5, 0.125)
    return dict(latent=latent, cotangent=cotangent, pixel_mask=pixel_mask, res_kernels=res_kernels, up_kernel=up_kernel)


EPS = 1e-06

def tile_conv(field, kernel, stride):
    return lax.conv_general_dilated(field.astype(jnp.float32)[None], kernel.astype(jnp.float32), (stride, stride), 'VALID', dimension_numbers=('NHWC', 'HWIO', 'NHWC'), precision=lax.Precision.HIGHEST)[0]

def padded_conv(field, kernel):
    padded = jnp.pad(field, ((1, 1), (1, 1), (0, 0)))
    return tile_conv(padded, kernel, 1)

def flipped(kernel):
    return jnp.transpose(kernel[::-1, ::-1], (0, 1, 3, 2))

def silu_slope(tensor):
    logistic = jax.nn.sigmoid(tensor)
    return logistic * (1.0 + tensor * (1.0 - logistic))

def norm_forward(tensor):
    grouped = tensor.reshape(-1, GROUPS, tensor.shape[-1] // GROUPS)
    average = lax.optimization_barrier(jnp.mean(grouped, axis=(0, 2)))
    centred = grouped - average[None, :, None]
    spread = lax.optimization_barrier(jnp.mean(centred * centred, axis=(0, 2)))
    inverse = lax.rsqrt(spread + EPS)
    return ((centred * inverse[None, :, None]).reshape(tensor.shape), inverse)

def norm_backward(gradient, normed, inverse):
    grouped = gradient.reshape(-1, GROUPS, gradient.shape[-1] // GROUPS)
    normal_g = normed.reshape(grouped.shape)
    total_grad = lax.optimization_barrier(jnp.mean(grouped, axis=(0, 2)))
    cross_grad = lax.optimization_barrier(jnp.mean(grouped * normal_g, axis=(0, 2)))
    result = inverse[None, :, None] * (grouped - total_grad[None, :, None] - normal_g * cross_grad[None, :, None])
    return result.reshape(gradient.shape)

def reference(latent, cotangent, pixel_mask, res_kernels, up_kernel):
    stream = latent.astype(jnp.float32)
    stored = []
    for layer_index in range(LAYERS):
        first_norm, first_inv = norm_forward(stream)
        hidden = padded_conv(jax.nn.silu(first_norm).astype(jnp.bfloat16), res_kernels[2 * layer_index])
        second_norm, second_inv = norm_forward(hidden)
        stored.append((first_norm, first_inv, second_norm, second_inv))
        if layer_index + 1 < LAYERS:
            stream = stream + padded_conv(jax.nn.silu(second_norm).astype(jnp.bfloat16), res_kernels[2 * layer_index + 1])
    masked = (pixel_mask.astype(jnp.float32)[:, :, None] * cotangent.astype(jnp.float32)).astype(jnp.bfloat16)
    upsampled = padded_conv(masked, flipped(up_kernel))
    gradient = upsampled.reshape(LAT_H, 2, LAT_W, 2, upsampled.shape[-1]).sum(axis=(1, 3))
    for layer_index in reversed(range(LAYERS)):
        first_norm, first_inv, second_norm, second_inv = stored[layer_index]
        second_grad = padded_conv(gradient.astype(jnp.bfloat16), flipped(res_kernels[2 * layer_index + 1])) * silu_slope(second_norm)
        hidden_grad = norm_backward(second_grad, second_norm, second_inv)
        first_grad = padded_conv(hidden_grad.astype(jnp.bfloat16), flipped(res_kernels[2 * layer_index])) * silu_slope(first_norm)
        gradient = gradient + norm_backward(first_grad, first_norm, first_inv)
    return gradient
```

```python
import functools

import jax
import jax.numpy as jnp
from jax import lax
from jax.experimental import pallas as pl
from jax.experimental.pallas import tpu as pltpu
from jax.sharding import PartitionSpec as P

LAYERS = 3
EPS = 1e-06
MESH = pl.DeviceIdType.MESH
F32 = jnp.float32
BF16 = jnp.bfloat16

H, W, C = 8, 64, 256
WT = W + 8
FH, FW = 2 * H, 2 * W
FWT = FW + 16
SIDE = 16
PIXELS = H * W
GROUP = 8


def position():
    c = lax.axis_index("cols")
    r = lax.axis_index("rows")
    core = c % 2
    chip = c // 2
    return c, r, core, chip % 4, chip // 4


def plane_peers():
    c, r, core, x, y = position()
    out = []
    for dy in range(4):
        for dx in range(4):
            if dx or dy:
                far = min(dx, 4 - dx) + min(dy, 4 - dy)
                out.append((far, dy * 4 + dx, (((y + dy) % 4) * 4 + (x + dx) % 4) * 2 + core, r))
    return [p[1:] for p in sorted(out, key=lambda p: -p[0])]


def column_peers():
    c, r, core, x, y = position()
    out = []
    for dz in range(8):
        for dc in range(2):
            if dz or dc:
                far = min(dz, 8 - dz)
                out.append((far, dz * 2 + dc, c - core + (core + dc) % 2, (r + dz) % 8))
    return [p[1:] for p in sorted(out, key=lambda p: -p[0])]


def neighbours():
    c, r, core, x, y = position()
    out = []
    for dr in (-1, 0, 1):
        for dc in (-1, 0, 1):
            if dr or dc:
                out.append((dr, dc, (c + dc + 32) % 32, (r + dr + 8) % 8))
    return out


def halo_copies(field, height, width, total, send, recv):
    copies = []
    for i, (dr, dc, col, row) in enumerate(neighbours()):
        src_r = pl.ds(1, height) if dr == 0 else (pl.ds(1, 1) if dr < 0 else pl.ds(height, 1))
        dst_r = pl.ds(1, height) if dr == 0 else (pl.ds(height + 1, 1) if dr < 0 else pl.ds(0, 1))
        src_c = pl.ds(0, width) if dc == 0 else (pl.ds(0, 1) if dc < 0 else pl.ds(width - 1, 1))
        dst_c = pl.ds(0, width) if dc == 0 else (pl.ds(width, 1) if dc < 0 else pl.ds(total - 1, 1))
        src, dst = (src_r, src_c, slice(None)), (dst_r, dst_c, slice(None))
        if len(field.shape) == 4:
            src, dst = (slice(None),) + src, (slice(None),) + dst
        copies.append(
            pltpu.make_async_remote_copy(
                src_ref=field.at[src],
                dst_ref=field.at[dst],
                send_sem=send.at[i],
                recv_sem=recv.at[i],
                device_id={"cols": col, "rows": row},
                device_id_type=MESH,
            )
        )
    return copies


def phase_start(buf, peers, send, recv):
    for slot, col, row in peers:
        pltpu.make_async_remote_copy(
            src_ref=buf.at[0],
            dst_ref=buf.at[slot],
            send_sem=send,
            recv_sem=recv,
            device_id={"cols": col, "rows": row},
            device_id_type=MESH,
        ).start()


def phase_wait(buf, sem):
    pltpu.make_async_copy(buf.at[pl.ds(1, SIDE - 1)], buf.at[pl.ds(1, SIDE - 1)], sem).wait()


def merge_moments(parts, count):
    mean = jnp.sum(parts[:, 0:2], axis=0) * (1.0 / SIDE)
    delta = parts[:, 0:2] - mean[None]
    square = jnp.sum(parts[:, 2:4] + delta * delta * float(count), axis=0)
    return mean, square


def lane_swap(value, step):
    lane = lax.broadcasted_iota(jnp.int32, value.shape, 1)
    return jnp.where((lane & step) != 0, pltpu.roll(value, step, 1), pltpu.roll(value, 128 - step, 1))


def wide(value):
    return jnp.concatenate([value[0:1], value[1:2]], axis=1).reshape(1, 1, C)


def sigmoid(v):
    return 1.0 / (1.0 + jnp.exp(-v))


def kernel(
    latent, mask, cot_hbm, res_hbm, up_hbm, out,
    cot, weights, fields, grads, total, fine, slopes, stats, taps, box_a, box_b, buf_a, buf_b,
    load_sem, send_a, send_b, recv_a, recv_b, hsend, hrecv,
):
    c, r, _, _, _ = position()
    top = jnp.where(r == 0, 0.0, 1.0).astype(F32)
    bottom = jnp.where(r == 7, 0.0, 1.0).astype(F32)
    left = jnp.where(c == 0, 0.0, 1.0).astype(F32)
    right = jnp.where(c == 31, 0.0, 1.0).astype(F32)
    side = lax.broadcasted_iota(jnp.int32, (1, 8, C), 1)
    edge = jnp.where(side == 0, right, jnp.where(side == 7, left, 0.0))

    barrier = pltpu.get_barrier_semaphore()
    plane, column = plane_peers(), column_peers()
    greeted = [p[1:] for p in plane] + [p[1:] for p in column] + [p[2:] for p in neighbours()]
    for col, row in greeted:
        pl.semaphore_signal(barrier, inc=1, device_id={"cols": col, "rows": row}, device_id_type=MESH)

    def weight_copy(k):
        return pltpu.make_async_copy(res_hbm.at[k], weights.at[k], load_sem.at[k])

    up_copy = pltpu.make_async_copy(up_hbm, weights.at[6], load_sem.at[6])
    cot_copy = pltpu.make_async_copy(cot_hbm, cot, load_sem.at[7])
    cot_copy.start()
    weight_copy(0).start()
    up_copy.start()
    for k in range(1, 6):
        weight_copy(k).start()

    def load_stats(k):
        return stats[k, 0:1, :].reshape(1, 1, C), stats[k, 1:2, :].reshape(1, 1, C)

    def put_moments(k, x):
        mean = jnp.sum(x, axis=(0, 1)).reshape(1, C) * (1.0 / PIXELS)
        delta = x - mean.reshape(1, 1, C)
        square = jnp.sum(delta * delta, axis=(0, 1)).reshape(1, C)
        buf_a[k, 0, 0:1, :] = mean[:, 0:128]
        buf_a[k, 0, 1:2, :] = mean[:, 128:256]
        buf_a[k, 0, 2:3, :] = square[:, 0:128]
        buf_a[k, 0, 3:4, :] = square[:, 128:256]

    def put_sums(t, d, normed):
        first = jnp.sum(d, axis=(0, 1)).reshape(1, C) * (1.0 / PIXELS)
        second = jnp.sum(d * normed, axis=(0, 1)).reshape(1, C) * (1.0 / PIXELS)
        buf_a[t, 0, 0:1, :] = first[:, 0:128]
        buf_a[t, 0, 1:2, :] = first[:, 128:256]
        buf_a[t, 0, 2:3, :] = second[:, 0:128]
        buf_a[t, 0, 3:4, :] = second[:, 128:256]

    def start_a(t):
        phase_start(buf_a.at[t], plane, send_a.at[t], recv_a.at[t])

    def start_b(t):
        phase_start(buf_b.at[t], column, send_b.at[t], recv_b.at[t])

    def field_copies(k):
        return halo_copies(fields.at[k], H, W, WT, hsend.at[k], hrecv.at[k])

    def grad_copies(k):
        return halo_copies(grads.at[k], H, W, WT, hsend.at[k + 6], hrecv.at[k + 6])

    def total_copies():
        return halo_copies(total, H, W, WT, hsend.at[12], hrecv.at[12])

    def fine_copies():
        return halo_copies(fine, FH, FW, FWT, hsend.at[13], hrecv.at[13])

    def put_taps(make):
        for first, rows, scale in ((0, 1, top), (1, H, None), (H + 1, 1, bottom)):
            u = make(first, rows)
            if scale is not None:
                u = u * scale
            u = jnp.concatenate([u[:, 0:W], u[:, W:WT] * edge], axis=1)
            at = slice(first, first + rows)
            taps[at, :, 0:C] = pltpu.roll(u, 1, 1)[:, 0:W].astype(BF16)
            taps[at, :, C : 2 * C] = u[:, 0:W].astype(BF16)
            taps[at, :, 2 * C : 3 * C] = pltpu.roll(u, WT - 1, 1)[:, 0:W].astype(BF16)

    def conv(k):
        rows = [taps[a : a + H].reshape(PIXELS, 3 * C) for a in range(3)]
        y = jnp.dot(jnp.concatenate(rows, axis=-1), weights[k].reshape(9 * C, C), preferred_element_type=F32)
        return y.reshape(H, W, C)

    def conv_back(piece, k):
        y = None
        for a in range(3):
            for b in range(3):
                d = lax.dot_general(
                    piece(a, b), weights[k, 8 - 3 * a - b], (((1,), (1,)), ((), ())), preferred_element_type=F32
                )
                y = d if y is None else y + d
        return y.reshape(H, W, C)

    def tap(a, b):
        return taps[a : a + H, :, b * C : (b + 1) * C].reshape(PIXELS, C)

    fields[0, 1 : H + 1, 0:W, :] = latent[...].astype(F32)
    put_moments(0, latent[...].astype(F32))
    cot_copy.wait()

    def mask_row(i, carry):
        row = jnp.broadcast_to(mask[pl.ds(i, 1), :].astype(F32), (FW, FW)).T
        fine[0, i + 1, 0:FW, :] = cot[i, :, 0:128].astype(F32) * row
        fine[1, i + 1, 0:FW, :] = cot[i, :, 128:256].astype(F32) * row
        return carry

    pl.semaphore_wait(barrier, len(greeted))
    start_a(0)
    for copy in field_copies(0):
        copy.start()
    lax.fori_loop(0, FH, mask_row, 0)
    for copy in fine_copies():
        copy.start()

    def slope(k):
        mean, inv = load_stats(k)
        n = (fields[k, 1 : H + 1, 0:W, :] - mean) * inv
        s = sigmoid(n)
        slopes[k] = s * (1.0 + n * (1.0 - s))

    def boxes():
        for copy in fine_copies():
            copy.wait_recv()
        fine[:, 0] = fine[:, 0] * top
        fine[:, FH + 1] = fine[:, FH + 1] * bottom
        fine[:, :, FW : FW + 8, :] = fine[:, :, FW : FW + 8, :] * right
        fine[:, :, FWT - 8 : FWT, :] = fine[:, :, FWT - 8 : FWT, :] * left

        def columns(v_even, v_odd, dst, i):
            dst[i, :, 0:C] = (pltpu.roll(v_odd, 1, 0) + v_even)[0:W].astype(BF16)
            dst[i, :, C : 2 * C] = (v_even + v_odd)[0:W].astype(BF16)
            dst[i, :, 2 * C : 3 * C] = (v_odd + pltpu.roll(v_even, WT - 1, 0))[0:W].astype(BF16)

        def pair(i, dst, at):
            even, odd = (
                jnp.concatenate(
                    [fine[h, i, pl.ds(q, WT, 2), :] + fine[h, i + 1, pl.ds(q, WT, 2), :] for h in (0, 1)], axis=1
                )
                for q in (0, 1)
            )
            columns(even, odd, dst, at)

        def body(i, carry):
            pair(2 * i, box_a, i)
            pair(2 * i + 1, box_b, i)
            return carry

        lax.fori_loop(0, H, body, 0)
        pair(2 * H, box_a, H)

    def upper():
        up_copy.wait()

        def piece(a, b):
            at = slice(b * C, (b + 1) * C)
            if a == 1:
                return box_b[:, :, at].reshape(PIXELS, C)
            return box_a[a // 2 : a // 2 + H, :, at].reshape(PIXELS, C)

        total[1 : H + 1, 0:W, :] = conv_back(piece, 6)
        for copy in total_copies():
            copy.start()

    def finish_moments(k):
        mean, square = merge_moments(buf_b[k], PIXELS * SIDE)
        count = float(PIXELS * SIDE * SIDE)
        for step in (1, 2, 4):
            other, squares = lane_swap(mean, step), lane_swap(square, step)
            delta = mean - other
            mean = (mean + other) * 0.5
            square = square + squares + delta * delta * (count * 0.5)
            count *= 2.0
        inv = lax.rsqrt(square * (1.0 / count) + EPS)
        mean, inv = wide(mean), wide(inv)
        stats[k, 0:1, :] = mean.reshape(1, C)
        stats[k, 1:2, :] = inv.reshape(1, C)
        return mean, inv

    def forward(k, carry):
        @pl.when(k > 0)
        def _():
            start_a(k)
            for copy in field_copies(k):
                copy.start()
            slope(k - 1)

        phase_wait(buf_a.at[k], recv_a.at[k])
        mean, square = merge_moments(buf_a[k], PIXELS)
        buf_b[k, 0, 0:2, :] = mean
        buf_b[k, 0, 2:4, :] = square
        start_b(k)

        @pl.when(k == 1)
        def _():
            boxes()

        @pl.when(k == 2)
        def _():
            upper()

        @pl.when(k < 5)
        def _():
            weight_copy(k).wait()

        for copy in field_copies(k):
            copy.wait_recv()
        phase_wait(buf_b.at[k], recv_b.at[k])
        mean, inv = finish_moments(k)

        @pl.when(k < 5)
        def _():
            def active(first, rows):
                n = (fields[k, first : first + rows] - mean) * inv
                return n * sigmoid(n)

            put_taps(active)
            y = conv(k)
            keep = jnp.where(k % 2 == 1, 1.0, 0.0).astype(F32)
            y = y + keep * fields[jnp.maximum(k - 1, 0), 1 : H + 1, 0:W, :]
            fields[k + 1, 1 : H + 1, 0:W, :] = y
            put_moments(k + 1, y)

        return carry

    lax.fori_loop(0, 6, forward, 0)

    slope(5)
    weight_copy(5).wait()
    for copy in total_copies():
        copy.wait()
    put_taps(lambda first, rows: total[first : first + rows])

    def next_grad(k):
        d = conv_back(tap, k) * slopes[k]
        grads[k, 1 : H + 1, 0:W, :] = d
        mean, inv = load_stats(k)
        put_sums(11 - k, d, (fields[k, 1 : H + 1, 0:W, :] - mean) * inv)

    next_grad(5)

    def backward(j, carry):
        k = 5 - j
        t = 6 + j
        start_a(t)
        for copy in grad_copies(k):
            copy.start()
        phase_wait(buf_a.at[t], recv_a.at[t])
        buf_b[t, 0] = jnp.sum(buf_a[t], axis=0) * (1.0 / SIDE)
        start_b(t)
        for copy in grad_copies(k):
            copy.wait_recv()
        phase_wait(buf_b.at[t], recv_b.at[t])
        sums = jnp.sum(buf_b[t], axis=0) * (1.0 / (SIDE * GROUP))
        for step in (1, 2, 4):
            sums = sums + lane_swap(sums, step)
        first_mean, second_mean = wide(sums[0:2]), wide(sums[2:4])
        mean, inv = load_stats(k)
        whole = jnp.where(k % 2 == 0, 1.0, 0.0).astype(F32)

        def back(first, rows):
            at = slice(first, first + rows)
            n = (fields[k, at] - mean) * inv
            u = inv * (grads[k, at] - first_mean - n * second_mean)
            u = u + whole * total[at]

            @pl.when(k % 2 == 0)
            def _():
                total[at] = u

            return u

        put_taps(back)

        @pl.when(k > 0)
        def _():
            next_grad(k - 1)

        return carry

    lax.fori_loop(0, 6, backward, 0)
    out[...] = total[1 : H + 1, 0:W, :]

    def drain(t, carry):
        phase_wait(buf_a.at[t], send_a.at[t])
        phase_wait(buf_b.at[t], send_b.at[t])
        return carry

    lax.fori_loop(0, 12, drain, 0)

    def drain_halos(k, carry):
        for copy in field_copies(k) + grad_copies(k):
            copy.wait_send()
        return carry

    lax.fori_loop(0, 6, drain_halos, 0)
    for copy in fine_copies():
        copy.wait_send()


def per_device(latent, cotangent, pixel_mask, res_kernels, up_kernel):
    vmem = pl.BlockSpec(memory_space=pltpu.VMEM)
    hbm = pl.BlockSpec(memory_space=pl.ANY)
    dma = pltpu.SemaphoreType.DMA
    return pl.pallas_call(
        kernel,
        out_shape=jax.ShapeDtypeStruct((H, W, C), F32),
        in_specs=[vmem, vmem, hbm, hbm, hbm],
        out_specs=vmem,
        scratch_shapes=[
            pltpu.VMEM((FH, FW, C), BF16),
            pltpu.VMEM((7, 9, C, C), BF16),
            pltpu.VMEM((6, H + 2, WT, C), F32),
            pltpu.VMEM((6, H + 2, WT, C), F32),
            pltpu.VMEM((H + 2, WT, C), F32),
            pltpu.VMEM((2, FH + 2, FWT, 128), F32),
            pltpu.VMEM((6, H, W, C), F32),
            pltpu.VMEM((6, 8, C), F32),
            pltpu.VMEM((H + 2, W, 3 * C), BF16),
            pltpu.VMEM((H + 1, W, 3 * C), BF16),
            pltpu.VMEM((H, W, 3 * C), BF16),
            pltpu.VMEM((12, SIDE, 4, 128), F32),
            pltpu.VMEM((12, SIDE, 4, 128), F32),
            dma((8,)),
            dma((12,)),
            dma((12,)),
            dma((12,)),
            dma((12,)),
            dma((14, 8)),
            dma((14, 8)),
        ],
        compiler_params=pltpu.CompilerParams(
            collective_id=0, has_side_effects=True, vmem_limit_bytes=56 * 2**20
        ),
    )(
        latent,
        pixel_mask,
        cotangent,
        res_kernels.reshape(6, 9, C, C),
        up_kernel.reshape(9, C, C),
    )


def solution(mesh):
    in_specs = (P("rows", "cols", None), P("rows", "cols", None), P("rows", "cols"), P(), P())
    out_specs = P("rows", "cols", None)
    return jax.shard_map(
        per_device, mesh=mesh, in_specs=in_specs, out_specs=out_specs, check_vma=False
    )
```

```python
import functools

import jax
import jax.numpy as jnp
from jax import lax
from jax.experimental import pallas as pl
from jax.experimental.pallas import tpu as pltpu
from jax.sharding import PartitionSpec as P

LAYERS = 3
EPS = 1e-06
MESH = pl.DeviceIdType.MESH
F32 = jnp.float32
BF16 = jnp.bfloat16

H, W, C = 8, 64, 256
T = 3
RT = H + 2 * T
WT = W + 8
WB = W + 16
FH, FW = 2 * H, 2 * W
FWT = FW + 16
SIDE = 16
PIXELS = H * W
GROUP = 8


def position():
    c = lax.axis_index("cols")
    r = lax.axis_index("rows")
    core = c % 2
    chip = c // 2
    return c, r, core, chip % 4, chip // 4


def plane_peers():
    c, r, core, x, y = position()
    out = []
    for dy in range(4):
        for dx in range(4):
            if dx or dy:
                far = min(dx, 4 - dx) + min(dy, 4 - dy)
                out.append((far, dy * 4 + dx, (((y + dy) % 4) * 4 + (x + dx) % 4) * 2 + core, r))
    return [p[1:] for p in sorted(out, key=lambda p: -p[0])]


def column_peers():
    c, r, core, x, y = position()
    out = []
    for dz in range(8):
        for dc in range(2):
            if dz or dc:
                far = min(dz, 8 - dz)
                out.append((far, dz * 2 + dc, c - core + (core + dc) % 2, (r + dz) % 8))
    return [p[1:] for p in sorted(out, key=lambda p: -p[0])]


def neighbours():
    c, r, core, x, y = position()
    out = []
    for dr in (-1, 0, 1):
        for dc in (-1, 0, 1):
            if dr or dc:
                out.append((dr, dc, (c + dc + 32) % 32, (r + dr + 8) % 8))
    return out


def halo_copies(field, top, height, width, total, edges, corners, send, recv):
    def spans(step, first, size, end, near, far):
        n = far - near + 1
        if step < 0:
            return pl.ds(first + near - 1, n), pl.ds(first + size + near - 1, n)
        if step > 0:
            return pl.ds(first + size - far, n), pl.ds(end - far, n)
        return pl.ds(first, size), pl.ds(first, size)

    copies = []
    for dr, dc, col, row in neighbours():
        band = corners if dr and dc else edges
        if band is None:
            continue
        src_r, dst_r = spans(dr, top, height, top, *band)
        src_c, dst_c = spans(dc, 0, width, total, *band)
        src, dst = (src_r, src_c, slice(None)), (dst_r, dst_c, slice(None))
        if len(field.shape) == 4:
            src, dst = (slice(None),) + src, (slice(None),) + dst
        copies.append(
            pltpu.make_async_remote_copy(
                src_ref=field.at[src],
                dst_ref=field.at[dst],
                send_sem=send.at[len(copies)],
                recv_sem=recv.at[len(copies)],
                device_id={"cols": col, "rows": row},
                device_id_type=MESH,
            )
        )
    return copies


def phase_start(buf, peers, send, recv):
    for slot, col, row in peers:
        pltpu.make_async_remote_copy(
            src_ref=buf.at[0],
            dst_ref=buf.at[slot],
            send_sem=send,
            recv_sem=recv,
            device_id={"cols": col, "rows": row},
            device_id_type=MESH,
        ).start()


def phase_wait(buf, sem):
    pltpu.make_async_copy(buf.at[pl.ds(1, SIDE - 1)], buf.at[pl.ds(1, SIDE - 1)], sem).wait()


def merge_moments(parts, count):
    mean = jnp.sum(parts[:, 0:2], axis=0) * (1.0 / SIDE)
    delta = parts[:, 0:2] - mean[None]
    square = jnp.sum(parts[:, 2:4] + delta * delta * float(count), axis=0)
    return mean, square


def lane_swap(value, step):
    lane = lax.broadcasted_iota(jnp.int32, value.shape, 1)
    return jnp.where((lane & step) != 0, pltpu.roll(value, step, 1), pltpu.roll(value, 128 - step, 1))


def wide(value):
    return jnp.concatenate([value[0:1], value[1:2]], axis=1).reshape(1, 1, C)


def sigmoid(v):
    return 1.0 / (1.0 + jnp.exp(-v))


def kernel(
    latent, mask, cot_hbm, res_hbm, up_hbm, out,
    cot, weights, fields, grads, total, pre, fine, slopes, stats, taps, ones, box_a, box_b,
    buf_a, buf_b, sum_a, sum_b, cor_own, cor_a, cor_b, cor_c, cor, expanded,
    load_sem, send_a, send_b, recv_a, recv_b, csend, crecv, hsend, hrecv,
):
    c, r, _, px, py = position()
    place = py * 4 + px
    top = jnp.where(r == 0, 0.0, 1.0).astype(F32)
    bottom = jnp.where(r == 7, 0.0, 1.0).astype(F32)
    left = jnp.where(c == 0, 0.0, 1.0).astype(F32)
    right = jnp.where(c == 31, 0.0, 1.0).astype(F32)
    side = lax.broadcasted_iota(jnp.int32, (1, 8, C), 1)
    edge = jnp.where(side < 4, right, left)

    barrier = pltpu.get_barrier_semaphore()
    plane, column = plane_peers(), column_peers()
    greeted = [p[1:] for p in plane] + [p[1:] for p in column] + [p[2:] for p in neighbours()]
    for col, row in greeted:
        pl.semaphore_signal(barrier, inc=1, device_id={"cols": col, "rows": row}, device_id_type=MESH)

    def weight_copy(k):
        return pltpu.make_async_copy(res_hbm.at[k], weights.at[k], load_sem.at[k])

    up_copy = pltpu.make_async_copy(up_hbm, weights.at[6], load_sem.at[6])
    cot_copy = pltpu.make_async_copy(cot_hbm, cot, load_sem.at[7])
    cot_copy.start()
    weight_copy(0).start()
    up_copy.start()
    for k in range(1, 6):
        weight_copy(k).start()

    def load_stats(k):
        return stats[k, 0:1, :].reshape(1, 1, C), stats[k, 1:2, :].reshape(1, 1, C)

    def normed(k, rows, columns=slice(0, WT)):
        mean, inv = load_stats(k)
        return (fields[k, rows, columns, :] - mean) * inv

    tile_rows, tile_columns = slice(T, T + H), slice(0, W)

    def put_rows(buf, at, first, second):
        buf[at : at + 1, :] = first[:, 0:128]
        buf[at + 1 : at + 2, :] = first[:, 128:256]
        buf[at + 2 : at + 3, :] = second[:, 0:128]
        buf[at + 3 : at + 4, :] = second[:, 128:256]

    def put_moments(k, x):
        mean = jnp.sum(x, axis=(0, 1)).reshape(1, C) * (1.0 / PIXELS)
        delta = x - mean.reshape(1, 1, C)
        square = jnp.sum(delta * delta, axis=(0, 1)).reshape(1, C)
        put_rows(buf_a.at[k, 0], 0, mean, square)

    def put_sums(l, at, d, n):
        first = jnp.sum(d, axis=(0, 1)).reshape(1, C) * (1.0 / PIXELS)
        second = jnp.sum(d * n, axis=(0, 1)).reshape(1, C) * (1.0 / PIXELS)
        put_rows(sum_a.at[l, 0], at, first, second)

    def ring_copies(k):
        return halo_copies(fields.at[k], T, H, W, WT, (1, 1), (1, 3), hsend.at[k], hrecv.at[k])

    def wide_copies(k):
        return halo_copies(fields.at[k], T, H, W, WT, (2, 3), None, hsend.at[k + 6], hrecv.at[k + 6])

    def grad_copies(l):
        return halo_copies(grads.at[l], T, H, W, WT, (1, 3), (1, 3), hsend.at[l + 12], hrecv.at[l + 12])

    def total_copies():
        return halo_copies(total, T, H, W, WT, (1, 2), (1, 2), hsend.at[15], hrecv.at[15])

    def fine_copies():
        return halo_copies(fine, 1, FH, FW, FWT, (1, 1), (1, 1), hsend.at[16], hrecv.at[16])

    def put_taps(make, first, last, columns):
        parts = ((first, T, top), (T, T + H, None), (T + H, last, bottom))
        for begin, end, scale in parts:
            u = make(begin, end - begin)
            if scale is not None:
                u = u * scale
            u = jnp.concatenate([u[:, 0:W], u[:, W:WT] * edge], axis=1)
            at = slice(begin - first, end - first)
            for b, v in enumerate((pltpu.roll(u, 1, 1), u, pltpu.roll(u, WT - 1, 1))):
                if columns > WT:
                    v = jnp.concatenate([v, jnp.zeros((end - begin, columns - WT, C), F32)], axis=1)
                taps[at, 0:columns, b * C : (b + 1) * C] = v[:, 0:columns].astype(BF16)

    def conv(k):
        rows = [taps[a : a + H, 0:W].reshape(PIXELS, 3 * C) for a in range(3)]
        y = jnp.dot(jnp.concatenate(rows, axis=-1), weights[k].reshape(9 * C, C), preferred_element_type=F32)
        return y.reshape(H, W, C)

    def conv_back(piece, k, rows, columns):
        y = None
        for a in range(3):
            for b in range(3):
                d = lax.dot_general(
                    piece(a, b), weights[k, 8 - 3 * a - b], (((1,), (1,)), ((), ())), preferred_element_type=F32
                )
                y = d if y is None else y + d
        return y.reshape(rows, columns, C)

    def tap_conv_back(k, rows, columns):
        def piece(a, b):
            return taps[a : a + rows, 0:columns, b * C : (b + 1) * C].reshape(rows * columns, C)

        return conv_back(piece, k, rows, columns)

    fields[0, tile_rows, tile_columns, :] = latent[...].astype(F32)
    put_moments(0, latent[...].astype(F32))

    def start_a(k):
        phase_start(buf_a.at[k], plane, send_a.at[k], recv_a.at[k])
        for copy in ring_copies(k) + wide_copies(k):
            copy.start()

    pl.semaphore_wait(barrier, len(greeted))
    start_a(0)
    cot_copy.wait()

    def mask_row(i, carry):
        row = jnp.broadcast_to(mask[pl.ds(i, 1), :].astype(F32), (FW, FW)).T
        fine[0, i + 1, 0:FW, :] = cot[i, :, 0:128].astype(F32) * row
        fine[1, i + 1, 0:FW, :] = cot[i, :, 128:256].astype(F32) * row
        return carry

    lax.fori_loop(0, FH, mask_row, 0)
    for copy in fine_copies():
        copy.start()

    inside = jnp.concatenate(
        [
            jnp.full((1, W + 16, 128), 1.0, F32) * top,
            jnp.full((H, W + 16, 128), 1.0, F32),
            jnp.full((1, W + 16, 128), 1.0, F32) * bottom,
        ],
        axis=0,
    )
    column_at = lax.broadcasted_iota(jnp.int32, (H + 2, W, 128), 1)
    for b, scale in enumerate((jnp.where(column_at == 0, left, 1.0), None, jnp.where(column_at == W - 1, right, 1.0))):
        v = inside[:, 0:W] if scale is None else inside[:, 0:W] * scale
        ones[:, :, b * 128 : (b + 1) * 128] = v.astype(BF16)

    def slope(k, first, last):
        n = normed(k, slice(first, last))
        s = sigmoid(n)
        slopes[k, first - 1 : last - 1] = s * (1.0 + n * (1.0 - s))

    def boxes():
        for copy in fine_copies():
            copy.wait_recv()
        fine[:, 0] = fine[:, 0] * top
        fine[:, FH + 1] = fine[:, FH + 1] * bottom
        fine[:, :, FW : FW + 8, :] = fine[:, :, FW : FW + 8, :] * right
        fine[:, :, FWT - 8 : FWT, :] = fine[:, :, FWT - 8 : FWT, :] * left

        def pair(i, dst, at):
            even, odd = (
                jnp.concatenate(
                    [fine[h, i, pl.ds(q, WT, 2), :] + fine[h, i + 1, pl.ds(q, WT, 2), :] for h in (0, 1)], axis=1
                )
                for q in (0, 1)
            )
            dst[at, :, 0:C] = (pltpu.roll(odd, 1, 0) + even)[0:W].astype(BF16)
            dst[at, :, C : 2 * C] = (even + odd)[0:W].astype(BF16)
            dst[at, :, 2 * C : 3 * C] = (odd + pltpu.roll(even, WT - 1, 0))[0:W].astype(BF16)

        def body(i, carry):
            pair(2 * i, box_a, i)
            pair(2 * i + 1, box_b, i)
            return carry

        lax.fori_loop(0, H, body, 0)
        pair(2 * H, box_a, H)

    def upper():
        up_copy.wait()

        def piece(a, b):
            at = slice(b * C, (b + 1) * C)
            if a == 1:
                return box_b[:, :, at].reshape(PIXELS, C)
            return box_a[a // 2 : a // 2 + H, :, at].reshape(PIXELS, C)

        total[tile_rows, tile_columns, :] = conv_back(piece, 6, H, W)
        for copy in total_copies():
            copy.start()

    def lift(k):
        put_taps(lambda first, rows: total[first : first + rows], T - 2, T + H + 2, WB)
        pre[...] = tap_conv_back(k, H + 2, WB)[:, 0:WT]

    def correlate(l):
        k = 2 * l
        mean = jnp.concatenate([buf_a[k + 1, 0, 0:1, :], buf_a[k + 1, 0, 1:2, :]], axis=1)
        put_taps(
            lambda first, rows: fields[k + 1, first : first + rows] - mean.reshape(1, 1, C), T - 1, T + H + 1, W
        )
        cor[...] = jnp.zeros_like(cor)

        def kind(i, carry):
            n = normed(k, tile_rows, tile_columns)
            q = slopes[k, T - 1 : T - 1 + H, 0:W] * jnp.where(i == 0, 1.0, n)
            q = q.reshape(PIXELS, C).astype(BF16)
            raw = plain = None
            for a in range(3):
                for b in range(3):
                    weight = weights[k, 8 - 3 * a - b].astype(F32)
                    over = (((0,), (0,)), ((), ()))
                    field = taps[a : a + H, 0:W, b * C : (b + 1) * C].reshape(PIXELS, C)
                    first = lax.dot_general(q, field, over, preferred_element_type=F32) * weight
                    unit = ones[a : a + H, :, b * 128 : (b + 1) * 128].reshape(PIXELS, 128)
                    second = lax.dot_general(q, unit, over, preferred_element_type=F32)
                    second = jnp.concatenate([second, second], axis=1) * weight
                    raw = first if raw is None else raw + first
                    plain = second if plain is None else plain + second
            raw = raw + plain * mean
            row = lax.broadcasted_iota(jnp.int32, (C, 128), 0) // GROUP
            lane = lax.broadcasted_iota(jnp.int32, (C, 128), 1)
            for j, block in enumerate((raw, plain)):
                block = jnp.sum(block.reshape(C // GROUP, GROUP, C), axis=1) * (1.0 / (PIXELS * SIDE * SIDE * GROUP))
                pick = jnp.where(lane == 64 * i + 32 * j + row, 1.0, 0.0).astype(F32)
                cor[...] += jnp.dot(block, pick, precision=lax.Precision.HIGHEST, preferred_element_type=F32)
            return carry

        lax.fori_loop(0, 2, kind, 0)
        for i in range(SIDE):
            cor_own[l, i] = cor[2 * i : 2 * i + 2, :]
        for slot, col, row in plane:
            x, y = (col // 2) % 4, col // 8
            pltpu.make_async_remote_copy(
                src_ref=cor_own.at[l, y * 4 + x],
                dst_ref=cor_a.at[l, slot],
                send_sem=csend.at[l],
                recv_sem=crecv.at[l],
                device_id={"cols": col, "rows": row},
                device_id_type=MESH,
            ).start()

    def correlate_b(l):
        phase_wait(cor_a.at[l], crecv.at[l])
        cor_b[l, 0] = cor_own[l, place] + jnp.sum(cor_a[l, 1:SIDE], axis=0)
        phase_start(cor_b.at[l], column, csend.at[l + 3], crecv.at[l + 3])

    def correlate_c(l):
        phase_wait(cor_b.at[l], crecv.at[l + 3])
        cor_c[l, place] = jnp.sum(cor_b[l], axis=0)
        for slot, col, row in plane:
            pltpu.make_async_remote_copy(
                src_ref=cor_c.at[l, place],
                dst_ref=cor_c.at[l, place],
                send_sem=csend.at[l + 6],
                recv_sem=crecv.at[l + 6],
                device_id={"cols": col, "rows": row},
                device_id_type=MESH,
            ).start()

    def expand(l):
        phase_wait(cor_c.at[l], crecv.at[l + 6])
        for i in range(SIDE):
            cor[2 * i : 2 * i + 2, :] = cor_c[l, i]
        whole = cor[...]
        high = whole.astype(BF16)
        low = (whole - high.astype(F32)).astype(BF16)
        group = lax.broadcasted_iota(jnp.int32, (32, C), 1) // GROUP
        spread = jnp.where(lax.broadcasted_iota(jnp.int32, (32, C), 0) == group, 1.0, 0.0).astype(BF16)
        lane = lax.broadcasted_iota(jnp.int32, (128, C), 0)
        channel = lax.broadcasted_iota(jnp.int32, (128, C), 1) // GROUP
        for i in range(2):
            for j in range(2):
                pick = jnp.where(lane == 64 * i + 32 * j + channel, 1.0, 0.0).astype(BF16)
                for part, value in enumerate((high, low)):
                    block = jnp.dot(value, pick, preferred_element_type=F32).astype(BF16)
                    block = lax.dot_general(
                        block, spread, (((0,), (0,)), ((), ())), preferred_element_type=F32
                    )
                    expanded[part, j * C : (j + 1) * C, i * C : (i + 1) * C] = block.astype(BF16)

    def finish_moments(k):
        mean, square = merge_moments(buf_b[k], PIXELS * SIDE)
        count = float(PIXELS * SIDE * SIDE)
        for step in (1, 2, 4):
            other, squares = lane_swap(mean, step), lane_swap(square, step)
            delta = mean - other
            mean = (mean + other) * 0.5
            square = square + squares + delta * delta * (count * 0.5)
            count *= 2.0
        inv = lax.rsqrt(square * (1.0 / count) + EPS)
        mean, inv = wide(mean), wide(inv)
        stats[k, 0:1, :] = mean.reshape(1, C)
        stats[k, 1:2, :] = inv.reshape(1, C)
        return mean, inv

    def forward(k, carry):
        @pl.when(k > 0)
        def _():
            start_a(k)
            slope(k - 1, 1, RT - 1)

        @pl.when((k == 2) | (k == 4))
        def _():
            correlate_b(k // 2 - 1)

        phase_wait(buf_a.at[k], recv_a.at[k])
        mean, square = merge_moments(buf_a[k], PIXELS)
        buf_b[k, 0, 0:2, :] = mean
        buf_b[k, 0, 2:4, :] = square
        phase_start(buf_b.at[k], column, send_b.at[k], recv_b.at[k])

        for copy in ring_copies(k) + wide_copies(k)[1:3]:
            copy.wait_recv()

        @pl.when(k % 2 == 1)
        def _():
            correlate(k // 2)

        @pl.when((k == 2) | (k == 4))
        def _():
            correlate_c(k // 2 - 1)

        @pl.when(k == 2)
        def _():
            boxes()
            upper()

        @pl.when(k == 4)
        def _():
            weight_copy(5).wait()
            for copy in total_copies():
                copy.wait()
            lift(5)

        @pl.when(k < 5)
        def _():
            weight_copy(k).wait()

        for copy in wide_copies(k)[0::3]:
            copy.wait_recv()
        phase_wait(buf_b.at[k], recv_b.at[k])
        mean, inv = finish_moments(k)

        @pl.when(k < 5)
        def _():
            def active(first, rows):
                n = (fields[k, first : first + rows] - mean) * inv
                return n * sigmoid(n)

            put_taps(active, T - 1, T + H + 1, W)
            y = conv(k)
            keep = jnp.where(k % 2 == 1, 1.0, 0.0).astype(F32)
            y = y + keep * fields[jnp.maximum(k - 1, 0), tile_rows, tile_columns, :]
            fields[k + 1, tile_rows, tile_columns, :] = y
            put_moments(k + 1, y)

        return carry

    lax.fori_loop(0, 6, forward, 0)
    slope(5, T - 1, T + H + 1)

    def layer(l, last):
        k = 2 * l
        mean1, inv1 = load_stats(k)
        mean2, inv2 = load_stats(k + 1)
        t = 8 - l
        grads[l, tile_rows, tile_columns, :] = (
            pre[1 : H + 1, 0:W] * slopes[k + 1, T - 1 : T - 1 + H, 0:W]
        )
        put_sums(l, 0, grads[l, tile_rows, tile_columns, :], normed(k + 1, tile_rows, tile_columns))

        def unprojected(first, rows):
            at = first - T + 1
            return inv2 * (pre[at : at + rows] * slopes[k + 1, first - 1 : first - 1 + rows])

        put_taps(unprojected, T - 1, T + H + 1, W)
        d = tap_conv_back(k, H, W) * slopes[k, T - 1 : T - 1 + H, 0:W]
        put_sums(l, 4, d, normed(k, tile_rows, tile_columns))
        phase_start(sum_a.at[l], plane, send_a.at[t], recv_a.at[t])
        for copy in grad_copies(l):
            copy.start()

        @pl.when(l == 2)
        def _():
            correlate_b(l)

        phase_wait(sum_a.at[l], recv_a.at[t])
        sum_b[l, 0] = jnp.sum(sum_a[l], axis=0) * (1.0 / SIDE)
        phase_start(sum_b.at[l], column, send_b.at[t], recv_b.at[t])

        @pl.when(l == 2)
        def _():
            correlate_c(l)

        expand(l)
        for copy in grad_copies(l):
            copy.wait_recv()
        phase_wait(sum_b.at[l], recv_b.at[t])
        sums = jnp.sum(sum_b[l], axis=0) * (1.0 / (SIDE * GROUP))
        for step in (1, 2, 4):
            sums = sums + lane_swap(sums, step)
        first2, second2, first1, second1 = (wide(sums[i : i + 2]) for i in (0, 2, 4, 6))
        scaled = inv2 * second2
        source = jnp.concatenate([inv2 * scaled, inv2 * (first2 - mean2 * scaled)], axis=-1).reshape(1, 2 * C)
        source = jnp.broadcast_to(source * (1.0 / GROUP), (16, 2 * C))
        high = source.astype(BF16)
        low = (source - high.astype(F32)).astype(BF16)
        moved = (
            jnp.dot(high, expanded[0], preferred_element_type=F32)
            + jnp.dot(low, expanded[0], preferred_element_type=F32)
            + jnp.dot(high, expanded[1], preferred_element_type=F32)
        )
        first1 = first1 - moved[0:1, 0:C].reshape(1, 1, C)
        second1 = second1 - moved[0:1, C : 2 * C].reshape(1, 1, C)

        def back(first, rows):
            at = slice(first, first + rows)
            return inv2 * (grads[l, at] - first2 - normed(k + 1, at) * second2)

        if last:
            put_taps(back, T - 1, T + H + 1, W)
            d = tap_conv_back(k, H, W) * slopes[k, T - 1 : T - 1 + H, 0:W]
            n = normed(k, tile_rows, tile_columns)
            out[...] = total[tile_rows, tile_columns, :] + inv1 * (d - first1 - n * second1)
        else:
            put_taps(back, 0, RT, WB)
            d = tap_conv_back(k, H + 4, WB)[:, 0:WT] * slopes[k]
            rows = slice(T - 2, T + H + 2)
            total[rows] += inv1 * (d - first1 - normed(k, rows) * second1)
            lift(k - 1)

    def backward(j, carry):
        layer(2 - j, False)
        return carry

    lax.fori_loop(0, 2, backward, 0)
    layer(0, True)

    def drain(k, carry):
        phase_wait(buf_a.at[k], send_a.at[k])
        phase_wait(buf_b.at[k], send_b.at[k])
        for copy in ring_copies(k) + wide_copies(k):
            copy.wait_send()
        return carry

    lax.fori_loop(0, 6, drain, 0)

    def drain_back(l, carry):
        phase_wait(sum_a.at[l], send_a.at[8 - l])
        phase_wait(sum_b.at[l], send_b.at[8 - l])
        phase_wait(cor_a.at[l], csend.at[l])
        phase_wait(cor_b.at[l], csend.at[l + 3])
        phase_wait(cor_c.at[l], csend.at[l + 6])
        for copy in grad_copies(l):
            copy.wait_send()
        return carry

    lax.fori_loop(0, 3, drain_back, 0)
    for copy in fine_copies():
        copy.wait_send()


def per_device(latent, cotangent, pixel_mask, res_kernels, up_kernel):
    vmem = pl.BlockSpec(memory_space=pltpu.VMEM)
    hbm = pl.BlockSpec(memory_space=pl.ANY)
    dma = pltpu.SemaphoreType.DMA
    return pl.pallas_call(
        kernel,
        out_shape=jax.ShapeDtypeStruct((H, W, C), F32),
        in_specs=[vmem, vmem, hbm, hbm, hbm],
        out_specs=vmem,
        scratch_shapes=[
            pltpu.VMEM((FH, FW, C), BF16),
            pltpu.VMEM((7, 9, C, C), BF16),
            pltpu.VMEM((6, RT, WT, C), F32),
            pltpu.VMEM((3, RT, WT, C), F32),
            pltpu.VMEM((RT, WT, C), F32),
            pltpu.VMEM((H + 2, WT, C), F32),
            pltpu.VMEM((2, FH + 2, FWT, 128), F32),
            pltpu.VMEM((6, RT - 2, WT, C), F32),
            pltpu.VMEM((6, 8, C), F32),
            pltpu.VMEM((RT, WB, 3 * C), BF16),
            pltpu.VMEM((H + 2, W, 3 * 128), BF16),
            pltpu.VMEM((H + 1, W, 3 * C), BF16),
            pltpu.VMEM((H, W, 3 * C), BF16),
            pltpu.VMEM((6, SIDE, 4, 128), F32),
            pltpu.VMEM((6, SIDE, 4, 128), F32),
            pltpu.VMEM((3, SIDE, 8, 128), F32),
            pltpu.VMEM((3, SIDE, 8, 128), F32),
            pltpu.VMEM((3, SIDE, 2, 128), F32),
            pltpu.VMEM((3, SIDE, 2, 128), F32),
            pltpu.VMEM((3, SIDE, 2, 128), F32),
            pltpu.VMEM((3, SIDE, 2, 128), F32),
            pltpu.VMEM((32, 128), F32),
            pltpu.VMEM((2, 2 * C, 2 * C), BF16),
            dma((8,)),
            dma((9,)),
            dma((9,)),
            dma((9,)),
            dma((9,)),
            dma((9,)),
            dma((9,)),
            dma((17, 8)),
            dma((17, 8)),
        ],
        compiler_params=pltpu.CompilerParams(
            collective_id=0, has_side_effects=True, vmem_limit_bytes=56 * 2**20
        ),
    )(
        latent,
        pixel_mask,
        cotangent,
        res_kernels.reshape(6, 9, C, C),
        up_kernel.reshape(9, C, C),
    )


def solution(mesh):
    in_specs = (P("rows", "cols", None), P("rows", "cols", None), P("rows", "cols"), P(), P())
    out_specs = P("rows", "cols", None)
    return jax.shard_map(
        per_device, mesh=mesh, in_specs=in_specs, out_specs=out_specs, check_vma=False
    )
```

```python
import functools

import jax
import jax.numpy as jnp
from jax import lax
from jax.experimental import pallas as pl
from jax.experimental.pallas import tpu as pltpu
from jax.sharding import PartitionSpec as P

LAYERS = 3
EPS = 1e-06
MESH = pl.DeviceIdType.MESH
F32 = jnp.float32
BF16 = jnp.bfloat16

H, W, C = 8, 64, 256
T = 3
RT = H + 2 * T
WT = W + 8
WB = W + 16
FH, FW = 2 * H, 2 * W
FWT = FW + 16
SIDE = 16
PIXELS = H * W
GROUP = 8


def position():
    c = lax.axis_index("cols")
    r = lax.axis_index("rows")
    core = c % 2
    chip = c // 2
    return c, r, core, chip % 4, chip // 4


def plane_peers():
    c, r, core, x, y = position()
    out = []
    for dy in range(4):
        for dx in range(4):
            if dx or dy:
                far = min(dx, 4 - dx) + min(dy, 4 - dy)
                out.append((far, dy * 4 + dx, (((y + dy) % 4) * 4 + (x + dx) % 4) * 2 + core, r))
    return [p[1:] for p in sorted(out, key=lambda p: -p[0])]


def column_peers():
    c, r, core, x, y = position()
    out = []
    for dz in range(8):
        for dc in range(2):
            if dz or dc:
                far = min(dz, 8 - dz)
                out.append((far, dz * 2 + dc, c - core + (core + dc) % 2, (r + dz) % 8))
    return [p[1:] for p in sorted(out, key=lambda p: -p[0])]


def neighbours():
    c, r, core, x, y = position()
    out = []
    for dr in (-1, 0, 1):
        for dc in (-1, 0, 1):
            if dr or dc:
                out.append((dr, dc, (c + dc + 32) % 32, (r + dr + 8) % 8))
    return out


def halo_copies(field, top, height, width, total, edges, corners, send, recv):
    def spans(step, first, size, end, near, far):
        n = far - near + 1
        if step < 0:
            return pl.ds(first + near - 1, n), pl.ds(first + size + near - 1, n)
        if step > 0:
            return pl.ds(first + size - far, n), pl.ds(end - far, n)
        return pl.ds(first, size), pl.ds(first, size)

    copies = []
    for dr, dc, col, row in neighbours():
        band = corners if dr and dc else edges
        if band is None:
            continue
        src_r, dst_r = spans(dr, top, height, top, *band)
        src_c, dst_c = spans(dc, 0, width, total, *band)
        src, dst = (src_r, src_c, slice(None)), (dst_r, dst_c, slice(None))
        if len(field.shape) == 4:
            src, dst = (slice(None),) + src, (slice(None),) + dst
        copies.append(
            pltpu.make_async_remote_copy(
                src_ref=field.at[src],
                dst_ref=field.at[dst],
                send_sem=send.at[len(copies)],
                recv_sem=recv.at[len(copies)],
                device_id={"cols": col, "rows": row},
                device_id_type=MESH,
            )
        )
    return copies


def phase_start(buf, peers, send, recv):
    for slot, col, row in peers:
        pltpu.make_async_remote_copy(
            src_ref=buf.at[0],
            dst_ref=buf.at[slot],
            send_sem=send,
            recv_sem=recv,
            device_id={"cols": col, "rows": row},
            device_id_type=MESH,
        ).start()


def phase_wait(buf, sem):
    pltpu.make_async_copy(buf.at[pl.ds(1, SIDE - 1)], buf.at[pl.ds(1, SIDE - 1)], sem).wait()


def merge_moments(parts, count):
    mean = jnp.sum(parts[:, 0:2], axis=0) * (1.0 / SIDE)
    delta = parts[:, 0:2] - mean[None]
    square = jnp.sum(parts[:, 2:4] + delta * delta * float(count), axis=0)
    return mean, square


def lane_swap(value, step):
    lane = lax.broadcasted_iota(jnp.int32, value.shape, 1)
    return jnp.where((lane & step) != 0, pltpu.roll(value, step, 1), pltpu.roll(value, 128 - step, 1))


def wide(value):
    return jnp.concatenate([value[0:1], value[1:2]], axis=1).reshape(1, 1, C)


def sigmoid(v):
    return 1.0 / (1.0 + jnp.exp(-v))


def kernel(
    mask, latent_hbm, cot_hbm, res_hbm, up_hbm, out,
    latent, cot, weights, fields, grads, total, pre, fine, slopes, stats, taps, taps_n, box_a, box_b,
    buf_a, buf_b, sum_a, sum_b, cor_own, cor_a, cor_b, cor_c, cor, expanded,
    load_sem, send_a, send_b, recv_a, recv_b, csend, crecv, hsend, hrecv,
):
    c, r, _, px, py = position()
    place = py * 4 + px
    top = jnp.where(r == 0, 0.0, 1.0).astype(F32)
    bottom = jnp.where(r == 7, 0.0, 1.0).astype(F32)
    left = jnp.where(c == 0, 0.0, 1.0).astype(F32)
    right = jnp.where(c == 31, 0.0, 1.0).astype(F32)
    side = lax.broadcasted_iota(jnp.int32, (1, 8, C), 1)
    edge = jnp.where(side < 4, right, left)

    def weight_copy(k):
        return pltpu.make_async_copy(res_hbm.at[k], weights.at[k], load_sem.at[k])

    up_copy = pltpu.make_async_copy(up_hbm, weights.at[6], load_sem.at[6])
    cot_copy = pltpu.make_async_copy(cot_hbm, cot, load_sem.at[7])
    latent_copy = pltpu.make_async_copy(latent_hbm, latent, load_sem.at[8])
    latent_copy.start()
    barrier = pltpu.get_barrier_semaphore()
    plane, column = plane_peers(), column_peers()
    greeted = [p[1:] for p in plane] + [p[1:] for p in column] + [p[2:] for p in neighbours()]
    for col, row in greeted:
        pl.semaphore_signal(barrier, inc=1, device_id={"cols": col, "rows": row}, device_id_type=MESH)

    cot_copy.start()
    weight_copy(0).start()
    up_copy.start()
    for k in range(1, 6):
        weight_copy(k).start()

    def load_stats(k):
        return stats[k, 0:1, :].reshape(1, 1, C), stats[k, 1:2, :].reshape(1, 1, C)

    def normed(k, rows, columns=slice(0, WT)):
        mean, inv = load_stats(k)
        return (fields[k, rows, columns, :] - mean) * inv

    tile_rows, tile_columns = slice(T, T + H), slice(0, W)

    def put_rows(buf, at, first, second):
        buf[at : at + 1, :] = first[:, 0:128]
        buf[at + 1 : at + 2, :] = first[:, 128:256]
        buf[at + 2 : at + 3, :] = second[:, 0:128]
        buf[at + 3 : at + 4, :] = second[:, 128:256]

    def put_moments(k, x):
        mean = jnp.sum(x, axis=(0, 1)).reshape(1, C) * (1.0 / PIXELS)
        delta = x - mean.reshape(1, 1, C)
        square = jnp.sum(delta * delta, axis=(0, 1)).reshape(1, C)
        put_rows(buf_a.at[k, 0], 0, mean, square)

    def put_sums(l, at, d, n):
        first = jnp.sum(d, axis=(0, 1)).reshape(1, C) * (1.0 / PIXELS)
        second = jnp.sum(d * n, axis=(0, 1)).reshape(1, C) * (1.0 / PIXELS)
        put_rows(sum_a.at[l, 0], at, first, second)

    def ring_copies(k):
        return halo_copies(fields.at[k], T, H, W, WT, (1, 1), (1, 3), hsend.at[k], hrecv.at[k])

    def wide_copies(k):
        return halo_copies(fields.at[k], T, H, W, WT, (2, 3), None, hsend.at[k + 6], hrecv.at[k + 6])

    def grad_copies(l):
        return halo_copies(grads.at[l], T, H, W, WT, (1, 3), (1, 3), hsend.at[l + 12], hrecv.at[l + 12])

    def total_copies():
        return halo_copies(total, T, H, W, WT, (1, 2), (1, 2), hsend.at[15], hrecv.at[15])

    def fine_copies():
        return halo_copies(fine, 1, FH, FW, FWT, (1, 1), (1, 1), hsend.at[16], hrecv.at[16])

    def put_taps(make, first, last, columns, dst=taps):
        parts = ((first, T, top), (T, T + H, None), (T + H, last, bottom))
        for begin, end, scale in parts:
            u = make(begin, end - begin)
            if scale is not None:
                u = u * scale
            u = jnp.concatenate([u[:, 0:W], u[:, W:WT] * edge], axis=1)
            at = slice(begin - first, end - first)
            for b, v in enumerate((pltpu.roll(u, 1, 1), u, pltpu.roll(u, WT - 1, 1))):
                if columns > WT:
                    v = jnp.concatenate([v, jnp.zeros((end - begin, columns - WT, C), F32)], axis=1)
                dst[at, 0:columns, b * C : (b + 1) * C] = v[:, 0:columns].astype(BF16)

    def conv(k):
        rows = [taps[a : a + H, 0:W].reshape(PIXELS, 3 * C) for a in range(3)]
        y = jnp.dot(jnp.concatenate(rows, axis=-1), weights[k].reshape(9 * C, C), preferred_element_type=F32)
        return y.reshape(H, W, C)

    def conv_back(piece, k, rows, columns):
        y = None
        for a in range(3):
            for b in range(3):
                d = lax.dot_general(
                    piece(a, b), weights[k, 8 - 3 * a - b], (((1,), (1,)), ((), ())), preferred_element_type=F32
                )
                y = d if y is None else y + d
        return y.reshape(rows, columns, C)

    def tap_conv_back(k, rows, columns):
        parts = []
        chunks = 1 if rows * columns <= PIXELS else 2
        height = rows // chunks
        for begin in range(0, rows, height):

            def piece(a, b):
                at = slice(begin + a, begin + a + height)
                return taps[at, 0:columns, b * C : (b + 1) * C].reshape(height * columns, C)

            parts.append(conv_back(piece, k, height, columns))
        return parts[0] if chunks == 1 else jnp.concatenate(parts, axis=0)

    latent_copy.wait()
    fields[0, tile_rows, tile_columns, :] = latent[...].astype(F32)
    put_moments(0, latent[...].astype(F32))

    def start_a(k):
        phase_start(buf_a.at[k], column, send_a.at[k], recv_a.at[k])
        for copy in ring_copies(k) + wide_copies(k):
            copy.start()

    pl.semaphore_wait(barrier, len(greeted))
    start_a(0)
    cot_copy.wait()

    def mask_row(i, carry):
        row = jnp.broadcast_to(mask[pl.ds(i, 1), :].astype(F32), (FW, FW)).T
        fine[0, i + 1, 0:FW, :] = cot[i, :, 0:128].astype(F32) * row
        fine[1, i + 1, 0:FW, :] = cot[i, :, 128:256].astype(F32) * row
        return carry

    lax.fori_loop(0, FH, mask_row, 0)
    for copy in fine_copies():
        copy.start()

    def slope(k, first, last):
        n = normed(k, slice(first, last))
        s = sigmoid(n)
        slopes[k, first - 1 : last - 1] = s * (1.0 + n * (1.0 - s))

    def boxes():
        for copy in fine_copies():
            copy.wait_recv()
        fine[:, 0] = fine[:, 0] * top
        fine[:, FH + 1] = fine[:, FH + 1] * bottom
        fine[:, :, FW : FW + 8, :] = fine[:, :, FW : FW + 8, :] * right
        fine[:, :, FWT - 8 : FWT, :] = fine[:, :, FWT - 8 : FWT, :] * left

        def pair(i, dst, at):
            even, odd = (
                jnp.concatenate(
                    [fine[h, i, pl.ds(q, WT, 2), :] + fine[h, i + 1, pl.ds(q, WT, 2), :] for h in (0, 1)], axis=1
                )
                for q in (0, 1)
            )
            dst[at, :, 0:C] = (pltpu.roll(odd, 1, 0) + even)[0:W].astype(BF16)
            dst[at, :, C : 2 * C] = (even + odd)[0:W].astype(BF16)
            dst[at, :, 2 * C : 3 * C] = (odd + pltpu.roll(even, WT - 1, 0))[0:W].astype(BF16)

        def body(i, carry):
            pair(2 * i, box_a, i)
            pair(2 * i + 1, box_b, i)
            return carry

        lax.fori_loop(0, H, body, 0)
        pair(2 * H, box_a, H)

    def upper():
        up_copy.wait()

        def piece(a, b):
            at = slice(b * C, (b + 1) * C)
            if a == 1:
                return box_b[:, :, at].reshape(PIXELS, C)
            return box_a[a // 2 : a // 2 + H, :, at].reshape(PIXELS, C)

        total[tile_rows, tile_columns, :] = conv_back(piece, 6, H, W)
        for copy in total_copies():
            copy.start()

    def lift(k):
        put_taps(lambda first, rows: total[first : first + rows], T - 2, T + H + 2, WB)
        pre[...] = tap_conv_back(k, H + 2, WB)[:, 0:WT]

    def correlate(l):
        k = 2 * l
        mean = jnp.concatenate([buf_a[k + 1, 0, 0:1, :], buf_a[k + 1, 0, 1:2, :]], axis=1)

        def plain_slope(first, rows):
            return slopes[k, first - 1 : first - 1 + rows]

        def normed_slope(first, rows):
            return slopes[k, first - 1 : first - 1 + rows] * normed(k, slice(first, first + rows))

        put_taps(plain_slope, T - 1, T + H + 1, W)
        put_taps(normed_slope, T - 1, T + H + 1, W, taps_n)
        x = (fields[k + 1, tile_rows, tile_columns, :] - mean.reshape(1, 1, C)).reshape(PIXELS, C).astype(BF16)
        raw = plain = None
        for b in range(3):
            at = slice(b * C, (b + 1) * C)
            sums = [jnp.sum(src[0 : H + 2, 0:W, at].astype(F32), axis=1) for src in (taps, taps_n)]
            for a in range(3):
                weight = weights[k, 3 * a + b].astype(F32).T
                weight = jnp.concatenate([weight, weight], axis=1)
                q = jnp.concatenate(
                    [src[a : a + H, 0:W, at].reshape(PIXELS, C) for src in (taps, taps_n)], axis=1
                )
                first = lax.dot_general(x, q, (((0,), (0,)), ((), ())), preferred_element_type=F32) * weight
                total_q = jnp.concatenate([jnp.sum(v[a : a + H], axis=0, keepdims=True) for v in sums], axis=1)
                second = total_q * weight
                raw = first if raw is None else raw + first
                plain = second if plain is None else plain + second
        shift = jnp.broadcast_to(mean, (8, C)).T[:, 0:1]
        raw = raw + plain * shift
        row = lax.broadcasted_iota(jnp.int32, (2 * C, 128), 0) // GROUP
        lane = lax.broadcasted_iota(jnp.int32, (2 * C, 128), 1)
        whole = None
        for j, block in enumerate((raw, plain)):
            block = jnp.sum(block.reshape(C // GROUP, GROUP, 2 * C), axis=1) * (1.0 / (PIXELS * SIDE * SIDE * GROUP))
            pick = jnp.where(lane == 64 * j + row, 1.0, 0.0).astype(F32)
            part = jnp.dot(block, pick, precision=lax.Precision.HIGHEST, preferred_element_type=F32)
            whole = part if whole is None else whole + part
        cor[...] = whole
        for i in range(SIDE):
            cor_own[l, i] = cor[2 * i : 2 * i + 2, :]
        for slot, col, row in plane:
            x, y = (col // 2) % 4, col // 8
            pltpu.make_async_remote_copy(
                src_ref=cor_own.at[l, y * 4 + x],
                dst_ref=cor_a.at[l, slot],
                send_sem=csend.at[l],
                recv_sem=crecv.at[l],
                device_id={"cols": col, "rows": row},
                device_id_type=MESH,
            ).start()

    def correlate_b(l):
        phase_wait(cor_a.at[l], crecv.at[l])
        cor_b[l, 0] = cor_own[l, place] + jnp.sum(cor_a[l, 1:SIDE], axis=0)
        phase_start(cor_b.at[l], column, csend.at[l + 3], crecv.at[l + 3])

    def correlate_c(l):
        phase_wait(cor_b.at[l], crecv.at[l + 3])
        cor_c[l, place] = jnp.sum(cor_b[l], axis=0)
        for slot, col, row in plane:
            pltpu.make_async_remote_copy(
                src_ref=cor_c.at[l, place],
                dst_ref=cor_c.at[l, place],
                send_sem=csend.at[l + 6],
                recv_sem=crecv.at[l + 6],
                device_id={"cols": col, "rows": row},
                device_id_type=MESH,
            ).start()

    def expand(l):
        phase_wait(cor_c.at[l], crecv.at[l + 6])
        for i in range(SIDE):
            cor[2 * i : 2 * i + 2, :] = cor_c[l, i]
        whole = cor[...]
        high = whole.astype(BF16)
        low = (whole - high.astype(F32)).astype(BF16)
        group = lax.broadcasted_iota(jnp.int32, (32, C), 1) // GROUP
        spread = jnp.where(lax.broadcasted_iota(jnp.int32, (32, C), 0) == group, 1.0, 0.0).astype(BF16)
        lane = lax.broadcasted_iota(jnp.int32, (128, 2 * C), 0)
        channel = lax.broadcasted_iota(jnp.int32, (128, 2 * C), 1) // GROUP
        for j in range(2):
            pick = jnp.where(lane == 64 * j + channel, 1.0, 0.0).astype(BF16)
            for part, value in enumerate((high, low)):
                block = jnp.dot(value, pick, preferred_element_type=F32).astype(BF16)
                block = lax.dot_general(spread, block, (((0,), (0,)), ((), ())), preferred_element_type=F32)
                expanded[part, j * C : (j + 1) * C, :] = block.astype(BF16)

    def finish_moments(k):
        mean, square = merge_moments(buf_b[k], PIXELS * SIDE)
        count = float(PIXELS * SIDE * SIDE)
        for step in (1, 2, 4):
            other, squares = lane_swap(mean, step), lane_swap(square, step)
            delta = mean - other
            mean = (mean + other) * 0.5
            square = square + squares + delta * delta * (count * 0.5)
            count *= 2.0
        inv = lax.rsqrt(square * (1.0 / count) + EPS)
        mean, inv = wide(mean), wide(inv)
        stats[k, 0:1, :] = mean.reshape(1, C)
        stats[k, 1:2, :] = inv.reshape(1, C)
        return mean, inv

    def forward(k, carry):
        @pl.when(k > 0)
        def _():
            start_a(k)
            slope(k - 1, 1, RT - 1)

        @pl.when(k % 2 == 1)
        def _():
            correlate(k // 2)

        @pl.when((k == 2) | (k == 4))
        def _():
            correlate_c(k // 2 - 1)

        phase_wait(buf_a.at[k], recv_a.at[k])
        mean, square = merge_moments(buf_a[k], PIXELS)
        buf_b[k, 0, 0:2, :] = mean
        buf_b[k, 0, 2:4, :] = square
        phase_start(buf_b.at[k], plane, send_b.at[k], recv_b.at[k])

        @pl.when(k % 2 == 1)
        def _():
            correlate_b(k // 2)

        @pl.when(k == 2)
        def _():
            boxes()
            upper()

        @pl.when(k == 4)
        def _():
            weight_copy(5).wait()
            for copy in total_copies():
                copy.wait()
            lift(5)

        @pl.when(k < 5)
        def _():
            weight_copy(k).wait()

        for copy in ring_copies(k) + wide_copies(k):
            copy.wait_recv()
        phase_wait(buf_b.at[k], recv_b.at[k])
        mean, inv = finish_moments(k)

        @pl.when(k < 5)
        def _():
            def active(first, rows):
                n = (fields[k, first : first + rows] - mean) * inv
                return n * sigmoid(n)

            put_taps(active, T - 1, T + H + 1, W)
            y = conv(k)
            keep = jnp.where(k % 2 == 1, 1.0, 0.0).astype(F32)
            y = y + keep * fields[jnp.maximum(k - 1, 0), tile_rows, tile_columns, :]
            fields[k + 1, tile_rows, tile_columns, :] = y
            put_moments(k + 1, y)

        return carry

    lax.fori_loop(0, 6, forward, 0)
    slope(5, T - 1, T + H + 1)

    def drain(k, carry):
        phase_wait(buf_a.at[k], send_a.at[k])
        phase_wait(buf_b.at[k], send_b.at[k])
        for copy in ring_copies(k) + wide_copies(k):
            copy.wait_send()
        return carry

    def layer(l, last):
        k = 2 * l
        mean1, inv1 = load_stats(k)
        mean2, inv2 = load_stats(k + 1)
        t = 8 - l
        grads[l, tile_rows, tile_columns, :] = (
            pre[1 : H + 1, 0:W] * slopes[k + 1, T - 1 : T - 1 + H, 0:W]
        )
        put_sums(l, 0, grads[l, tile_rows, tile_columns, :], normed(k + 1, tile_rows, tile_columns))

        def unprojected(first, rows):
            at = first - T + 1
            return inv2 * (pre[at : at + rows] * slopes[k + 1, first - 1 : first - 1 + rows])

        put_taps(unprojected, T - 1, T + H + 1, W)
        d = tap_conv_back(k, H, W) * slopes[k, T - 1 : T - 1 + H, 0:W]
        put_sums(l, 4, d, normed(k, tile_rows, tile_columns))
        phase_start(sum_a.at[l], column, send_a.at[t], recv_a.at[t])
        for copy in grad_copies(l):
            copy.start()

        @pl.when(l == 2)
        def _():
            correlate_c(l)

        phase_wait(sum_a.at[l], recv_a.at[t])
        sum_b[l, 0] = jnp.sum(sum_a[l], axis=0) * (1.0 / SIDE)
        phase_start(sum_b.at[l], plane, send_b.at[t], recv_b.at[t])

        expand(l)
        if not last:

            @pl.when(l == 1)
            def _():
                lax.fori_loop(0, 6, drain, 0)

        for copy in grad_copies(l):
            copy.wait_recv()
        phase_wait(sum_b.at[l], recv_b.at[t])
        sums = jnp.sum(sum_b[l], axis=0) * (1.0 / (SIDE * GROUP))
        for step in (1, 2, 4):
            sums = sums + lane_swap(sums, step)
        first2, second2, first1, second1 = (wide(sums[i : i + 2]) for i in (0, 2, 4, 6))
        scaled = inv2 * second2
        source = jnp.concatenate([inv2 * scaled, inv2 * (first2 - mean2 * scaled)], axis=-1).reshape(1, 2 * C)
        source = jnp.broadcast_to(source * (1.0 / GROUP), (16, 2 * C))
        high = source.astype(BF16)
        low = (source - high.astype(F32)).astype(BF16)
        moved = (
            jnp.dot(high, expanded[0], preferred_element_type=F32)
            + jnp.dot(low, expanded[0], preferred_element_type=F32)
            + jnp.dot(high, expanded[1], preferred_element_type=F32)
        )
        first1 = first1 - moved[0:1, 0:C].reshape(1, 1, C)
        second1 = second1 - moved[0:1, C : 2 * C].reshape(1, 1, C)

        def back(first, rows):
            at = slice(first, first + rows)
            return inv2 * (grads[l, at] - first2 - normed(k + 1, at) * second2)

        if last:
            put_taps(back, T - 1, T + H + 1, W)
            d = tap_conv_back(k, H, W) * slopes[k, T - 1 : T - 1 + H, 0:W]
            n = normed(k, tile_rows, tile_columns)
            out[...] = total[tile_rows, tile_columns, :] + inv1 * (d - first1 - n * second1)
        else:
            put_taps(back, 0, RT, WB)
            d = tap_conv_back(k, H + 4, WB)[:, 0:WT] * slopes[k]
            rows = slice(T - 2, T + H + 2)
            total[rows] += inv1 * (d - first1 - normed(k, rows) * second1)
            lift(k - 1)

    def backward(j, carry):
        layer(2 - j, False)
        return carry

    lax.fori_loop(0, 2, backward, 0)
    layer(0, True)

    def drain_back(l, carry):
        phase_wait(sum_a.at[l], send_a.at[8 - l])
        phase_wait(sum_b.at[l], send_b.at[8 - l])
        phase_wait(cor_a.at[l], csend.at[l])
        phase_wait(cor_b.at[l], csend.at[l + 3])
        phase_wait(cor_c.at[l], csend.at[l + 6])
        for copy in grad_copies(l):
            copy.wait_send()
        return carry

    lax.fori_loop(0, 3, drain_back, 0)
    for copy in fine_copies():
        copy.wait_send()


def per_device(latent, cotangent, pixel_mask, res_kernels, up_kernel):
    vmem = pl.BlockSpec(memory_space=pltpu.VMEM)
    hbm = pl.BlockSpec(memory_space=pl.ANY)
    dma = pltpu.SemaphoreType.DMA
    return pl.pallas_call(
        kernel,
        out_shape=jax.ShapeDtypeStruct((H, W, C), F32),
        in_specs=[vmem, hbm, hbm, hbm, hbm],
        out_specs=vmem,
        scratch_shapes=[
            pltpu.VMEM((H, W, C), BF16),
            pltpu.VMEM((FH, FW, C), BF16),
            pltpu.VMEM((7, 9, C, C), BF16),
            pltpu.VMEM((6, RT, WT, C), F32),
            pltpu.VMEM((3, RT, WT, C), F32),
            pltpu.VMEM((RT, WT, C), F32),
            pltpu.VMEM((H + 2, WT, C), F32),
            pltpu.VMEM((2, FH + 2, FWT, 128), F32),
            pltpu.VMEM((6, RT - 2, WT, C), F32),
            pltpu.VMEM((6, 8, C), F32),
            pltpu.VMEM((RT, WB, 3 * C), BF16),
            pltpu.VMEM((H + 2, W, 3 * C), BF16),
            pltpu.VMEM((H + 1, W, 3 * C), BF16),
            pltpu.VMEM((H, W, 3 * C), BF16),
            pltpu.VMEM((6, SIDE, 4, 128), F32),
            pltpu.VMEM((6, SIDE, 4, 128), F32),
            pltpu.VMEM((3, SIDE, 8, 128), F32),
            pltpu.VMEM((3, SIDE, 8, 128), F32),
            pltpu.VMEM((3, SIDE, 2, 128), F32),
            pltpu.VMEM((3, SIDE, 2, 128), F32),
            pltpu.VMEM((3, SIDE, 2, 128), F32),
            pltpu.VMEM((3, SIDE, 2, 128), F32),
            pltpu.VMEM((32, 128), F32),
            pltpu.VMEM((2, 2 * C, 2 * C), BF16),
            dma((9,)),
            dma((9,)),
            dma((9,)),
            dma((9,)),
            dma((9,)),
            dma((9,)),
            dma((9,)),
            dma((17, 8)),
            dma((17, 8)),
        ],
        compiler_params=pltpu.CompilerParams(
            collective_id=0, has_side_effects=True, vmem_limit_bytes=56 * 2**20
        ),
    )(
        pixel_mask,
        latent,
        cotangent,
        res_kernels.reshape(6, 9, C, C),
        up_kernel.reshape(9, C, C),
    )


def solution(mesh):
    in_specs = (P("rows", "cols", None), P("rows", "cols", None), P("rows", "cols"), P(), P())
    out_specs = P("rows", "cols", None)
    return jax.shard_map(
        per_device, mesh=mesh, in_specs=in_specs, out_specs=out_specs, check_vma=False
    )
```

```python
import functools

import jax
import jax.numpy as jnp
from jax import lax
from jax.experimental import pallas as pl
from jax.experimental.pallas import tpu as pltpu
from jax.sharding import PartitionSpec as P

LAYERS = 3
EPS = 1e-06
MESH = pl.DeviceIdType.MESH
F32 = jnp.float32
BF16 = jnp.bfloat16

H, W, C = 8, 64, 256
T = 3
RT = H + 2 * T
WT = W + 8
WB = W + 16
FH, FW = 2 * H, 2 * W
FWT = FW + 16
SIDE = 16
CHIPS = 128
PIXELS = H * W
GROUP = 8


def position():
    c = lax.axis_index("cols")
    r = lax.axis_index("rows")
    core = c % 2
    chip = c // 2
    return c, r, core, chip % 4, chip // 4


def plane_peers():
    c, r, core, x, y = position()
    out = []
    for dy in range(4):
        for dx in range(4):
            if dx or dy:
                far = min(dx, 4 - dx) + min(dy, 4 - dy)
                out.append((far, dy * 4 + dx, (((y + dy) % 4) * 4 + (x + dx) % 4) * 2 + core, r))
    return [p[1:] for p in sorted(out, key=lambda p: -p[0])]


def column_peers():
    c, r, core, x, y = position()
    out = []
    for dz in range(8):
        for dc in range(2):
            if dz or dc:
                far = min(dz, 8 - dz)
                out.append((far, dz * 2 + dc, c - core + (core + dc) % 2, (r + dz) % 8))
    return [p[1:] for p in sorted(out, key=lambda p: -p[0])]


def other_core():
    c, r, core, x, y = position()
    return c - core + (core + 1) % 2, r


def chip_peers(visit):
    c, r, core, x, y = position()
    plane = [(0, c, r)] + plane_peers()[::-1]

    def level(i, carry):
        dz = jnp.where(i % 2 == 0, 4 + i // 2, 4 - (i + 1) // 2)
        row = (r + dz) % 8
        for slot, col, _ in plane[::-1]:
            visit(dz * SIDE + slot, col, row)
        return carry

    lax.fori_loop(0, 7, level, 0)


def neighbours():
    c, r, core, x, y = position()
    out = []
    for dr in (-1, 0, 1):
        for dc in (-1, 0, 1):
            if dr or dc:
                out.append((dr, dc, (c + dc + 32) % 32, (r + dr + 8) % 8))
    return out


def halo_copies(field, top, height, width, total, edges, corners, send, recv):
    def spans(step, first, size, end, near, far):
        n = far - near + 1
        if step < 0:
            return pl.ds(first + near - 1, n), pl.ds(first + size + near - 1, n)
        if step > 0:
            return pl.ds(first + size - far, n), pl.ds(end - far, n)
        return pl.ds(first, size), pl.ds(first, size)

    copies = []
    for dr, dc, col, row in neighbours():
        band = corners if dr and dc else edges
        if band is None:
            continue
        src_r, dst_r = spans(dr, top, height, top, *band)
        src_c, dst_c = spans(dc, 0, width, total, *band)
        src, dst = (src_r, src_c, slice(None)), (dst_r, dst_c, slice(None))
        if len(field.shape) == 4:
            src, dst = (slice(None),) + src, (slice(None),) + dst
        copies.append(
            pltpu.make_async_remote_copy(
                src_ref=field.at[src],
                dst_ref=field.at[dst],
                send_sem=send.at[len(copies)],
                recv_sem=recv.at[len(copies)],
                device_id={"cols": col, "rows": row},
                device_id_type=MESH,
            )
        )
    return copies


def phase_start(buf, peers, send, recv):
    for slot, col, row in peers:
        pltpu.make_async_remote_copy(
            src_ref=buf.at[0],
            dst_ref=buf.at[slot],
            send_sem=send,
            recv_sem=recv,
            device_id={"cols": col, "rows": row},
            device_id_type=MESH,
        ).start()


def phase_wait(buf, sem):
    pltpu.make_async_copy(buf.at[pl.ds(1, SIDE - 1)], buf.at[pl.ds(1, SIDE - 1)], sem).wait()


def lane_swap(value, step):
    lane = lax.broadcasted_iota(jnp.int32, value.shape, 1)
    return jnp.where((lane & step) != 0, pltpu.roll(value, step, 1), pltpu.roll(value, 128 - step, 1))


def own_lanes():
    lane = lax.broadcasted_iota(jnp.int32, (8, 128), 1)
    return (lane & 7) == lax.broadcasted_iota(jnp.int32, (8, 128), 0)


def packed(rows):
    return jnp.sum(jnp.where(own_lanes(), rows, 0.0), axis=0, keepdims=True)


def unpacked(row):
    rows = jnp.where(own_lanes(), jnp.broadcast_to(row, (8, 128)), 0.0)
    for step in (1, 2, 4):
        rows = rows + lane_swap(rows, step)
    return rows


def wide(value):
    return jnp.concatenate([value[0:1], value[1:2]], axis=1).reshape(1, 1, C)


def sigmoid(v):
    return 1.0 / (1.0 + jnp.exp(-v))


def kernel(
    mask, latent_hbm, cot_hbm, res_hbm, up_hbm, out,
    latent, cot, weights, fields, grads, total, pre, fine, slopes, stats, taps, taps_n, box_a, box_b,
    buf_a, buf_b, lines, means, cor_own, cor_a, cor_b, cor_c, cor, expanded,
    load_sem, send_a, send_b, recv_a, recv_b, csend, crecv, hsend, hrecv,
):
    c, r, _, px, py = position()
    place = py * 4 + px
    top = jnp.where(r == 0, 0.0, 1.0).astype(F32)
    bottom = jnp.where(r == 7, 0.0, 1.0).astype(F32)
    left = jnp.where(c == 0, 0.0, 1.0).astype(F32)
    right = jnp.where(c == 31, 0.0, 1.0).astype(F32)
    side = lax.broadcasted_iota(jnp.int32, (1, 8, C), 1)
    edge = jnp.where(side < 4, right, left)

    def weight_copy(k):
        return pltpu.make_async_copy(res_hbm.at[k], weights.at[k], load_sem.at[k])

    up_copy = pltpu.make_async_copy(up_hbm, weights.at[6], load_sem.at[6])
    cot_copy = pltpu.make_async_copy(cot_hbm, cot, load_sem.at[7])
    latent_copy = pltpu.make_async_copy(latent_hbm, latent, load_sem.at[8])
    latent_copy.start()
    barrier = pltpu.get_barrier_semaphore()
    plane, column = plane_peers(), column_peers()

    def greet(slot, col, row):
        pl.semaphore_signal(barrier, inc=1, device_id={"cols": col, "rows": row}, device_id_type=MESH)

    chip_peers(greet)
    greeted = plane + column + [(0,) + p[2:] for p in neighbours()]
    for peer in greeted:
        greet(*peer)

    cot_copy.start()
    weight_copy(0).start()
    up_copy.start()
    for k in range(1, 6):
        weight_copy(k).start()

    def load_stats(k):
        return stats[k, 0:1, :].reshape(1, 1, C), stats[k, 1:2, :].reshape(1, 1, C)

    def normed(k, rows, columns=slice(0, WT)):
        mean, inv = load_stats(k)
        return (fields[k, rows, columns, :] - mean) * inv

    tile_rows, tile_columns = slice(T, T + H), slice(0, W)

    def put_rows(buf, at, first, second):
        buf[at : at + 1, :] = first[:, 0:128]
        buf[at + 1 : at + 2, :] = first[:, 128:256]
        buf[at + 2 : at + 3, :] = second[:, 0:128]
        buf[at + 3 : at + 4, :] = second[:, 128:256]

    def put_moments(k, x):
        mean = jnp.sum(x, axis=(0, 1)).reshape(1, C) * (1.0 / PIXELS)
        delta = x - mean.reshape(1, 1, C)
        square = jnp.sum(delta * delta, axis=(0, 1)).reshape(1, C)
        means[k, 0:1, :] = mean
        put_rows(lines, 0, mean, square)
        mean, square = lines[0:2], lines[2:4]
        count = float(PIXELS)
        for step in (1, 2, 4):
            other, squares = lane_swap(mean, step), lane_swap(square, step)
            delta = mean - other
            mean = (mean + other) * 0.5
            square = square + squares + delta * delta * (count * 0.5)
            count *= 2.0
        lines[0:2] = mean
        lines[2:4] = square
        lines[4:8] = jnp.zeros((4, 128), F32)
        buf_a[k, 0:1, :] = packed(lines[...])

    def put_sums(at, d, n):
        first = jnp.sum(d, axis=(0, 1)).reshape(1, C) * (1.0 / PIXELS)
        second = jnp.sum(d * n, axis=(0, 1)).reshape(1, C) * (1.0 / PIXELS)
        put_rows(lines, at, first, second)

    def pack_sums(t):
        rows = lines[...]
        for step in (1, 2, 4):
            rows = rows + lane_swap(rows, step)
        buf_a[t, 0:1, :] = packed(rows * (1.0 / GROUP))

    def send_all(t, first, then):
        def send(slot, col, row):
            pltpu.make_async_remote_copy(
                src_ref=buf_a.at[t, pl.ds(0, 1)],
                dst_ref=buf_a.at[t, pl.ds(slot, 1)],
                send_sem=send_a.at[t],
                recv_sem=recv_a.at[t],
                device_id={"cols": col, "rows": row},
                device_id_type=MESH,
            ).start()

        chip_peers(send)
        for copy in first:
            copy.start()
        for peer in plane:
            send(*peer)
        for copy in then:
            copy.start()

    def wait_all(t, sem):
        part = buf_a.at[t, pl.ds(1, CHIPS - 1)]
        pltpu.make_async_copy(part, part, sem.at[t]).wait()

    def core_copy(t):
        col, row = other_core()
        return pltpu.make_async_remote_copy(
            src_ref=buf_b.at[t, 0],
            dst_ref=buf_b.at[t, 1],
            send_sem=send_b.at[t],
            recv_sem=recv_b.at[t],
            device_id={"cols": col, "rows": row},
            device_id_type=MESH,
        )

    def swap_cores(t, row):
        buf_b[t, 0] = jnp.broadcast_to(row, (8, 128))
        core_copy(t).start()

    def ring_copies(k):
        return halo_copies(fields.at[k], T, H, W, WT, (1, 1), (1, 3), hsend.at[k], hrecv.at[k])

    def wide_copies(k):
        return halo_copies(fields.at[k], T, H, W, WT, (2, 3), None, hsend.at[k + 6], hrecv.at[k + 6])

    def grad_copies(l):
        return halo_copies(grads.at[l], T, H, W, WT, (1, 3), (1, 3), hsend.at[l + 12], hrecv.at[l + 12])

    def total_copies():
        return halo_copies(total, T, H, W, WT, (1, 2), (1, 2), hsend.at[15], hrecv.at[15])

    def fine_copies():
        return halo_copies(fine, 1, FH, FW, FWT, (1, 1), (1, 1), hsend.at[16], hrecv.at[16])

    def put_taps(make, first, last, columns, dst=taps):
        parts = ((first, T, top), (T, T + H, None), (T + H, last, bottom))
        for begin, end, scale in parts:
            u = make(begin, end - begin)
            if scale is not None:
                u = u * scale
            u = jnp.concatenate([u[:, 0:W], u[:, W:WT] * edge], axis=1)
            at = slice(begin - first, end - first)
            for b, v in enumerate((pltpu.roll(u, 1, 1), u, pltpu.roll(u, WT - 1, 1))):
                if columns > WT:
                    v = jnp.concatenate([v, jnp.zeros((end - begin, columns - WT, C), F32)], axis=1)
                dst[at, 0:columns, b * C : (b + 1) * C] = v[:, 0:columns].astype(BF16)

    def conv(k):
        rows = [taps[a : a + H, 0:W].reshape(PIXELS, 3 * C) for a in range(3)]
        y = jnp.dot(jnp.concatenate(rows, axis=-1), weights[k].reshape(9 * C, C), preferred_element_type=F32)
        return y.reshape(H, W, C)

    def conv_back(piece, k, rows, columns):
        y = None
        for a in range(3):
            for b in range(3):
                d = lax.dot_general(
                    piece(a, b), weights[k, 8 - 3 * a - b], (((1,), (1,)), ((), ())), preferred_element_type=F32
                )
                y = d if y is None else y + d
        return y.reshape(rows, columns, C)

    def tap_conv_back(k, rows, columns):
        parts = []
        chunks = 1 if rows * columns <= PIXELS else 2
        height = rows // chunks
        for begin in range(0, rows, height):

            def piece(a, b):
                at = slice(begin + a, begin + a + height)
                return taps[at, 0:columns, b * C : (b + 1) * C].reshape(height * columns, C)

            parts.append(conv_back(piece, k, height, columns))
        return parts[0] if chunks == 1 else jnp.concatenate(parts, axis=0)

    latent_copy.wait()
    fields[0, tile_rows, tile_columns, :] = latent[...].astype(F32)
    put_moments(0, latent[...].astype(F32))

    def start_a(k):
        send_all(k, ring_copies(k), wide_copies(k))

    pl.semaphore_wait(barrier, CHIPS - SIDE + len(greeted))
    start_a(0)
    cot_copy.wait()

    def mask_row(i, carry):
        row = jnp.broadcast_to(mask[pl.ds(i, 1), :].astype(F32), (FW, FW)).T
        fine[0, i + 1, 0:FW, :] = cot[i, :, 0:128].astype(F32) * row
        fine[1, i + 1, 0:FW, :] = cot[i, :, 128:256].astype(F32) * row
        return carry

    lax.fori_loop(0, FH, mask_row, 0)
    for copy in fine_copies():
        copy.start()

    def slope(k, first, last):
        n = normed(k, slice(first, last))
        s = sigmoid(n)
        slopes[k, first - 1 : last - 1] = s * (1.0 + n * (1.0 - s))

    def boxes():
        for copy in fine_copies():
            copy.wait_recv()
        fine[:, 0] = fine[:, 0] * top
        fine[:, FH + 1] = fine[:, FH + 1] * bottom
        fine[:, :, FW : FW + 8, :] = fine[:, :, FW : FW + 8, :] * right
        fine[:, :, FWT - 8 : FWT, :] = fine[:, :, FWT - 8 : FWT, :] * left

        def pair(i, dst, at):
            even, odd = (
                jnp.concatenate(
                    [fine[h, i, pl.ds(q, WT, 2), :] + fine[h, i + 1, pl.ds(q, WT, 2), :] for h in (0, 1)], axis=1
                )
                for q in (0, 1)
            )
            dst[at, :, 0:C] = (pltpu.roll(odd, 1, 0) + even)[0:W].astype(BF16)
            dst[at, :, C : 2 * C] = (even + odd)[0:W].astype(BF16)
            dst[at, :, 2 * C : 3 * C] = (odd + pltpu.roll(even, WT - 1, 0))[0:W].astype(BF16)

        def body(i, carry):
            pair(2 * i, box_a, i)
            pair(2 * i + 1, box_b, i)
            return carry

        lax.fori_loop(0, H, body, 0)
        pair(2 * H, box_a, H)

    def upper():
        up_copy.wait()

        def piece(a, b):
            at = slice(b * C, (b + 1) * C)
            if a == 1:
                return box_b[:, :, at].reshape(PIXELS, C)
            return box_a[a // 2 : a // 2 + H, :, at].reshape(PIXELS, C)

        total[tile_rows, tile_columns, :] = conv_back(piece, 6, H, W)
        for copy in total_copies():
            copy.start()

    def lift(k):
        put_taps(lambda first, rows: total[first : first + rows], T - 2, T + H + 2, WB)
        pre[...] = tap_conv_back(k, H + 2, WB)[:, 0:WT]

    def correlate(l):
        k = 2 * l
        mean = means[k + 1, 0:1, :]

        def plain_slope(first, rows):
            return slopes[k, first - 1 : first - 1 + rows]

        def normed_slope(first, rows):
            return slopes[k, first - 1 : first - 1 + rows] * normed(k, slice(first, first + rows))

        put_taps(plain_slope, T - 1, T + H + 1, W)
        put_taps(normed_slope, T - 1, T + H + 1, W, taps_n)
        x = (fields[k + 1, tile_rows, tile_columns, :] - mean.reshape(1, 1, C)).reshape(PIXELS, C).astype(BF16)
        raw = plain = None
        for b in range(3):
            at = slice(b * C, (b + 1) * C)
            sums = [jnp.sum(src[0 : H + 2, 0:W, at].astype(F32), axis=1) for src in (taps, taps_n)]
            for a in range(3):
                weight = weights[k, 3 * a + b].astype(F32).T
                weight = jnp.concatenate([weight, weight], axis=1)
                q = jnp.concatenate(
                    [src[a : a + H, 0:W, at].reshape(PIXELS, C) for src in (taps, taps_n)], axis=1
                )
                first = lax.dot_general(x, q, (((0,), (0,)), ((), ())), preferred_element_type=F32) * weight
                total_q = jnp.concatenate([jnp.sum(v[a : a + H], axis=0, keepdims=True) for v in sums], axis=1)
                second = total_q * weight
                raw = first if raw is None else raw + first
                plain = second if plain is None else plain + second
        shift = jnp.broadcast_to(mean, (8, C)).T[:, 0:1]
        raw = raw + plain * shift
        row = lax.broadcasted_iota(jnp.int32, (2 * C, 128), 0) // GROUP
        lane = lax.broadcasted_iota(jnp.int32, (2 * C, 128), 1)
        whole = None
        for j, block in enumerate((raw, plain)):
            block = jnp.sum(block.reshape(C // GROUP, GROUP, 2 * C), axis=1) * (1.0 / (PIXELS * SIDE * SIDE * GROUP))
            pick = jnp.where(lane == 64 * j + row, 1.0, 0.0).astype(F32)
            part = jnp.dot(block, pick, precision=lax.Precision.HIGHEST, preferred_element_type=F32)
            whole = part if whole is None else whole + part
        cor[...] = whole
        for i in range(SIDE):
            cor_own[l, i] = cor[2 * i : 2 * i + 2, :]
        for slot, col, row in plane:
            x, y = (col // 2) % 4, col // 8
            pltpu.make_async_remote_copy(
                src_ref=cor_own.at[l, y * 4 + x],
                dst_ref=cor_a.at[l, slot],
                send_sem=csend.at[l],
                recv_sem=crecv.at[l],
                device_id={"cols": col, "rows": row},
                device_id_type=MESH,
            ).start()

    def correlate_b(l):
        phase_wait(cor_a.at[l], crecv.at[l])
        cor_b[l, 0] = cor_own[l, place] + jnp.sum(cor_a[l, 1:SIDE], axis=0)
        phase_start(cor_b.at[l], column, csend.at[l + 3], crecv.at[l + 3])

    def correlate_c(l):
        phase_wait(cor_b.at[l], crecv.at[l + 3])
        cor_c[l, place] = jnp.sum(cor_b[l], axis=0)
        for slot, col, row in plane:
            pltpu.make_async_remote_copy(
                src_ref=cor_c.at[l, place],
                dst_ref=cor_c.at[l, place],
                send_sem=csend.at[l + 6],
                recv_sem=crecv.at[l + 6],
                device_id={"cols": col, "rows": row},
                device_id_type=MESH,
            ).start()

    def expand(l):
        phase_wait(cor_c.at[l], crecv.at[l + 6])
        for i in range(SIDE):
            cor[2 * i : 2 * i + 2, :] = cor_c[l, i]
        whole = cor[...]
        high = whole.astype(BF16)
        low = (whole - high.astype(F32)).astype(BF16)
        group = lax.broadcasted_iota(jnp.int32, (32, C), 1) // GROUP
        spread = jnp.where(lax.broadcasted_iota(jnp.int32, (32, C), 0) == group, 1.0, 0.0).astype(BF16)
        lane = lax.broadcasted_iota(jnp.int32, (128, 2 * C), 0)
        channel = lax.broadcasted_iota(jnp.int32, (128, 2 * C), 1) // GROUP
        for j in range(2):
            pick = jnp.where(lane == 64 * j + channel, 1.0, 0.0).astype(BF16)
            for part, value in enumerate((high, low)):
                block = jnp.dot(value, pick, preferred_element_type=F32).astype(BF16)
                block = lax.dot_general(spread, block, (((0,), (0,)), ((), ())), preferred_element_type=F32)
                expanded[part, j * C : (j + 1) * C, :] = block.astype(BF16)

    lane = lax.broadcasted_iota(jnp.int32, (1, 128), 1) & 7

    def chips_moments(k):
        parts = buf_a[k]
        total_row = jnp.sum(parts, axis=0, keepdims=True)
        mean = total_row * (1.0 / CHIPS)
        delta = parts - mean
        square = jnp.sum(delta * delta, axis=0, keepdims=True) * float(PIXELS * GROUP)
        return jnp.where(lane < 2, mean, jnp.where(lane < 4, total_row + pltpu.roll(square, 2, 1), 0.0))

    def finish_moments(k):
        mine, theirs = buf_b[k, 0, 0:1], buf_b[k, 1, 0:1]
        delta = mine - theirs
        square = delta * delta * float(PIXELS * GROUP * CHIPS // 2)
        both = jnp.where(lane < 2, (mine + theirs) * 0.5, mine + theirs + pltpu.roll(square, 2, 1))
        rows = unpacked(both)
        mean = rows[0:2]
        inv = lax.rsqrt(rows[2:4] * (1.0 / (PIXELS * GROUP * CHIPS * 2)) + EPS)
        mean, inv = wide(mean), wide(inv)
        stats[k, 0:1, :] = mean.reshape(1, C)
        stats[k, 1:2, :] = inv.reshape(1, C)
        return mean, inv

    def forward(k, carry):
        @pl.when(k > 0)
        def _():
            start_a(k)
            for copy in wide_copies(k - 1)[0::3]:
                copy.wait_recv()
            slope(k - 1, 1, RT - 1)

        @pl.when((k == 3) | (k == 5))
        def _():
            correlate_c(k // 2 - 1)

        @pl.when(k % 2 == 1)
        def _():
            correlate(k // 2)

        @pl.when((k == 2) | (k == 4))
        def _():
            correlate_b(k // 2 - 1)

        @pl.when(k == 2)
        def _():
            boxes()
            upper()

        @pl.when(k == 4)
        def _():
            weight_copy(5).wait()
            for copy in total_copies():
                copy.wait()
            lift(5)

        @pl.when(k < 5)
        def _():
            weight_copy(k).wait()

        wait_all(k, recv_a)
        swap_cores(k, chips_moments(k))
        for copy in ring_copies(k) + wide_copies(k)[1:3]:
            copy.wait_recv()
        core_copy(k).wait_recv()
        mean, inv = finish_moments(k)

        @pl.when(k < 5)
        def _():
            def active(first, rows):
                n = (fields[k, first : first + rows] - mean) * inv
                return n * sigmoid(n)

            put_taps(active, T - 1, T + H + 1, W)
            y = conv(k)
            keep = jnp.where(k % 2 == 1, 1.0, 0.0).astype(F32)
            y = y + keep * fields[jnp.maximum(k - 1, 0), tile_rows, tile_columns, :]
            fields[k + 1, tile_rows, tile_columns, :] = y
            put_moments(k + 1, y)

        return carry

    lax.fori_loop(0, 6, forward, 0)
    slope(5, T - 1, T + H + 1)

    def drain(k, carry):
        wait_all(k, send_a)
        core_copy(k).wait_send()
        for copy in ring_copies(k) + wide_copies(k):
            copy.wait_send()
        return carry

    def layer(l, last):
        k = 2 * l
        mean1, inv1 = load_stats(k)
        mean2, inv2 = load_stats(k + 1)
        t = 8 - l
        grads[l, tile_rows, tile_columns, :] = (
            pre[1 : H + 1, 0:W] * slopes[k + 1, T - 1 : T - 1 + H, 0:W]
        )
        put_sums(0, grads[l, tile_rows, tile_columns, :], normed(k + 1, tile_rows, tile_columns))

        def unprojected(first, rows):
            at = first - T + 1
            return inv2 * (pre[at : at + rows] * slopes[k + 1, first - 1 : first - 1 + rows])

        put_taps(unprojected, T - 1, T + H + 1, W)
        d = tap_conv_back(k, H, W) * slopes[k, T - 1 : T - 1 + H, 0:W]
        put_sums(4, d, normed(k, tile_rows, tile_columns))
        pack_sums(t)
        send_all(t, grad_copies(l), [])

        if last:
            expand(l)
        else:

            @pl.when(l == 2)
            def _():
                correlate_b(l)
                for copy in wide_copies(5)[0::3]:
                    copy.wait_recv()

            @pl.when(l == 1)
            def _():
                expand(l)
                lax.fori_loop(0, 6, drain, 0)

        wait_all(t, recv_a)
        swap_cores(t, jnp.sum(buf_a[t], axis=0, keepdims=True) * (1.0 / CHIPS))
        if not last:

            @pl.when(l == 2)
            def _():
                correlate_c(l)
                expand(l)

        for copy in grad_copies(l):
            copy.wait_recv()
        core_copy(t).wait_recv()
        sums = unpacked((buf_b[t, 0, 0:1] + buf_b[t, 1, 0:1]) * 0.5)
        first2, second2, first1, second1 = (wide(sums[i : i + 2]) for i in (0, 2, 4, 6))
        scaled = inv2 * second2
        source = jnp.concatenate([inv2 * scaled, inv2 * (first2 - mean2 * scaled)], axis=-1).reshape(1, 2 * C)
        source = jnp.broadcast_to(source * (1.0 / GROUP), (16, 2 * C))
        high = source.astype(BF16)
        low = (source - high.astype(F32)).astype(BF16)
        moved = (
            jnp.dot(high, expanded[0], preferred_element_type=F32)
            + jnp.dot(low, expanded[0], preferred_element_type=F32)
            + jnp.dot(high, expanded[1], preferred_element_type=F32)
        )
        first1 = first1 - moved[0:1, 0:C].reshape(1, 1, C)
        second1 = second1 - moved[0:1, C : 2 * C].reshape(1, 1, C)

        def back(first, rows):
            at = slice(first, first + rows)
            return inv2 * (grads[l, at] - first2 - normed(k + 1, at) * second2)

        if last:
            put_taps(back, T - 1, T + H + 1, W)
            d = tap_conv_back(k, H, W) * slopes[k, T - 1 : T - 1 + H, 0:W]
            n = normed(k, tile_rows, tile_columns)
            out[...] = total[tile_rows, tile_columns, :] + inv1 * (d - first1 - n * second1)
        else:
            put_taps(back, 0, RT, WB)
            d = tap_conv_back(k, H + 4, WB)[:, 0:WT] * slopes[k]
            rows = slice(T - 2, T + H + 2)
            total[rows] += inv1 * (d - first1 - normed(k, rows) * second1)
            lift(k - 1)

    def backward(j, carry):
        layer(2 - j, False)
        return carry

    lax.fori_loop(0, 2, backward, 0)
    layer(0, True)

    def drain_back(l, carry):
        wait_all(8 - l, send_a)
        core_copy(8 - l).wait_send()
        phase_wait(cor_a.at[l], csend.at[l])
        phase_wait(cor_b.at[l], csend.at[l + 3])
        phase_wait(cor_c.at[l], csend.at[l + 6])
        for copy in grad_copies(l):
            copy.wait_send()
        return carry

    lax.fori_loop(0, 3, drain_back, 0)
    for copy in fine_copies():
        copy.wait_send()


def per_device(latent, cotangent, pixel_mask, res_kernels, up_kernel):
    vmem = pl.BlockSpec(memory_space=pltpu.VMEM)
    hbm = pl.BlockSpec(memory_space=pl.ANY)
    dma = pltpu.SemaphoreType.DMA
    return pl.pallas_call(
        kernel,
        out_shape=jax.ShapeDtypeStruct((H, W, C), F32),
        in_specs=[vmem, hbm, hbm, hbm, hbm],
        out_specs=vmem,
        scratch_shapes=[
            pltpu.VMEM((H, W, C), BF16),
            pltpu.VMEM((FH, FW, C), BF16),
            pltpu.VMEM((7, 9, C, C), BF16),
            pltpu.VMEM((6, RT, WT, C), F32),
            pltpu.VMEM((3, RT, WT, C), F32),
            pltpu.VMEM((RT, WT, C), F32),
            pltpu.VMEM((H + 2, WT, C), F32),
            pltpu.VMEM((2, FH + 2, FWT, 128), F32),
            pltpu.VMEM((6, RT - 2, WT, C), F32),
            pltpu.VMEM((6, 8, C), F32),
            pltpu.VMEM((RT, WB, 3 * C), BF16),
            pltpu.VMEM((H + 2, W, 3 * C), BF16),
            pltpu.VMEM((H + 1, W, 3 * C), BF16),
            pltpu.VMEM((H, W, 3 * C), BF16),
            pltpu.VMEM((9, CHIPS, 128), F32),
            pltpu.VMEM((9, 2, 8, 128), F32),
            pltpu.VMEM((8, 128), F32),
            pltpu.VMEM((6, 8, C), F32),
            pltpu.VMEM((3, SIDE, 2, 128), F32),
            pltpu.VMEM((3, SIDE, 2, 128), F32),
            pltpu.VMEM((3, SIDE, 2, 128), F32),
            pltpu.VMEM((3, SIDE, 2, 128), F32),
            pltpu.VMEM((32, 128), F32),
            pltpu.VMEM((2, 2 * C, 2 * C), BF16),
            dma((9,)),
            dma((9,)),
            dma((9,)),
            dma((9,)),
            dma((9,)),
            dma((9,)),
            dma((9,)),
            dma((17, 8)),
            dma((17, 8)),
        ],
        compiler_params=pltpu.CompilerParams(
            collective_id=0, has_side_effects=True, vmem_limit_bytes=56 * 2**20
        ),
    )(
        pixel_mask,
        latent,
        cotangent,
        res_kernels.reshape(6, 9, C, C),
        up_kernel.reshape(9, C, C),
    )


def solution(mesh):
    in_specs = (P("rows", "cols", None), P("rows", "cols", None), P("rows", "cols"), P(), P())
    out_specs = P("rows", "cols", None)
    return jax.shard_map(
        per_device, mesh=mesh, in_specs=in_specs, out_specs=out_specs, check_vma=False
    )
```

```python
import functools

import jax
import jax.numpy as jnp
from jax import lax
from jax.experimental import pallas as pl
from jax.experimental.pallas import tpu as pltpu
from jax.sharding import PartitionSpec as P

LAYERS = 3
EPS = 1e-06
MESH = pl.DeviceIdType.MESH
F32 = jnp.float32
BF16 = jnp.bfloat16

H, W, C = 8, 64, 256
T = 3
RT = H + 2 * T
WT = W + 8
WB = W + 16
FH, FW = 2 * H, 2 * W
FWT = FW + 16
SIDE = 16
CHIPS = 128
PIXELS = H * W
GROUP = 8


def position():
    c = lax.axis_index("cols")
    r = lax.axis_index("rows")
    core = c % 2
    chip = c // 2
    return c, r, core, chip % 4, chip // 4


def plane_peers():
    c, r, core, x, y = position()
    out = []
    for dy in range(4):
        for dx in range(4):
            if dx or dy:
                far = min(dx, 4 - dx) + min(dy, 4 - dy)
                out.append((far, dy * 4 + dx, (((y + dy) % 4) * 4 + (x + dx) % 4) * 2 + core, r))
    return [p[1:] for p in sorted(out, key=lambda p: -p[0])]


def column_peers():
    c, r, core, x, y = position()
    out = []
    for dz in range(8):
        for dc in range(2):
            if dz or dc:
                far = min(dz, 8 - dz)
                out.append((far, dz * 2 + dc, c - core + (core + dc) % 2, (r + dz) % 8))
    return [p[1:] for p in sorted(out, key=lambda p: -p[0])]


def other_core():
    c, r, core, x, y = position()
    return c - core + (core + 1) % 2, r


def chip_peers(visit):
    c, r, core, x, y = position()
    plane = [(0, c, r)] + plane_peers()[::-1]

    def level(i, carry):
        dz = jnp.where(i % 2 == 0, 4 + i // 2, 4 - (i + 1) // 2)
        row = (r + dz) % 8
        for slot, col, _ in plane[::-1]:
            visit(dz * SIDE + slot, col, row)
        return carry

    lax.fori_loop(0, 7, level, 0)


def neighbours():
    c, r, core, x, y = position()
    out = []
    for dr in (-1, 0, 1):
        for dc in (-1, 0, 1):
            if dr or dc:
                out.append((dr, dc, (c + dc + 32) % 32, (r + dr + 8) % 8))
    return out


def halo_copies(field, rows, columns, corners, send, recv, top=T, height=H, width=W, total=WT):
    def spans(step, first, size, end, near, far):
        n = far - near + 1
        if step < 0:
            return pl.ds(first + near - 1, n), pl.ds(first + size + near - 1, n)
        if step > 0:
            return pl.ds(first + size - far, n), pl.ds(end - far, n)
        return pl.ds(first, size), pl.ds(first, size)

    copies = []
    for dr, dc, col, row in neighbours():
        band = corners if dr and dc else (rows if dr else columns)
        if band is None:
            continue
        src_r, dst_r = spans(dr, top, height, top, *band)
        src_c, dst_c = spans(dc, 0, width, total, *band)
        src, dst = (src_r, src_c, slice(None)), (dst_r, dst_c, slice(None))
        if len(field.shape) == 4:
            src, dst = (slice(None),) + src, (slice(None),) + dst
        copies.append(
            pltpu.make_async_remote_copy(
                src_ref=field.at[src],
                dst_ref=field.at[dst],
                send_sem=send.at[len(copies)],
                recv_sem=recv.at[len(copies)],
                device_id={"cols": col, "rows": row},
                device_id_type=MESH,
            )
        )
    return copies


def phase_start(buf, peers, send, recv):
    for slot, col, row in peers:
        pltpu.make_async_remote_copy(
            src_ref=buf.at[0],
            dst_ref=buf.at[slot],
            send_sem=send,
            recv_sem=recv,
            device_id={"cols": col, "rows": row},
            device_id_type=MESH,
        ).start()


def phase_wait(buf, sem):
    pltpu.make_async_copy(buf.at[pl.ds(1, SIDE - 1)], buf.at[pl.ds(1, SIDE - 1)], sem).wait()


def lane_swap(value, step):
    lane = lax.broadcasted_iota(jnp.int32, value.shape, 1)
    return jnp.where((lane & step) != 0, pltpu.roll(value, step, 1), pltpu.roll(value, 128 - step, 1))


def own_lanes():
    lane = lax.broadcasted_iota(jnp.int32, (8, 128), 1)
    return (lane & 7) == lax.broadcasted_iota(jnp.int32, (8, 128), 0)


def packed(rows):
    return jnp.sum(jnp.where(own_lanes(), rows, 0.0), axis=0, keepdims=True)


def unpacked(row):
    rows = jnp.where(own_lanes(), jnp.broadcast_to(row, (8, 128)), 0.0)
    for step in (1, 2, 4):
        rows = rows + lane_swap(rows, step)
    return rows


def wide(value):
    return jnp.concatenate([value[0:1], value[1:2]], axis=1).reshape(1, 1, C)


def sigmoid(v):
    return 1.0 / (1.0 + jnp.exp(-v))


def kernel(
    mask, latent_hbm, cot_hbm, res_hbm, up_hbm, out,
    latent, cot, weights, fields, grads, grads_out, grads_in, total, pre, fine, rows_out, rows_in, slopes, stats, taps, taps_n, box_a, box_b,
    buf_a, buf_b, lines, means, cor_own, cor_a, cor_b, cor_c, cor, expanded,
    load_sem, send_a, send_b, recv_a, recv_b, csend, crecv, hsend, hrecv,
):
    c, r, _, px, py = position()
    place = py * 4 + px
    top = jnp.where(r == 0, 0.0, 1.0).astype(F32)
    bottom = jnp.where(r == 7, 0.0, 1.0).astype(F32)
    left = jnp.where(c == 0, 0.0, 1.0).astype(F32)
    right = jnp.where(c == 31, 0.0, 1.0).astype(F32)
    side = lax.broadcasted_iota(jnp.int32, (1, 8, C), 1)
    edge = jnp.where(side < 4, right, left)

    def weight_copy(k):
        return pltpu.make_async_copy(res_hbm.at[k], weights.at[k], load_sem.at[k])

    up_copy = pltpu.make_async_copy(up_hbm, weights.at[6], load_sem.at[6])
    cot_copy = pltpu.make_async_copy(cot_hbm, cot, load_sem.at[7])
    latent_copy = pltpu.make_async_copy(latent_hbm, latent, load_sem.at[8])
    latent_copy.start()
    barrier = pltpu.get_barrier_semaphore()
    plane, column = plane_peers(), column_peers()

    def greet(slot, col, row):
        pl.semaphore_signal(barrier, inc=1, device_id={"cols": col, "rows": row}, device_id_type=MESH)

    chip_peers(greet)
    greeted = plane + column + [(0,) + p[2:] for p in neighbours()]
    for peer in greeted:
        greet(*peer)

    cot_copy.start()
    weight_copy(0).start()
    up_copy.start()
    for k in range(1, 6):
        weight_copy(k).start()

    def load_stats(k):
        return stats[k, 0:1, :].reshape(1, 1, C), stats[k, 1:2, :].reshape(1, 1, C)

    def normed(k, rows, columns=slice(0, WT)):
        mean, inv = load_stats(k)
        return (fields[k, rows, columns, :] - mean) * inv

    tile_rows, tile_columns = slice(T, T + H), slice(0, W)

    def put_rows(buf, at, first, second):
        buf[at : at + 1, :] = first[:, 0:128]
        buf[at + 1 : at + 2, :] = first[:, 128:256]
        buf[at + 2 : at + 3, :] = second[:, 0:128]
        buf[at + 3 : at + 4, :] = second[:, 128:256]

    def put_moments(k, x):
        mean = jnp.sum(x, axis=(0, 1)).reshape(1, C) * (1.0 / PIXELS)
        delta = x - mean.reshape(1, 1, C)
        square = jnp.sum(delta * delta, axis=(0, 1)).reshape(1, C)
        means[k, 0:1, :] = mean
        put_rows(lines, 0, mean, square)
        mean, square = lines[0:2], lines[2:4]
        count = float(PIXELS)
        for step in (1, 2, 4):
            other, squares = lane_swap(mean, step), lane_swap(square, step)
            delta = mean - other
            mean = (mean + other) * 0.5
            square = square + squares + delta * delta * (count * 0.5)
            count *= 2.0
        lines[0:2] = mean
        lines[2:4] = square
        lines[4:8] = jnp.zeros((4, 128), F32)
        buf_a[k, 0:1, :] = packed(lines[...])

    def put_sums(at, d, n):
        first = jnp.sum(d, axis=(0, 1)).reshape(1, C) * (1.0 / PIXELS)
        second = jnp.sum(d * n, axis=(0, 1)).reshape(1, C) * (1.0 / PIXELS)
        put_rows(lines, at, first, second)

    def pack_sums(t):
        rows = lines[...]
        for step in (1, 2, 4):
            rows = rows + lane_swap(rows, step)
        buf_a[t, 0:1, :] = packed(rows * (1.0 / GROUP))

    def send_all(t, first, then):
        def send(slot, col, row):
            pltpu.make_async_remote_copy(
                src_ref=buf_a.at[t, pl.ds(0, 1)],
                dst_ref=buf_a.at[t, pl.ds(slot, 1)],
                send_sem=send_a.at[t],
                recv_sem=recv_a.at[t],
                device_id={"cols": col, "rows": row},
                device_id_type=MESH,
            ).start()

        chip_peers(send)
        for copy in first:
            copy.start()
        for peer in plane:
            send(*peer)
        for copy in then:
            copy.start()

    def wait_all(t, sem):
        part = buf_a.at[t, pl.ds(1, CHIPS - 1)]
        pltpu.make_async_copy(part, part, sem.at[t]).wait()

    def core_copy(t):
        col, row = other_core()
        return pltpu.make_async_remote_copy(
            src_ref=buf_b.at[t, 0],
            dst_ref=buf_b.at[t, 1],
            send_sem=send_b.at[t],
            recv_sem=recv_b.at[t],
            device_id={"cols": col, "rows": row},
            device_id_type=MESH,
        )

    def swap_cores(t, row):
        buf_b[t, 0] = jnp.broadcast_to(row, (8, 128))
        core_copy(t).start()

    def ring_copies(k):
        return halo_copies(fields.at[k], (1, 1), (1, 3), (1, 3), hsend.at[k], hrecv.at[k])

    def wide_copies(k):
        return halo_copies(fields.at[k], (2, 3), None, None, hsend.at[k + 6], hrecv.at[k + 6])

    def grad_copies(l, last):
        far = 1 if last else 3
        copies = halo_copies(grads.at[l], None, (1, far), (1, far), hsend.at[l + 12], hrecv.at[l + 12])
        c, r, _, _, _ = position()
        for i, (first, dst_first) in enumerate(((0, 0), (H - far, 3 - far))):
            copies.append(
                pltpu.make_async_remote_copy(
                    src_ref=grads_out.at[l, pl.ds(first, far)],
                    dst_ref=grads_in.at[l, 1 - i, pl.ds(dst_first, far)],
                    send_sem=hsend.at[l + 12, 6 + i],
                    recv_sem=hrecv.at[l + 12, 6 + i],
                    device_id={"cols": c, "rows": (r + 2 * i + 7) % 8},
                    device_id_type=MESH,
                )
            )
        return copies

    def total_copies():
        return halo_copies(total, (1, 2), (1, 2), (1, 2), hsend.at[15], hrecv.at[15])

    def fine_copies():
        copies = []
        for i, (dr, dc, col, row) in enumerate(neighbours()):
            if dc == 0:
                src, dst = rows_out.at[max(dr, 0)], rows_in.at[max(-dr, 0)]
            else:
                src_r = pl.ds(1, FH) if dr == 0 else (pl.ds(1, 1) if dr < 0 else pl.ds(FH, 1))
                dst_r = pl.ds(1, FH) if dr == 0 else (pl.ds(FH + 1, 1) if dr < 0 else pl.ds(0, 1))
                src = fine.at[:, src_r, pl.ds(0 if dc < 0 else FW - 1, 1), :]
                dst = fine.at[:, dst_r, pl.ds(FW if dc < 0 else FWT - 1, 1), :]
            copies.append(
                pltpu.make_async_remote_copy(
                    src_ref=src,
                    dst_ref=dst,
                    send_sem=hsend.at[16, i],
                    recv_sem=hrecv.at[16, i],
                    device_id={"cols": col, "rows": row},
                    device_id_type=MESH,
                )
            )
        return copies

    def put_taps(make, first, last, columns, dst=taps):
        parts = ((first, T, top), (T, T + H, None), (T + H, last, bottom))
        for begin, end, scale in parts:
            u = make(begin, end - begin)
            if scale is not None:
                u = u * scale
            u = jnp.concatenate([u[:, 0:W], u[:, W:WT] * edge], axis=1)
            at = slice(begin - first, end - first)
            for b, v in enumerate((pltpu.roll(u, 1, 1), u, pltpu.roll(u, WT - 1, 1))):
                if columns > WT:
                    v = jnp.concatenate([v, jnp.zeros((end - begin, columns - WT, C), F32)], axis=1)
                dst[at, 0:columns, b * C : (b + 1) * C] = v[:, 0:columns].astype(BF16)

    def conv(k):
        rows = [taps[a : a + H, 0:W].reshape(PIXELS, 3 * C) for a in range(3)]
        y = jnp.dot(jnp.concatenate(rows, axis=-1), weights[k].reshape(9 * C, C), preferred_element_type=F32)
        return y.reshape(H, W, C)

    def conv_back(piece, k, rows, columns):
        y = None
        for a in range(3):
            for b in range(3):
                d = lax.dot_general(
                    piece(a, b), weights[k, 8 - 3 * a - b], (((1,), (1,)), ((), ())), preferred_element_type=F32
                )
                y = d if y is None else y + d
        return y.reshape(rows, columns, C)

    def tap_conv_back(k, rows, columns):
        parts = []
        chunks = 1 if rows * columns <= PIXELS else 2
        height = rows // chunks
        for begin in range(0, rows, height):

            def piece(a, b):
                at = slice(begin + a, begin + a + height)
                return taps[at, 0:columns, b * C : (b + 1) * C].reshape(height * columns, C)

            parts.append(conv_back(piece, k, height, columns))
        return parts[0] if chunks == 1 else jnp.concatenate(parts, axis=0)

    latent_copy.wait()
    fields[0, tile_rows, tile_columns, :] = latent[...].astype(F32)
    put_moments(0, latent[...].astype(F32))

    def start_a(k):
        send_all(k, ring_copies(k), wide_copies(k))

    pl.semaphore_wait(barrier, CHIPS - SIDE + len(greeted))
    send_all(0, ring_copies(0), wide_copies(0))
    cot_copy.wait()

    def mask_row(i, carry):
        row = jnp.broadcast_to(mask[pl.ds(i, 1), :].astype(F32), (FW, FW)).T
        fine[0, i + 1, 0:FW, :] = cot[i, :, 0:128].astype(F32) * row
        fine[1, i + 1, 0:FW, :] = cot[i, :, 128:256].astype(F32) * row
        return carry

    lax.fori_loop(0, FH, mask_row, 0)
    for i, at in enumerate((1, FH)):
        rows_out[i] = jnp.concatenate([fine[0, at, 0:FW, :], fine[1, at, 0:FW, :]], axis=1).astype(BF16)
    for copy in fine_copies():
        copy.start()

    def slope(k, first, last):
        n = normed(k, slice(first, last))
        s = sigmoid(n)
        slopes[k, first - 1 : last - 1] = s * (1.0 + n * (1.0 - s))

    def boxes():
        for copy in fine_copies():
            copy.wait_recv()
        for i, (at, scale) in enumerate(((0, top), (FH + 1, bottom))):
            edge_row = rows_in[i].astype(F32) * scale
            fine[0, at, 0:FW, :] = edge_row[:, 0:128]
            fine[1, at, 0:FW, :] = edge_row[:, 128:256]
            fine[:, at, FW:FWT, :] = fine[:, at, FW:FWT, :] * scale
        fine[:, :, FW : FW + 8, :] = fine[:, :, FW : FW + 8, :] * right
        fine[:, :, FWT - 8 : FWT, :] = fine[:, :, FWT - 8 : FWT, :] * left

        def pair(i, dst, at):
            even, odd = (
                jnp.concatenate(
                    [fine[h, i, pl.ds(q, WT, 2), :] + fine[h, i + 1, pl.ds(q, WT, 2), :] for h in (0, 1)], axis=1
                )
                for q in (0, 1)
            )
            dst[at, :, 0:C] = (pltpu.roll(odd, 1, 0) + even)[0:W].astype(BF16)
            dst[at, :, C : 2 * C] = (even + odd)[0:W].astype(BF16)
            dst[at, :, 2 * C : 3 * C] = (odd + pltpu.roll(even, WT - 1, 0))[0:W].astype(BF16)

        def body(i, carry):
            pair(2 * i, box_a, i)
            pair(2 * i + 1, box_b, i)
            return carry

        lax.fori_loop(0, H, body, 0)
        pair(2 * H, box_a, H)

    def upper():
        up_copy.wait()

        def piece(a, b):
            at = slice(b * C, (b + 1) * C)
            if a == 1:
                return box_b[:, :, at].reshape(PIXELS, C)
            return box_a[a // 2 : a // 2 + H, :, at].reshape(PIXELS, C)

        total[tile_rows, tile_columns, :] = conv_back(piece, 6, H, W)
        for copy in total_copies():
            copy.start()

    def lift(k):
        put_taps(lambda first, rows: total[first : first + rows], T - 2, T + H + 2, WB)
        pre[...] = tap_conv_back(k, H + 2, WB)[:, 0:WT]

    def correlate(l):
        k = 2 * l
        mean = means[k + 1, 0:1, :]

        def plain_slope(first, rows):
            return slopes[k, first - 1 : first - 1 + rows]

        def normed_slope(first, rows):
            return slopes[k, first - 1 : first - 1 + rows] * normed(k, slice(first, first + rows))

        put_taps(plain_slope, T - 1, T + H + 1, W)
        put_taps(normed_slope, T - 1, T + H + 1, W, taps_n)
        x = (fields[k + 1, tile_rows, tile_columns, :] - mean.reshape(1, 1, C)).reshape(PIXELS, C).astype(BF16)
        raw = plain = None
        for b in range(3):
            at = slice(b * C, (b + 1) * C)
            sums = [jnp.sum(src[0 : H + 2, 0:W, at].astype(F32), axis=1) for src in (taps, taps_n)]
            for a in range(3):
                weight = weights[k, 3 * a + b].astype(F32).T
                weight = jnp.concatenate([weight, weight], axis=1)
                q = jnp.concatenate(
                    [src[a : a + H, 0:W, at].reshape(PIXELS, C) for src in (taps, taps_n)], axis=1
                )
                first = lax.dot_general(x, q, (((0,), (0,)), ((), ())), preferred_element_type=F32) * weight
                total_q = jnp.concatenate([jnp.sum(v[a : a + H], axis=0, keepdims=True) for v in sums], axis=1)
                second = total_q * weight
                raw = first if raw is None else raw + first
                plain = second if plain is None else plain + second
        shift = jnp.broadcast_to(mean, (8, C)).T[:, 0:1]
        raw = raw + plain * shift
        row = lax.broadcasted_iota(jnp.int32, (2 * C, 128), 0) // GROUP
        lane = lax.broadcasted_iota(jnp.int32, (2 * C, 128), 1)
        whole = None
        for j, block in enumerate((raw, plain)):
            block = jnp.sum(block.reshape(C // GROUP, GROUP, 2 * C), axis=1) * (1.0 / (PIXELS * SIDE * SIDE * GROUP))
            pick = jnp.where(lane == 64 * j + row, 1.0, 0.0).astype(F32)
            part = jnp.dot(block, pick, precision=lax.Precision.HIGHEST, preferred_element_type=F32)
            whole = part if whole is None else whole + part
        cor[...] = whole
        for i in range(SIDE):
            cor_own[l, i] = cor[2 * i : 2 * i + 2, :]
        for slot, col, row in plane:
            x, y = (col // 2) % 4, col // 8
            pltpu.make_async_remote_copy(
                src_ref=cor_own.at[l, y * 4 + x],
                dst_ref=cor_a.at[l, slot],
                send_sem=csend.at[l],
                recv_sem=crecv.at[l],
                device_id={"cols": col, "rows": row},
                device_id_type=MESH,
            ).start()

    def correlate_b(l):
        phase_wait(cor_a.at[l], crecv.at[l])
        cor_b[l, 0] = cor_own[l, place] + jnp.sum(cor_a[l, 1:SIDE], axis=0)
        phase_start(cor_b.at[l], column, csend.at[l + 3], crecv.at[l + 3])

    def correlate_c(l):
        phase_wait(cor_b.at[l], crecv.at[l + 3])
        cor_c[l, place] = jnp.sum(cor_b[l], axis=0)
        for slot, col, row in plane:
            pltpu.make_async_remote_copy(
                src_ref=cor_c.at[l, place],
                dst_ref=cor_c.at[l, place],
                send_sem=csend.at[l + 6],
                recv_sem=crecv.at[l + 6],
                device_id={"cols": col, "rows": row},
                device_id_type=MESH,
            ).start()

    def expand(l):
        phase_wait(cor_c.at[l], crecv.at[l + 6])
        for i in range(SIDE):
            cor[2 * i : 2 * i + 2, :] = cor_c[l, i]
        whole = cor[...]
        high = whole.astype(BF16)
        low = (whole - high.astype(F32)).astype(BF16)
        group = lax.broadcasted_iota(jnp.int32, (32, C), 1) // GROUP
        spread = jnp.where(lax.broadcasted_iota(jnp.int32, (32, C), 0) == group, 1.0, 0.0).astype(BF16)
        lane = lax.broadcasted_iota(jnp.int32, (128, 2 * C), 0)
        channel = lax.broadcasted_iota(jnp.int32, (128, 2 * C), 1) // GROUP
        for j in range(2):
            pick = jnp.where(lane == 64 * j + channel, 1.0, 0.0).astype(BF16)
            for part, value in enumerate((high, low)):
                block = jnp.dot(value, pick, preferred_element_type=F32).astype(BF16)
                block = lax.dot_general(spread, block, (((0,), (0,)), ((), ())), preferred_element_type=F32)
                expanded[part, j * C : (j + 1) * C, :] = block.astype(BF16)

    lane = lax.broadcasted_iota(jnp.int32, (1, 128), 1) & 7

    def chips_moments(k):
        parts = buf_a[k]
        total_row = jnp.sum(parts, axis=0, keepdims=True)
        mean = total_row * (1.0 / CHIPS)
        delta = parts - mean
        square = jnp.sum(delta * delta, axis=0, keepdims=True) * float(PIXELS * GROUP)
        return jnp.where(lane < 2, mean, jnp.where(lane < 4, total_row + pltpu.roll(square, 2, 1), 0.0))

    def finish_moments(k):
        mine, theirs = buf_b[k, 0, 0:1], buf_b[k, 1, 0:1]
        delta = mine - theirs
        square = delta * delta * float(PIXELS * GROUP * CHIPS // 2)
        both = jnp.where(lane < 2, (mine + theirs) * 0.5, mine + theirs + pltpu.roll(square, 2, 1))
        rows = unpacked(both)
        mean = rows[0:2]
        inv = lax.rsqrt(rows[2:4] * (1.0 / (PIXELS * GROUP * CHIPS * 2)) + EPS)
        mean, inv = wide(mean), wide(inv)
        stats[k, 0:1, :] = mean.reshape(1, C)
        stats[k, 1:2, :] = inv.reshape(1, C)
        return mean, inv

    def forward(k, carry):
        @pl.when(k > 0)
        def _():
            start_a(k)
            for copy in wide_copies(k - 1):
                copy.wait_recv()
            slope(k - 1, 1, RT - 1)

        @pl.when((k == 3) | (k == 5))
        def _():
            correlate_c(k // 2 - 1)

        @pl.when(k % 2 == 1)
        def _():
            correlate(k // 2)

        @pl.when((k == 2) | (k == 4))
        def _():
            correlate_b(k // 2 - 1)

        @pl.when(k == 2)
        def _():
            boxes()
            upper()

        @pl.when(k == 4)
        def _():
            weight_copy(5).wait()
            for copy in total_copies():
                copy.wait()
            lift(5)

        @pl.when(k < 5)
        def _():
            weight_copy(k).wait()

        wait_all(k, recv_a)
        swap_cores(k, chips_moments(k))
        for copy in ring_copies(k):
            copy.wait_recv()
        core_copy(k).wait_recv()
        mean, inv = finish_moments(k)

        @pl.when(k < 5)
        def _():
            def active(first, rows):
                n = (fields[k, first : first + rows] - mean) * inv
                return n * sigmoid(n)

            put_taps(active, T - 1, T + H + 1, W)
            y = conv(k)
            keep = jnp.where(k % 2 == 1, 1.0, 0.0).astype(F32)
            y = y + keep * fields[jnp.maximum(k - 1, 0), tile_rows, tile_columns, :]
            fields[k + 1, tile_rows, tile_columns, :] = y
            put_moments(k + 1, y)

        return carry

    lax.fori_loop(0, 6, forward, 0)
    slope(5, T - 1, T + H + 1)

    def drain(k, carry):
        wait_all(k, send_a)
        core_copy(k).wait_send()
        for copy in ring_copies(k) + wide_copies(k):
            copy.wait_send()
        return carry

    def layer(l, last):
        k = 2 * l
        mean1, inv1 = load_stats(k)
        mean2, inv2 = load_stats(k + 1)
        t = 8 - l
        grads[l, tile_rows, tile_columns, :] = (
            pre[1 : H + 1, 0:W] * slopes[k + 1, T - 1 : T - 1 + H, 0:W]
        )
        grads_out[l] = grads[l, tile_rows, tile_columns, :].astype(BF16)
        put_sums(0, grads[l, tile_rows, tile_columns, :], normed(k + 1, tile_rows, tile_columns))

        def unprojected(first, rows):
            at = first - T + 1
            return inv2 * (pre[at : at + rows] * slopes[k + 1, first - 1 : first - 1 + rows])

        put_taps(unprojected, T - 1, T + H + 1, W)
        d = tap_conv_back(k, H, W) * slopes[k, T - 1 : T - 1 + H, 0:W]
        put_sums(4, d, normed(k, tile_rows, tile_columns))
        pack_sums(t)
        send_all(t, grad_copies(l, last), [])

        if last:
            expand(l)
        else:

            @pl.when(l == 2)
            def _():
                correlate_b(l)
                for copy in wide_copies(5):
                    copy.wait_recv()

            @pl.when(l == 1)
            def _():
                expand(l)
                lax.fori_loop(0, 6, drain, 0)

        wait_all(t, recv_a)
        swap_cores(t, jnp.sum(buf_a[t], axis=0, keepdims=True) * (1.0 / CHIPS))
        if not last:

            @pl.when(l == 2)
            def _():
                correlate_c(l)

        for copy in grad_copies(l, last):
            copy.wait_recv()
        far = 1 if last else 3
        grads[l, T - far : T, tile_columns, :] = grads_in[l, 0, 3 - far : 3].astype(F32)
        grads[l, T + H : T + H + far, tile_columns, :] = grads_in[l, 1, 0:far].astype(F32)
        core_copy(t).wait_recv()
        sums = unpacked((buf_b[t, 0, 0:1] + buf_b[t, 1, 0:1]) * 0.5)
        first2, second2, first1_raw, second1_raw = (wide(sums[i : i + 2]) for i in (0, 2, 4, 6))
        def second_sums():
            scaled = inv2 * second2
            source = jnp.concatenate([inv2 * scaled, inv2 * (first2 - mean2 * scaled)], axis=-1).reshape(1, 2 * C)
            source = jnp.broadcast_to(source * (1.0 / GROUP), (16, 2 * C))
            high = source.astype(BF16)
            low = (source - high.astype(F32)).astype(BF16)
            moved = (
                jnp.dot(high, expanded[0], preferred_element_type=F32)
                + jnp.dot(low, expanded[0], preferred_element_type=F32)
                + jnp.dot(high, expanded[1], preferred_element_type=F32)
            )
            first1_left = first1_raw - moved[0:1, 0:C].reshape(1, 1, C)
            second1_left = second1_raw - moved[0:1, C : 2 * C].reshape(1, 1, C)
            return first1_left, second1_left

        def back(first, rows):
            at = slice(first, first + rows)
            return inv2 * (grads[l, at] - first2 - normed(k + 1, at) * second2)

        if last:
            put_taps(back, T - 1, T + H + 1, W)
            d = tap_conv_back(k, H, W) * slopes[k, T - 1 : T - 1 + H, 0:W]
            n = normed(k, tile_rows, tile_columns)
            first1, second1 = second_sums()
            out[...] = total[tile_rows, tile_columns, :] + inv1 * (d - first1 - n * second1)
        else:
            put_taps(back, 0, RT, WB)
            d = tap_conv_back(k, H + 4, WB)[:, 0:WT] * slopes[k]
            rows = slice(T - 2, T + H + 2)

            @pl.when(l == 2)
            def _():
                expand(l)

            first1, second1 = second_sums()
            total[rows] += inv1 * (d - first1 - normed(k, rows) * second1)
            lift(k - 1)

    def backward(j, carry):
        layer(2 - j, False)
        return carry

    lax.fori_loop(0, 2, backward, 0)
    layer(0, True)

    for l in range(3):
        wait_all(8 - l, send_a)
        core_copy(8 - l).wait_send()
        phase_wait(cor_a.at[l], csend.at[l])
        phase_wait(cor_b.at[l], csend.at[l + 3])
        phase_wait(cor_c.at[l], csend.at[l + 6])
        for copy in grad_copies(l, l == 0):
            copy.wait_send()
    for copy in fine_copies():
        copy.wait_send()


def per_device(latent, cotangent, pixel_mask, res_kernels, up_kernel):
    vmem = pl.BlockSpec(memory_space=pltpu.VMEM)
    hbm = pl.BlockSpec(memory_space=pl.ANY)
    dma = pltpu.SemaphoreType.DMA
    return pl.pallas_call(
        kernel,
        out_shape=jax.ShapeDtypeStruct((H, W, C), F32),
        in_specs=[vmem, hbm, hbm, hbm, hbm],
        out_specs=vmem,
        scratch_shapes=[
            pltpu.VMEM((H, W, C), BF16),
            pltpu.VMEM((FH, FW, C), BF16),
            pltpu.VMEM((7, 9, C, C), BF16),
            pltpu.VMEM((6, RT, WT, C), F32),
            pltpu.VMEM((3, RT, WT, C), F32),
            pltpu.VMEM((3, H, W, C), BF16),
            pltpu.VMEM((3, 2, 3, W, C), BF16),
            pltpu.VMEM((RT, WT, C), F32),
            pltpu.VMEM((H + 2, WT, C), F32),
            pltpu.VMEM((2, FH + 2, FWT, 128), F32),
            pltpu.VMEM((2, FW, C), BF16),
            pltpu.VMEM((2, FW, C), BF16),
            pltpu.VMEM((6, RT - 2, WT, C), F32),
            pltpu.VMEM((6, 8, C), F32),
            pltpu.VMEM((RT, WB, 3 * C), BF16),
            pltpu.VMEM((H + 2, W, 3 * C), BF16),
            pltpu.VMEM((H + 1, W, 3 * C), BF16),
            pltpu.VMEM((H, W, 3 * C), BF16),
            pltpu.VMEM((9, CHIPS, 128), F32),
            pltpu.VMEM((9, 2, 8, 128), F32),
            pltpu.VMEM((8, 128), F32),
            pltpu.VMEM((6, 8, C), F32),
            pltpu.VMEM((3, SIDE, 2, 128), F32),
            pltpu.VMEM((3, SIDE, 2, 128), F32),
            pltpu.VMEM((3, SIDE, 2, 128), F32),
            pltpu.VMEM((3, SIDE, 2, 128), F32),
            pltpu.VMEM((32, 128), F32),
            pltpu.VMEM((2, 2 * C, 2 * C), BF16),
            dma((9,)),
            dma((9,)),
            dma((9,)),
            dma((9,)),
            dma((9,)),
            dma((9,)),
            dma((9,)),
            dma((17, 8)),
            dma((17, 8)),
        ],
        compiler_params=pltpu.CompilerParams(
            collective_id=0, has_side_effects=True, vmem_limit_bytes=56 * 2**20
        ),
    )(
        pixel_mask,
        latent,
        cotangent,
        res_kernels.reshape(6, 9, C, C),
        up_kernel.reshape(9, C, C),
    )


def solution(mesh):
    in_specs = (P("rows", "cols", None), P("rows", "cols", None), P("rows", "cols"), P(), P())
    out_specs = P("rows", "cols", None)
    return jax.shard_map(
        per_device, mesh=mesh, in_specs=in_specs, out_specs=out_specs, check_vma=False
    )
```

```python
import functools

import jax
import jax.numpy as jnp
from jax import lax
from jax.experimental import pallas as pl
from jax.experimental.pallas import tpu as pltpu
from jax.sharding import PartitionSpec as P

LAYERS = 3
EPS = 1e-06
MESH = pl.DeviceIdType.MESH
F32 = jnp.float32
BF16 = jnp.bfloat16

H, W, C = 8, 64, 256
T = 3
RT = H + 2 * T
WT = W + 8
WB = W + 16
FH, FW = 2 * H, 2 * W
FWT = FW + 16
SIDE = 16
HALF = 64
OWN = 3 * SIDE
PIXELS = H * W
GROUP = 8


def position():
    c = lax.axis_index("cols")
    r = lax.axis_index("rows")
    core = c % 2
    chip = c // 2
    return c, r, core, chip % 4, chip // 4


def plane_peers():
    c, r, core, x, y = position()
    out = []
    for dy in range(4):
        for dx in range(4):
            if dx or dy:
                far = min(dx, 4 - dx) + min(dy, 4 - dy)
                out.append((far, dy * 4 + dx, (((y + dy) % 4) * 4 + (x + dx) % 4) * 2 + core, r))
    return [p[1:] for p in sorted(out, key=lambda p: -p[0])]


def column_peers():
    c, r, core, x, y = position()
    out = []
    for dz in range(8):
        for dc in range(2):
            if dz or dc:
                far = min(dz, 8 - dz)
                out.append((far, dz * 2 + dc, c - core + (core + dc) % 2, (r + dz) % 8))
    return [p[1:] for p in sorted(out, key=lambda p: -p[0])]


def other_core():
    c, r, core, x, y = position()
    return c - core + (core + 1) % 2, r


def chip_peers(visit):
    c, r, core, x, y = position()
    plane = plane_peers()

    def level(i):
        even = jnp.where(i == 0, 4, jnp.where(i == 1, 2, jnp.where(i == 2, 6, 0)))
        odd = jnp.where(i == 0, 3, jnp.where(i == 1, 5, jnp.where(i == 2, 1, 7)))
        row = (r + jnp.where(core == 0, even, odd)) % 8
        for slot, col, _ in plane:
            visit(i * SIDE + slot, col, row)
        return row

    def whole_level(i, carry):
        row = level(i)
        visit(i * SIDE, c, row)
        return carry

    lax.fori_loop(0, 3, whole_level, 0)
    row = level(3)

    @pl.when(core == 1)
    def _():
        visit(OWN, c, row)


def neighbours():
    c, r, core, x, y = position()
    out = []
    for dr in (-1, 0, 1):
        for dc in (-1, 0, 1):
            if dr or dc:
                out.append((dr, dc, (c + dc + 32) % 32, (r + dr + 8) % 8))
    return out


def halo_copies(field, rows, columns, corners, send, recv, top=T, height=H, width=W, total=WT):
    def spans(step, first, size, end, near, far):
        n = far - near + 1
        if step < 0:
            return pl.ds(first + near - 1, n), pl.ds(first + size + near - 1, n)
        if step > 0:
            return pl.ds(first + size - far, n), pl.ds(end - far, n)
        return pl.ds(first, size), pl.ds(first, size)

    copies = []
    for dr, dc, col, row in neighbours():
        band = corners if dr and dc else (rows if dr else columns)
        if band is None:
            continue
        src_r, dst_r = spans(dr, top, height, top, *band)
        src_c, dst_c = spans(dc, 0, width, total, *band)
        src, dst = (src_r, src_c, slice(None)), (dst_r, dst_c, slice(None))
        if len(field.shape) == 4:
            src, dst = (slice(None),) + src, (slice(None),) + dst
        copies.append(
            pltpu.make_async_remote_copy(
                src_ref=field.at[src],
                dst_ref=field.at[dst],
                send_sem=send.at[len(copies)],
                recv_sem=recv.at[len(copies)],
                device_id={"cols": col, "rows": row},
                device_id_type=MESH,
            )
        )
    return copies


def phase_start(buf, peers, send, recv):
    for slot, col, row in peers:
        pltpu.make_async_remote_copy(
            src_ref=buf.at[0],
            dst_ref=buf.at[slot],
            send_sem=send,
            recv_sem=recv,
            device_id={"cols": col, "rows": row},
            device_id_type=MESH,
        ).start()


def phase_wait(buf, sem):
    pltpu.make_async_copy(buf.at[pl.ds(1, SIDE - 1)], buf.at[pl.ds(1, SIDE - 1)], sem).wait()


def lane_swap(value, step):
    lane = lax.broadcasted_iota(jnp.int32, value.shape, 1)
    return jnp.where((lane & step) != 0, pltpu.roll(value, step, 1), pltpu.roll(value, 128 - step, 1))


def own_lanes():
    lane = lax.broadcasted_iota(jnp.int32, (8, 128), 1)
    return (lane & 7) == lax.broadcasted_iota(jnp.int32, (8, 128), 0)


def packed(rows):
    return jnp.sum(jnp.where(own_lanes(), rows, 0.0), axis=0, keepdims=True)


def unpacked(row):
    rows = jnp.where(own_lanes(), jnp.broadcast_to(row, (8, 128)), 0.0)
    for step in (1, 2, 4):
        rows = rows + lane_swap(rows, step)
    return rows


def wide(value):
    return jnp.concatenate([value[0:1], value[1:2]], axis=1).reshape(1, 1, C)


def sigmoid(v):
    return 1.0 / (1.0 + jnp.exp(-v))


def kernel(
    mask, latent_hbm, cot_hbm, res_hbm, up_hbm, out,
    latent, cot, weights, fields, grads, grads_out, grads_in, total, pre, fine, rows_out, rows_in, slopes, stats, taps, taps_n, box_a, box_b,
    buf_a, buf_b, pair, joint, lines, means, cor_own, cor_a, cor_b, cor_c, cor, expanded,
    load_sem, send_a, send_b, recv_a, recv_b, send_p, recv_p, csend, crecv, hsend, hrecv,
):
    c, r, core, px, py = position()
    place = py * 4 + px
    top = jnp.where(r == 0, 0.0, 1.0).astype(F32)
    bottom = jnp.where(r == 7, 0.0, 1.0).astype(F32)
    left = jnp.where(c == 0, 0.0, 1.0).astype(F32)
    right = jnp.where(c == 31, 0.0, 1.0).astype(F32)
    side = lax.broadcasted_iota(jnp.int32, (1, 8, C), 1)
    edge = jnp.where(side < 4, right, left)

    def weight_copy(k):
        return pltpu.make_async_copy(res_hbm.at[k], weights.at[k], load_sem.at[k])

    up_copy = pltpu.make_async_copy(up_hbm, weights.at[6], load_sem.at[6])
    cot_copy = pltpu.make_async_copy(cot_hbm, cot, load_sem.at[7])
    latent_copy = pltpu.make_async_copy(latent_hbm, latent, load_sem.at[8])
    latent_copy.start()
    barrier = pltpu.get_barrier_semaphore()
    plane, column = plane_peers(), column_peers()

    def greet(slot, col, row):
        pl.semaphore_signal(barrier, inc=1, device_id={"cols": col, "rows": row}, device_id_type=MESH)

    chip_peers(greet)
    greeted = plane + column + [(0,) + p[2:] for p in neighbours()]
    for peer in greeted:
        greet(*peer)

    cot_copy.start()
    weight_copy(0).start()
    up_copy.start()
    for k in range(1, 6):
        weight_copy(k).start()

    def load_stats(k):
        return stats[k, 0:1, :].reshape(1, 1, C), stats[k, 1:2, :].reshape(1, 1, C)

    def normed(k, rows, columns=slice(0, WT)):
        mean, inv = load_stats(k)
        return (fields[k, rows, columns, :] - mean) * inv

    tile_rows, tile_columns = slice(T, T + H), slice(0, W)

    def put_rows(buf, at, first, second):
        buf[at : at + 1, :] = first[:, 0:128]
        buf[at + 1 : at + 2, :] = first[:, 128:256]
        buf[at + 2 : at + 3, :] = second[:, 0:128]
        buf[at + 3 : at + 4, :] = second[:, 128:256]

    def moments(k, x):
        mean = jnp.sum(x, axis=(0, 1)).reshape(1, C) * (1.0 / PIXELS)
        delta = x - mean.reshape(1, 1, C)
        square = jnp.sum(delta * delta, axis=(0, 1)).reshape(1, C)
        means[k, 0:1, :] = mean
        put_rows(lines, 0, mean, square)
        mean, square = lines[0:2], lines[2:4]
        count = float(PIXELS)
        for step in (1, 2, 4):
            other, squares = lane_swap(mean, step), lane_swap(square, step)
            delta = mean - other
            mean = (mean + other) * 0.5
            square = square + squares + delta * delta * (count * 0.5)
            count *= 2.0
        lines[0:2] = mean
        lines[2:4] = square
        lines[4:8] = jnp.zeros((4, 128), F32)
        return packed(lines[...])

    def put_moments(k, x):
        swap_cores(pair, k, moments(k, x), send_p, recv_p)

    def put_sums(at, d, n):
        first = jnp.sum(d, axis=(0, 1)).reshape(1, C) * (1.0 / PIXELS)
        second = jnp.sum(d * n, axis=(0, 1)).reshape(1, C) * (1.0 / PIXELS)
        put_rows(lines, at, first, second)

    def pack_sums(t):
        rows = lines[...]
        for step in (1, 2, 4):
            rows = rows + lane_swap(rows, step)
        swap_cores(pair, t, packed(rows * (1.0 / GROUP)), send_p, recv_p)

    def send_all(t, row, then):
        joint[t] = jnp.broadcast_to(row, (8, 128))

        def send(slot, col, row):
            pltpu.make_async_remote_copy(
                src_ref=joint.at[t, pl.ds(0, 1)],
                dst_ref=buf_a.at[t, pl.ds(slot, 1)],
                send_sem=send_a.at[t],
                recv_sem=recv_a.at[t],
                device_id={"cols": col, "rows": row},
                device_id_type=MESH,
            ).start()

        chip_peers(send)
        for copy in then:
            copy.start()

        @pl.when(core == 0)
        def _():
            buf_a[t, OWN : OWN + 1, :] = joint[t, 0:1]

    def wait_all(t, sem):
        for which, count in ((0, HALF - 1), (1, HALF)):

            @pl.when(core == which)
            def _():
                part = buf_a.at[t, pl.ds(0, count)]
                pltpu.make_async_copy(part, part, sem.at[t]).wait()

    def core_copy(buf, t, send, recv):
        col, row = other_core()
        return pltpu.make_async_remote_copy(
            src_ref=buf.at[t, 0],
            dst_ref=buf.at[t, 1],
            send_sem=send.at[t],
            recv_sem=recv.at[t],
            device_id={"cols": col, "rows": row},
            device_id_type=MESH,
        )

    def swap_cores(buf, t, row, send, recv):
        buf[t, 0] = jnp.broadcast_to(row, (8, 128))
        core_copy(buf, t, send, recv).start()

    def swapped(buf, t, send, recv):
        core_copy(buf, t, send, recv).wait_recv()
        return buf[t, 0, 0:1], buf[t, 1, 0:1]

    lane = lax.broadcasted_iota(jnp.int32, (1, 128), 1) & 7

    def join_moments(parts, count):
        mine, theirs = parts
        delta = mine - theirs
        square = delta * delta * (count * 0.5)
        return jnp.where(lane < 2, (mine + theirs) * 0.5, mine + theirs + pltpu.roll(square, 2, 1))

    def join_means(parts):
        return (parts[0] + parts[1]) * 0.5

    def ring_copies(k):
        return halo_copies(fields.at[k], (1, 1), (1, 3), (1, 3), hsend.at[k], hrecv.at[k])

    def wide_copies(k):
        return halo_copies(fields.at[k], (2, 3), None, None, hsend.at[k + 6], hrecv.at[k + 6])

    def grad_copies(l, last):
        far = 1 if last else 3
        copies = halo_copies(grads.at[l], None, (1, far), (1, far), hsend.at[l + 12], hrecv.at[l + 12])
        c, r, _, _, _ = position()
        for i, (first, dst_first) in enumerate(((0, 0), (H - far, 3 - far))):
            copies.append(
                pltpu.make_async_remote_copy(
                    src_ref=grads_out.at[l, pl.ds(first, far)],
                    dst_ref=grads_in.at[l, 1 - i, pl.ds(dst_first, far)],
                    send_sem=hsend.at[l + 12, 6 + i],
                    recv_sem=hrecv.at[l + 12, 6 + i],
                    device_id={"cols": c, "rows": (r + 2 * i + 7) % 8},
                    device_id_type=MESH,
                )
            )
        return copies

    def total_copies():
        return halo_copies(total, (1, 2), (1, 2), (1, 2), hsend.at[15], hrecv.at[15])

    def fine_copies():
        copies = []
        for i, (dr, dc, col, row) in enumerate(neighbours()):
            if dc == 0:
                src, dst = rows_out.at[max(dr, 0)], rows_in.at[max(-dr, 0)]
            else:
                src_r = pl.ds(1, FH) if dr == 0 else (pl.ds(1, 1) if dr < 0 else pl.ds(FH, 1))
                dst_r = pl.ds(1, FH) if dr == 0 else (pl.ds(FH + 1, 1) if dr < 0 else pl.ds(0, 1))
                src = fine.at[:, src_r, pl.ds(0 if dc < 0 else FW - 1, 1), :]
                dst = fine.at[:, dst_r, pl.ds(FW if dc < 0 else FWT - 1, 1), :]
            copies.append(
                pltpu.make_async_remote_copy(
                    src_ref=src,
                    dst_ref=dst,
                    send_sem=hsend.at[16, i],
                    recv_sem=hrecv.at[16, i],
                    device_id={"cols": col, "rows": row},
                    device_id_type=MESH,
                )
            )
        return copies

    def put_taps(make, first, last, columns, dst=taps):
        parts = ((first, T, top), (T, T + H, None), (T + H, last, bottom))
        for begin, end, scale in parts:
            u = make(begin, end - begin)
            if scale is not None:
                u = u * scale
            u = jnp.concatenate([u[:, 0:W], u[:, W:WT] * edge], axis=1)
            at = slice(begin - first, end - first)
            for b, v in enumerate((pltpu.roll(u, 1, 1), u, pltpu.roll(u, WT - 1, 1))):
                if columns > WT:
                    v = jnp.concatenate([v, jnp.zeros((end - begin, columns - WT, C), F32)], axis=1)
                dst[at, 0:columns, b * C : (b + 1) * C] = v[:, 0:columns].astype(BF16)

    def conv(k):
        rows = [taps[a : a + H, 0:W].reshape(PIXELS, 3 * C) for a in range(3)]
        y = jnp.dot(jnp.concatenate(rows, axis=-1), weights[k].reshape(9 * C, C), preferred_element_type=F32)
        return y.reshape(H, W, C)

    def conv_back(piece, k, rows, columns):
        y = None
        for a in range(3):
            for b in range(3):
                d = lax.dot_general(
                    piece(a, b), weights[k, 8 - 3 * a - b], (((1,), (1,)), ((), ())), preferred_element_type=F32
                )
                y = d if y is None else y + d
        return y.reshape(rows, columns, C)

    def tap_conv_back(k, rows, columns):
        parts = []
        chunks = 1 if rows * columns <= PIXELS else 2
        height = rows // chunks
        for begin in range(0, rows, height):

            def piece(a, b):
                at = slice(begin + a, begin + a + height)
                return taps[at, 0:columns, b * C : (b + 1) * C].reshape(height * columns, C)

            parts.append(conv_back(piece, k, height, columns))
        return parts[0] if chunks == 1 else jnp.concatenate(parts, axis=0)

    latent_copy.wait()
    fields[0, tile_rows, tile_columns, :] = latent[...].astype(F32)
    first_row = moments(0, latent[...].astype(F32))

    def start_a(k):
        row = join_moments(swapped(pair, k, send_p, recv_p), float(PIXELS * GROUP))
        send_all(k, row, ring_copies(k) + wide_copies(k))

    pl.semaphore_wait(barrier, HALF - 1 + core + len(greeted))
    swap_cores(pair, 0, first_row, send_p, recv_p)
    start_a(0)
    cot_copy.wait()

    def mask_row(i, carry):
        row = jnp.broadcast_to(mask[pl.ds(i, 1), :].astype(F32), (FW, FW)).T
        fine[0, i + 1, 0:FW, :] = cot[i, :, 0:128].astype(F32) * row
        fine[1, i + 1, 0:FW, :] = cot[i, :, 128:256].astype(F32) * row
        return carry

    lax.fori_loop(0, FH, mask_row, 0)
    for i, at in enumerate((1, FH)):
        rows_out[i] = jnp.concatenate([fine[0, at, 0:FW, :], fine[1, at, 0:FW, :]], axis=1).astype(BF16)
    for copy in fine_copies():
        copy.start()

    def slope(k, first, last):
        n = normed(k, slice(first, last))
        s = sigmoid(n)
        slopes[k, first - 1 : last - 1] = s * (1.0 + n * (1.0 - s))

    def boxes():
        for copy in fine_copies():
            copy.wait_recv()
        for i, (at, scale) in enumerate(((0, top), (FH + 1, bottom))):
            edge_row = rows_in[i].astype(F32) * scale
            fine[0, at, 0:FW, :] = edge_row[:, 0:128]
            fine[1, at, 0:FW, :] = edge_row[:, 128:256]
            fine[:, at, FW:FWT, :] = fine[:, at, FW:FWT, :] * scale
        fine[:, :, FW : FW + 8, :] = fine[:, :, FW : FW + 8, :] * right
        fine[:, :, FWT - 8 : FWT, :] = fine[:, :, FWT - 8 : FWT, :] * left

        def pair(i, dst, at):
            even, odd = (
                jnp.concatenate(
                    [fine[h, i, pl.ds(q, WT, 2), :] + fine[h, i + 1, pl.ds(q, WT, 2), :] for h in (0, 1)], axis=1
                )
                for q in (0, 1)
            )
            dst[at, :, 0:C] = (pltpu.roll(odd, 1, 0) + even)[0:W].astype(BF16)
            dst[at, :, C : 2 * C] = (even + odd)[0:W].astype(BF16)
            dst[at, :, 2 * C : 3 * C] = (odd + pltpu.roll(even, WT - 1, 0))[0:W].astype(BF16)

        def body(i, carry):
            pair(2 * i, box_a, i)
            pair(2 * i + 1, box_b, i)
            return carry

        lax.fori_loop(0, H, body, 0)
        pair(2 * H, box_a, H)

    def upper():
        up_copy.wait()

        def piece(a, b):
            at = slice(b * C, (b + 1) * C)
            if a == 1:
                return box_b[:, :, at].reshape(PIXELS, C)
            return box_a[a // 2 : a // 2 + H, :, at].reshape(PIXELS, C)

        total[tile_rows, tile_columns, :] = conv_back(piece, 6, H, W)
        for copy in total_copies():
            copy.start()

    def lift(k):
        put_taps(lambda first, rows: total[first : first + rows], T - 2, T + H + 2, WB)
        pre[...] = tap_conv_back(k, H + 2, WB)[:, 0:WT]

    def correlate(l):
        k = 2 * l
        mean = means[k + 1, 0:1, :]

        def plain_slope(first, rows):
            return slopes[k, first - 1 : first - 1 + rows]

        def normed_slope(first, rows):
            return slopes[k, first - 1 : first - 1 + rows] * normed(k, slice(first, first + rows))

        put_taps(plain_slope, T - 1, T + H + 1, W)
        put_taps(normed_slope, T - 1, T + H + 1, W, taps_n)
        x = (fields[k + 1, tile_rows, tile_columns, :] - mean.reshape(1, 1, C)).reshape(PIXELS, C).astype(BF16)
        raw = plain = None
        for b in range(3):
            at = slice(b * C, (b + 1) * C)
            sums = [jnp.sum(src[0 : H + 2, 0:W, at].astype(F32), axis=1) for src in (taps, taps_n)]
            for a in range(3):
                weight = weights[k, 3 * a + b].astype(F32).T
                weight = jnp.concatenate([weight, weight], axis=1)
                q = jnp.concatenate(
                    [src[a : a + H, 0:W, at].reshape(PIXELS, C) for src in (taps, taps_n)], axis=1
                )
                first = lax.dot_general(x, q, (((0,), (0,)), ((), ())), preferred_element_type=F32) * weight
                total_q = jnp.concatenate([jnp.sum(v[a : a + H], axis=0, keepdims=True) for v in sums], axis=1)
                second = total_q * weight
                raw = first if raw is None else raw + first
                plain = second if plain is None else plain + second
        shift = jnp.broadcast_to(mean, (8, C)).T[:, 0:1]
        raw = raw + plain * shift
        row = lax.broadcasted_iota(jnp.int32, (2 * C, 128), 0) // GROUP
        lane = lax.broadcasted_iota(jnp.int32, (2 * C, 128), 1)
        whole = None
        for j, block in enumerate((raw, plain)):
            block = jnp.sum(block.reshape(C // GROUP, GROUP, 2 * C), axis=1) * (1.0 / (PIXELS * SIDE * SIDE * GROUP))
            pick = jnp.where(lane == 64 * j + row, 1.0, 0.0).astype(F32)
            part = jnp.dot(block, pick, precision=lax.Precision.HIGHEST, preferred_element_type=F32)
            whole = part if whole is None else whole + part
        cor[...] = whole
        for i in range(SIDE):
            cor_own[l, i] = cor[2 * i : 2 * i + 2, :]
        for slot, col, row in plane:
            x, y = (col // 2) % 4, col // 8
            pltpu.make_async_remote_copy(
                src_ref=cor_own.at[l, y * 4 + x],
                dst_ref=cor_a.at[l, slot],
                send_sem=csend.at[l],
                recv_sem=crecv.at[l],
                device_id={"cols": col, "rows": row},
                device_id_type=MESH,
            ).start()

    def correlate_b(l):
        phase_wait(cor_a.at[l], crecv.at[l])
        cor_b[l, 0] = cor_own[l, place] + jnp.sum(cor_a[l, 1:SIDE], axis=0)
        phase_start(cor_b.at[l], column, csend.at[l + 3], crecv.at[l + 3])

    def correlate_c(l):
        phase_wait(cor_b.at[l], crecv.at[l + 3])
        cor_c[l, place] = jnp.sum(cor_b[l], axis=0)
        for slot, col, row in plane:
            pltpu.make_async_remote_copy(
                src_ref=cor_c.at[l, place],
                dst_ref=cor_c.at[l, place],
                send_sem=csend.at[l + 6],
                recv_sem=crecv.at[l + 6],
                device_id={"cols": col, "rows": row},
                device_id_type=MESH,
            ).start()

    def expand(l):
        phase_wait(cor_c.at[l], crecv.at[l + 6])
        for i in range(SIDE):
            cor[2 * i : 2 * i + 2, :] = cor_c[l, i]
        whole = cor[...]
        high = whole.astype(BF16)
        low = (whole - high.astype(F32)).astype(BF16)
        group = lax.broadcasted_iota(jnp.int32, (32, C), 1) // GROUP
        spread = jnp.where(lax.broadcasted_iota(jnp.int32, (32, C), 0) == group, 1.0, 0.0).astype(BF16)
        lane = lax.broadcasted_iota(jnp.int32, (128, 2 * C), 0)
        channel = lax.broadcasted_iota(jnp.int32, (128, 2 * C), 1) // GROUP
        for j in range(2):
            pick = jnp.where(lane == 64 * j + channel, 1.0, 0.0).astype(BF16)
            for part, value in enumerate((high, low)):
                block = jnp.dot(value, pick, preferred_element_type=F32).astype(BF16)
                block = lax.dot_general(spread, block, (((0,), (0,)), ((), ())), preferred_element_type=F32)
                expanded[part, j * C : (j + 1) * C, :] = block.astype(BF16)

    def chips_moments(k):
        parts = buf_a[k]
        total_row = jnp.sum(parts, axis=0, keepdims=True)
        mean = total_row * (1.0 / HALF)
        delta = parts - mean
        square = jnp.sum(delta * delta, axis=0, keepdims=True) * float(PIXELS * GROUP * 2)
        return jnp.where(lane < 2, mean, jnp.where(lane < 4, total_row + pltpu.roll(square, 2, 1), 0.0))

    def finish_moments(k):
        both = join_moments(swapped(buf_b, k, send_b, recv_b), float(PIXELS * GROUP * 2 * HALF))
        rows = unpacked(both)
        mean = rows[0:2]
        inv = lax.rsqrt(rows[2:4] * (1.0 / (PIXELS * GROUP * HALF * 4)) + EPS)
        mean, inv = wide(mean), wide(inv)
        stats[k, 0:1, :] = mean.reshape(1, C)
        stats[k, 1:2, :] = inv.reshape(1, C)
        return mean, inv

    def forward(k, carry):
        @pl.when(k > 0)
        def _():
            start_a(k)
            for copy in wide_copies(k - 1):
                copy.wait_recv()
            slope(k - 1, 1, RT - 1)

        @pl.when((k == 3) | (k == 5))
        def _():
            correlate_c(k // 2 - 1)

        @pl.when(k % 2 == 1)
        def _():
            correlate(k // 2)

        @pl.when((k == 2) | (k == 4))
        def _():
            correlate_b(k // 2 - 1)

        @pl.when(k == 2)
        def _():
            boxes()
            upper()

        @pl.when(k == 4)
        def _():
            weight_copy(5).wait()
            for copy in total_copies():
                copy.wait()
            lift(5)

        @pl.when(k < 5)
        def _():
            weight_copy(k).wait()

        wait_all(k, recv_a)
        swap_cores(buf_b, k, chips_moments(k), send_b, recv_b)
        for copy in ring_copies(k):
            copy.wait_recv()
        mean, inv = finish_moments(k)

        @pl.when(k < 5)
        def _():
            def active(first, rows):
                n = (fields[k, first : first + rows] - mean) * inv
                return n * sigmoid(n)

            put_taps(active, T - 1, T + H + 1, W)
            y = conv(k)
            keep = jnp.where(k % 2 == 1, 1.0, 0.0).astype(F32)
            y = y + keep * fields[jnp.maximum(k - 1, 0), tile_rows, tile_columns, :]
            fields[k + 1, tile_rows, tile_columns, :] = y
            put_moments(k + 1, y)

        return carry

    lax.fori_loop(0, 6, forward, 0)
    slope(5, T - 1, T + H + 1)

    def drain_sums(t):
        wait_all(t, send_a)
        core_copy(buf_b, t, send_b, recv_b).wait_send()
        core_copy(pair, t, send_p, recv_p).wait_send()

    def drain(k, carry):
        drain_sums(k)
        for copy in ring_copies(k) + wide_copies(k):
            copy.wait_send()
        return carry

    def drain_layer(l):
        drain_sums(8 - l)
        phase_wait(cor_a.at[l], csend.at[l])
        phase_wait(cor_b.at[l], csend.at[l + 3])
        phase_wait(cor_c.at[l], csend.at[l + 6])
        for copy in grad_copies(l, l == 0):
            copy.wait_send()

    def layer(l, last):
        k = 2 * l
        mean1, inv1 = load_stats(k)
        mean2, inv2 = load_stats(k + 1)
        t = 8 - l
        grads[l, tile_rows, tile_columns, :] = (
            pre[1 : H + 1, 0:W] * slopes[k + 1, T - 1 : T - 1 + H, 0:W]
        )
        grads_out[l] = grads[l, tile_rows, tile_columns, :].astype(BF16)
        put_sums(0, grads[l, tile_rows, tile_columns, :], normed(k + 1, tile_rows, tile_columns))

        def unprojected(first, rows):
            at = first - T + 1
            return inv2 * (pre[at : at + rows] * slopes[k + 1, first - 1 : first - 1 + rows])

        put_taps(unprojected, T - 1, T + H + 1, W)
        d = tap_conv_back(k, H, W) * slopes[k, T - 1 : T - 1 + H, 0:W]
        put_sums(4, d, normed(k, tile_rows, tile_columns))
        pack_sums(t)
        send_all(t, join_means(swapped(pair, t, send_p, recv_p)), grad_copies(l, last))

        if last:
            expand(l)
            drain_layer(2)
            drain_layer(1)
            for copy in fine_copies():
                copy.wait_send()
        else:

            @pl.when(l == 2)
            def _():
                correlate_b(l)
                for copy in wide_copies(5):
                    copy.wait_recv()

            @pl.when(l == 1)
            def _():
                expand(l)
                lax.fori_loop(0, 6, drain, 0)

        wait_all(t, recv_a)
        half = jnp.sum(buf_a[t], axis=0, keepdims=True) * (1.0 / HALF)
        swap_cores(buf_b, t, half, send_b, recv_b)
        if not last:

            @pl.when(l == 2)
            def _():
                correlate_c(l)

        for copy in grad_copies(l, last):
            copy.wait_recv()
        far = 1 if last else 3
        grads[l, T - far : T, tile_columns, :] = grads_in[l, 0, 3 - far : 3].astype(F32)
        grads[l, T + H : T + H + far, tile_columns, :] = grads_in[l, 1, 0:far].astype(F32)
        sums = unpacked(join_means(swapped(buf_b, t, send_b, recv_b)))
        first2, second2, first1_raw, second1_raw = (wide(sums[i : i + 2]) for i in (0, 2, 4, 6))
        def second_sums():
            scaled = inv2 * second2
            source = jnp.concatenate([inv2 * scaled, inv2 * (first2 - mean2 * scaled)], axis=-1).reshape(1, 2 * C)
            source = jnp.broadcast_to(source * (1.0 / GROUP), (16, 2 * C))
            high = source.astype(BF16)
            low = (source - high.astype(F32)).astype(BF16)
            moved = (
                jnp.dot(high, expanded[0], preferred_element_type=F32)
                + jnp.dot(low, expanded[0], preferred_element_type=F32)
                + jnp.dot(high, expanded[1], preferred_element_type=F32)
            )
            first1_left = first1_raw - moved[0:1, 0:C].reshape(1, 1, C)
            second1_left = second1_raw - moved[0:1, C : 2 * C].reshape(1, 1, C)
            return first1_left, second1_left

        def back(first, rows):
            at = slice(first, first + rows)
            return inv2 * (grads[l, at] - first2 - normed(k + 1, at) * second2)

        if last:
            put_taps(back, T - 1, T + H + 1, W)
            d = tap_conv_back(k, H, W) * slopes[k, T - 1 : T - 1 + H, 0:W]
            n = normed(k, tile_rows, tile_columns)
            first1, second1 = second_sums()
            out[...] = total[tile_rows, tile_columns, :] + inv1 * (d - first1 - n * second1)
        else:
            put_taps(back, 0, RT, WB)
            d = tap_conv_back(k, H + 4, WB)[:, 0:WT] * slopes[k]
            rows = slice(T - 2, T + H + 2)

            @pl.when(l == 2)
            def _():
                expand(l)

            first1, second1 = second_sums()
            total[rows] += inv1 * (d - first1 - normed(k, rows) * second1)
            lift(k - 1)

    def backward(j, carry):
        layer(2 - j, False)
        return carry

    lax.fori_loop(0, 2, backward, 0)
    layer(0, True)

    drain_layer(0)


def per_device(latent, cotangent, pixel_mask, res_kernels, up_kernel):
    vmem = pl.BlockSpec(memory_space=pltpu.VMEM)
    hbm = pl.BlockSpec(memory_space=pl.ANY)
    dma = pltpu.SemaphoreType.DMA
    return pl.pallas_call(
        kernel,
        out_shape=jax.ShapeDtypeStruct((H, W, C), F32),
        in_specs=[vmem, hbm, hbm, hbm, hbm],
        out_specs=vmem,
        scratch_shapes=[
            pltpu.VMEM((H, W, C), BF16),
            pltpu.VMEM((FH, FW, C), BF16),
            pltpu.VMEM((7, 9, C, C), BF16),
            pltpu.VMEM((6, RT, WT, C), F32),
            pltpu.VMEM((3, RT, WT, C), F32),
            pltpu.VMEM((3, H, W, C), BF16),
            pltpu.VMEM((3, 2, 3, W, C), BF16),
            pltpu.VMEM((RT, WT, C), F32),
            pltpu.VMEM((H + 2, WT, C), F32),
            pltpu.VMEM((2, FH + 2, FWT, 128), F32),
            pltpu.VMEM((2, FW, C), BF16),
            pltpu.VMEM((2, FW, C), BF16),
            pltpu.VMEM((6, RT - 2, WT, C), F32),
            pltpu.VMEM((6, 8, C), F32),
            pltpu.VMEM((RT, WB, 3 * C), BF16),
            pltpu.VMEM((H + 2, W, 3 * C), BF16),
            pltpu.VMEM((H + 1, W, 3 * C), BF16),
            pltpu.VMEM((H, W, 3 * C), BF16),
            pltpu.VMEM((9, HALF, 128), F32),
            pltpu.VMEM((9, 2, 8, 128), F32),
            pltpu.VMEM((9, 2, 8, 128), F32),
            pltpu.VMEM((9, 8, 128), F32),
            pltpu.VMEM((8, 128), F32),
            pltpu.VMEM((6, 8, C), F32),
            pltpu.VMEM((3, SIDE, 2, 128), F32),
            pltpu.VMEM((3, SIDE, 2, 128), F32),
            pltpu.VMEM((3, SIDE, 2, 128), F32),
            pltpu.VMEM((3, SIDE, 2, 128), F32),
            pltpu.VMEM((32, 128), F32),
            pltpu.VMEM((2, 2 * C, 2 * C), BF16),
            dma((9,)),
            dma((9,)),
            dma((9,)),
            dma((9,)),
            dma((9,)),
            dma((9,)),
            dma((9,)),
            dma((9,)),
            dma((9,)),
            dma((17, 8)),
            dma((17, 8)),
        ],
        compiler_params=pltpu.CompilerParams(
            collective_id=0, has_side_effects=True, vmem_limit_bytes=56 * 2**20
        ),
    )(
        pixel_mask,
        latent,
        cotangent,
        res_kernels.reshape(6, 9, C, C),
        up_kernel.reshape(9, C, C),
    )


def solution(mesh):
    in_specs = (P("rows", "cols", None), P("rows", "cols", None), P("rows", "cols"), P(), P())
    out_specs = P("rows", "cols", None)
    return jax.shard_map(
        per_device, mesh=mesh, in_specs=in_specs, out_specs=out_specs, check_vma=False
    )
```

```python
import functools

import jax
import jax.numpy as jnp
from jax import lax
from jax.experimental import pallas as pl
from jax.experimental.pallas import tpu as pltpu
from jax.sharding import PartitionSpec as P

LAYERS = 3
EPS = 1e-06
MESH = pl.DeviceIdType.MESH
F32 = jnp.float32
BF16 = jnp.bfloat16

H, W, C = 8, 64, 256
T = 3
RT = H + 2 * T
WT = W + 8
WB = W + 16
FH, FW = 2 * H, 2 * W
FWT = FW + 16
SIDE = 16
CHIPS = 128
PIXELS = H * W
GROUP = 8


def position():
    c = lax.axis_index("cols")
    r = lax.axis_index("rows")
    core = c % 2
    chip = c // 2
    return c, r, core, chip % 4, chip // 4


def plane_peers():
    c, r, core, x, y = position()
    out = []
    for dy in range(4):
        for dx in range(4):
            if dx or dy:
                far = min(dx, 4 - dx) + min(dy, 4 - dy)
                out.append((far, dy * 4 + dx, (((y + dy) % 4) * 4 + (x + dx) % 4) * 2 + core, r))
    return [p[1:] for p in sorted(out, key=lambda p: -p[0])]


def column_peers():
    c, r, core, x, y = position()
    out = []
    for dz in range(8):
        for dc in range(2):
            if dz or dc:
                far = min(dz, 8 - dz)
                out.append((far, dz * 2 + dc, c - core + (core + dc) % 2, (r + dz) % 8))
    return [p[1:] for p in sorted(out, key=lambda p: -p[0])]


def other_core():
    c, r, core, x, y = position()
    return c - core + (core + 1) % 2, r


def chip_peers(visit, middle=None):
    c, r, core, x, y = position()
    plane = [(0, c, r)] + plane_peers()[::-1]

    def level(i, carry):
        dz = jnp.where(i % 2 == 0, 4 + i // 2, 4 - (i + 1) // 2)
        row = (r + dz) % 8
        for slot, col, _ in plane[::-1]:
            visit(dz * SIDE + slot, col, row)
        return carry

    lax.fori_loop(0, 4, level, 0)
    if middle is not None:
        middle()
    lax.fori_loop(4, 7, level, 0)


def neighbours():
    c, r, core, x, y = position()
    out = []
    for dr in (-1, 0, 1):
        for dc in (-1, 0, 1):
            if dr or dc:
                out.append((dr, dc, (c + dc + 32) % 32, (r + dr + 8) % 8))
    return out


def halo_copies(field, rows, columns, corners, send, recv, top=T, height=H, width=W, total=WT):
    def spans(step, first, size, end, near, far):
        n = far - near + 1
        if step < 0:
            return pl.ds(first + near - 1, n), pl.ds(first + size + near - 1, n)
        if step > 0:
            return pl.ds(first + size - far, n), pl.ds(end - far, n)
        return pl.ds(first, size), pl.ds(first, size)

    copies = []
    for dr, dc, col, row in neighbours():
        band = corners if dr and dc else (rows if dr else columns)
        if band is None:
            continue
        src_r, dst_r = spans(dr, top, height, top, *band)
        src_c, dst_c = spans(dc, 0, width, total, *band)
        src, dst = (src_r, src_c, slice(None)), (dst_r, dst_c, slice(None))
        if len(field.shape) == 4:
            src, dst = (slice(None),) + src, (slice(None),) + dst
        copies.append(
            pltpu.make_async_remote_copy(
                src_ref=field.at[src],
                dst_ref=field.at[dst],
                send_sem=send.at[len(copies)],
                recv_sem=recv.at[len(copies)],
                device_id={"cols": col, "rows": row},
                device_id_type=MESH,
            )
        )
    return copies


def phase_start(buf, peers, send, recv):
    for slot, col, row in peers:
        pltpu.make_async_remote_copy(
            src_ref=buf.at[0],
            dst_ref=buf.at[slot],
            send_sem=send,
            recv_sem=recv,
            device_id={"cols": col, "rows": row},
            device_id_type=MESH,
        ).start()


def phase_wait(buf, sem):
    pltpu.make_async_copy(buf.at[pl.ds(1, SIDE - 1)], buf.at[pl.ds(1, SIDE - 1)], sem).wait()


def lane_swap(value, step):
    lane = lax.broadcasted_iota(jnp.int32, value.shape, 1)
    return jnp.where((lane & step) != 0, pltpu.roll(value, step, 1), pltpu.roll(value, 128 - step, 1))


def own_lanes():
    lane = lax.broadcasted_iota(jnp.int32, (8, 128), 1)
    return (lane & 7) == lax.broadcasted_iota(jnp.int32, (8, 128), 0)


def packed(rows):
    return jnp.sum(jnp.where(own_lanes(), rows, 0.0), axis=0, keepdims=True)


def unpacked(row):
    rows = jnp.where(own_lanes(), jnp.broadcast_to(row, (8, 128)), 0.0)
    for step in (1, 2, 4):
        rows = rows + lane_swap(rows, step)
    return rows


def wide(value):
    return jnp.concatenate([value[0:1], value[1:2]], axis=1).reshape(1, 1, C)


def sigmoid(v):
    return 1.0 / (1.0 + jnp.exp(-v))


def kernel(
    mask, latent_hbm, cot_hbm, res_hbm, up_hbm, out,
    latent, cot, weights, fields, grads, grads_out, grads_in, total, pre, fine, rows_out, rows_in, slopes, stats, taps, taps_n, box_a, box_b,
    buf_a, buf_b, lines, means, cor_own, cor_a, cor_b, cor_c, cor, expanded,
    load_sem, send_a, send_b, recv_a, recv_b, csend, crecv, hsend, hrecv,
):
    c, r, _, px, py = position()
    place = py * 4 + px
    top = jnp.where(r == 0, 0.0, 1.0).astype(F32)
    bottom = jnp.where(r == 7, 0.0, 1.0).astype(F32)
    left = jnp.where(c == 0, 0.0, 1.0).astype(F32)
    right = jnp.where(c == 31, 0.0, 1.0).astype(F32)
    side = lax.broadcasted_iota(jnp.int32, (1, 8, C), 1)
    edge = jnp.where(side < 4, right, left)

    def weight_copy(k):
        return pltpu.make_async_copy(res_hbm.at[k], weights.at[k], load_sem.at[k])

    up_copy = pltpu.make_async_copy(up_hbm, weights.at[6], load_sem.at[6])
    cot_copy = pltpu.make_async_copy(cot_hbm, cot, load_sem.at[7])
    latent_copy = pltpu.make_async_copy(latent_hbm, latent, load_sem.at[8])
    latent_copy.start()
    barrier = pltpu.get_barrier_semaphore()
    plane, column = plane_peers(), column_peers()

    def greet(slot, col, row):
        pl.semaphore_signal(barrier, inc=1, device_id={"cols": col, "rows": row}, device_id_type=MESH)

    chip_peers(greet)
    greeted = plane + [p for p in column if p[0] % 2 == 1] + [(0,) + p[2:] for p in neighbours()]
    for peer in greeted:
        greet(*peer)

    cot_copy.start()
    weight_copy(0).start()
    up_copy.start()
    for k in range(1, 6):
        weight_copy(k).start()

    def load_stats(k):
        return stats[k, 0:1, :].reshape(1, 1, C), stats[k, 1:2, :].reshape(1, 1, C)

    def normed(k, rows, columns=slice(0, WT)):
        mean, inv = load_stats(k)
        return (fields[k, rows, columns, :] - mean) * inv

    tile_rows, tile_columns = slice(T, T + H), slice(0, W)

    def put_rows(buf, at, first, second):
        buf[at : at + 1, :] = first[:, 0:128]
        buf[at + 1 : at + 2, :] = first[:, 128:256]
        buf[at + 2 : at + 3, :] = second[:, 0:128]
        buf[at + 3 : at + 4, :] = second[:, 128:256]

    def put_moments(k, x):
        mean = jnp.sum(x, axis=(0, 1)).reshape(1, C) * (1.0 / PIXELS)
        delta = x - mean.reshape(1, 1, C)
        square = jnp.sum(delta * delta, axis=(0, 1)).reshape(1, C)
        means[k, 0:1, :] = mean
        put_rows(lines, 0, mean, square)
        mean, square = lines[0:2], lines[2:4]
        count = float(PIXELS)
        for step in (1, 2, 4):
            other, squares = lane_swap(mean, step), lane_swap(square, step)
            delta = mean - other
            mean = (mean + other) * 0.5
            square = square + squares + delta * delta * (count * 0.5)
            count *= 2.0
        lines[0:2] = mean
        lines[2:4] = square
        lines[4:8] = jnp.zeros((4, 128), F32)
        buf_a[k, 0:1, :] = packed(lines[...])

    def put_sums(at, d, n):
        first = jnp.sum(d, axis=(0, 1)).reshape(1, C) * (1.0 / PIXELS)
        second = jnp.sum(d * n, axis=(0, 1)).reshape(1, C) * (1.0 / PIXELS)
        put_rows(lines, at, first, second)

    def pack_sums(t):
        rows = lines[...]
        for step in (1, 2, 4):
            rows = rows + lane_swap(rows, step)
        buf_a[t, 0:1, :] = packed(rows * (1.0 / GROUP))

    def send_all(t, first, then, middle=None):
        def send(slot, col, row):
            pltpu.make_async_remote_copy(
                src_ref=buf_a.at[t, pl.ds(0, 1)],
                dst_ref=buf_a.at[t, pl.ds(slot, 1)],
                send_sem=send_a.at[t],
                recv_sem=recv_a.at[t],
                device_id={"cols": col, "rows": row},
                device_id_type=MESH,
            ).start()

        chip_peers(send, middle)
        for copy in first:
            copy.start()
        for peer in plane:
            send(*peer)
        for copy in then:
            copy.start()

    def wait_all(t, sem):
        part = buf_a.at[t, pl.ds(1, CHIPS - 1)]
        pltpu.make_async_copy(part, part, sem.at[t]).wait()

    def core_copy(t):
        col, row = other_core()
        return pltpu.make_async_remote_copy(
            src_ref=buf_b.at[t, 0],
            dst_ref=buf_b.at[t, 1],
            send_sem=send_b.at[t],
            recv_sem=recv_b.at[t],
            device_id={"cols": col, "rows": row},
            device_id_type=MESH,
        )

    def swap_cores(t, row):
        buf_b[t, 0] = jnp.broadcast_to(row, (8, 128))
        core_copy(t).start()

    def ring_copies(k):
        return halo_copies(fields.at[k], (1, 1), (1, 3), (1, 3), hsend.at[k], hrecv.at[k])

    def wide_copies(k):
        return halo_copies(fields.at[k], (2, 3), None, None, hsend.at[k + 6], hrecv.at[k + 6])

    def grad_copies(l, last):
        far = 1 if last else 3
        copies = halo_copies(grads.at[l], None, (1, far), (1, far), hsend.at[l + 12], hrecv.at[l + 12])
        c, r, _, _, _ = position()
        for i, (first, dst_first) in enumerate(((0, 0), (H - far, 3 - far))):
            copies.append(
                pltpu.make_async_remote_copy(
                    src_ref=grads_out.at[l, pl.ds(first, far)],
                    dst_ref=grads_in.at[l, 1 - i, pl.ds(dst_first, far)],
                    send_sem=hsend.at[l + 12, 6 + i],
                    recv_sem=hrecv.at[l + 12, 6 + i],
                    device_id={"cols": c, "rows": (r + 2 * i + 7) % 8},
                    device_id_type=MESH,
                )
            )
        return copies

    def total_copies():
        return halo_copies(total, (1, 2), (1, 2), (1, 2), hsend.at[15], hrecv.at[15])

    def fine_copies():
        copies = []
        for i, (dr, dc, col, row) in enumerate(neighbours()):
            if dc == 0:
                src, dst = rows_out.at[max(dr, 0)], rows_in.at[max(-dr, 0)]
            else:
                src_r = pl.ds(1, FH) if dr == 0 else (pl.ds(1, 1) if dr < 0 else pl.ds(FH, 1))
                dst_r = pl.ds(1, FH) if dr == 0 else (pl.ds(FH + 1, 1) if dr < 0 else pl.ds(0, 1))
                src = fine.at[:, src_r, pl.ds(0 if dc < 0 else FW - 1, 1), :]
                dst = fine.at[:, dst_r, pl.ds(FW if dc < 0 else FWT - 1, 1), :]
            copies.append(
                pltpu.make_async_remote_copy(
                    src_ref=src,
                    dst_ref=dst,
                    send_sem=hsend.at[16, i],
                    recv_sem=hrecv.at[16, i],
                    device_id={"cols": col, "rows": row},
                    device_id_type=MESH,
                )
            )
        return copies

    def put_taps(make, first, last, columns, dst=taps):
        parts = ((first, T, top), (T, T + H, None), (T + H, last, bottom))
        for begin, end, scale in parts:
            u = make(begin, end - begin)
            if scale is not None:
                u = u * scale
            u = jnp.concatenate([u[:, 0:W], u[:, W:WT] * edge], axis=1)
            at = slice(begin - first, end - first)
            for b, v in enumerate((pltpu.roll(u, 1, 1), u, pltpu.roll(u, WT - 1, 1))):
                if columns > WT:
                    v = jnp.concatenate([v, jnp.zeros((end - begin, columns - WT, C), F32)], axis=1)
                dst[at, 0:columns, b * C : (b + 1) * C] = v[:, 0:columns].astype(BF16)

    def conv(k):
        rows = [taps[a : a + H, 0:W].reshape(PIXELS, 3 * C) for a in range(3)]
        y = jnp.dot(jnp.concatenate(rows, axis=-1), weights[k].reshape(9 * C, C), preferred_element_type=F32)
        return y.reshape(H, W, C)

    def conv_back(piece, k, rows, columns):
        y = None
        for a in range(3):
            for b in range(3):
                d = lax.dot_general(
                    piece(a, b), weights[k, 8 - 3 * a - b], (((1,), (1,)), ((), ())), preferred_element_type=F32
                )
                y = d if y is None else y + d
        return y.reshape(rows, columns, C)

    def tap_conv_back(k, rows, columns):
        parts = []
        chunks = 1 if rows * columns <= PIXELS else 2
        height = rows // chunks
        for begin in range(0, rows, height):

            def piece(a, b):
                at = slice(begin + a, begin + a + height)
                return taps[at, 0:columns, b * C : (b + 1) * C].reshape(height * columns, C)

            parts.append(conv_back(piece, k, height, columns))
        return parts[0] if chunks == 1 else jnp.concatenate(parts, axis=0)

    latent_copy.wait()
    fields[0, tile_rows, tile_columns, :] = latent[...].astype(F32)
    put_moments(0, latent[...].astype(F32))

    def start_a(k):
        send_all(k, ring_copies(k), wide_copies(k))

    pl.semaphore_wait(barrier, CHIPS - SIDE + len(greeted))
    send_all(0, ring_copies(0), wide_copies(0))
    cot_copy.wait()

    def mask_row(i, carry):
        row = jnp.broadcast_to(mask[pl.ds(i, 1), :].astype(F32), (FW, FW)).T
        fine[0, i + 1, 0:FW, :] = cot[i, :, 0:128].astype(F32) * row
        fine[1, i + 1, 0:FW, :] = cot[i, :, 128:256].astype(F32) * row
        return carry

    lax.fori_loop(0, FH, mask_row, 0)
    for i, at in enumerate((1, FH)):
        rows_out[i] = jnp.concatenate([fine[0, at, 0:FW, :], fine[1, at, 0:FW, :]], axis=1).astype(BF16)
    for copy in fine_copies():
        copy.start()

    def slope(k, first, last):
        n = normed(k, slice(first, last))
        s = sigmoid(n)
        slopes[k, first - 1 : last - 1] = s * (1.0 + n * (1.0 - s))

    def boxes():
        for copy in fine_copies():
            copy.wait_recv()
        for i, (at, scale) in enumerate(((0, top), (FH + 1, bottom))):
            edge_row = rows_in[i].astype(F32) * scale
            fine[0, at, 0:FW, :] = edge_row[:, 0:128]
            fine[1, at, 0:FW, :] = edge_row[:, 128:256]
            fine[:, at, FW:FWT, :] = fine[:, at, FW:FWT, :] * scale
        fine[:, :, FW : FW + 8, :] = fine[:, :, FW : FW + 8, :] * right
        fine[:, :, FWT - 8 : FWT, :] = fine[:, :, FWT - 8 : FWT, :] * left

        def pair(i, dst, at):
            even, odd = (
                jnp.concatenate(
                    [fine[h, i, pl.ds(q, WT, 2), :] + fine[h, i + 1, pl.ds(q, WT, 2), :] for h in (0, 1)], axis=1
                )
                for q in (0, 1)
            )
            dst[at, :, 0:C] = (pltpu.roll(odd, 1, 0) + even)[0:W].astype(BF16)
            dst[at, :, C : 2 * C] = (even + odd)[0:W].astype(BF16)
            dst[at, :, 2 * C : 3 * C] = (odd + pltpu.roll(even, WT - 1, 0))[0:W].astype(BF16)

        def body(i, carry):
            pair(2 * i, box_a, i)
            pair(2 * i + 1, box_b, i)
            return carry

        lax.fori_loop(0, H, body, 0)
        pair(2 * H, box_a, H)

    def upper():
        up_copy.wait()

        def piece(a, b):
            at = slice(b * C, (b + 1) * C)
            if a == 1:
                return box_b[:, :, at].reshape(PIXELS, C)
            return box_a[a // 2 : a // 2 + H, :, at].reshape(PIXELS, C)

        total[tile_rows, tile_columns, :] = conv_back(piece, 6, H, W)
        for copy in total_copies():
            copy.start()

    def lift(k):
        put_taps(lambda first, rows: total[first : first + rows], T - 2, T + H + 2, WB)
        pre[...] = tap_conv_back(k, H + 2, WB)[:, 0:WT]

    def correlate(l):
        k = 2 * l
        mean = means[k + 1, 0:1, :]

        def plain_slope(first, rows):
            return slopes[k, first - 1 : first - 1 + rows]

        def normed_slope(first, rows):
            return slopes[k, first - 1 : first - 1 + rows] * normed(k, slice(first, first + rows))

        put_taps(plain_slope, T - 1, T + H + 1, W)
        put_taps(normed_slope, T - 1, T + H + 1, W, taps_n)
        x = (fields[k + 1, tile_rows, tile_columns, :] - mean.reshape(1, 1, C)).reshape(PIXELS, C).astype(BF16)
        raw = plain = None
        for b in range(3):
            at = slice(b * C, (b + 1) * C)
            sums = [jnp.sum(src[0 : H + 2, 0:W, at].astype(F32), axis=1) for src in (taps, taps_n)]
            for a in range(3):
                weight = weights[k, 3 * a + b].astype(F32).T
                weight = jnp.concatenate([weight, weight], axis=1)
                q = jnp.concatenate(
                    [src[a : a + H, 0:W, at].reshape(PIXELS, C) for src in (taps, taps_n)], axis=1
                )
                first = lax.dot_general(x, q, (((0,), (0,)), ((), ())), preferred_element_type=F32) * weight
                total_q = jnp.concatenate([jnp.sum(v[a : a + H], axis=0, keepdims=True) for v in sums], axis=1)
                second = total_q * weight
                raw = first if raw is None else raw + first
                plain = second if plain is None else plain + second
        shift = jnp.broadcast_to(mean, (8, C)).T[:, 0:1]
        raw = raw + plain * shift
        row = lax.broadcasted_iota(jnp.int32, (2 * C, 128), 0) // GROUP
        lane = lax.broadcasted_iota(jnp.int32, (2 * C, 128), 1)
        whole = None
        for j, block in enumerate((raw, plain)):
            block = jnp.sum(block.reshape(C // GROUP, GROUP, 2 * C), axis=1) * (1.0 / (PIXELS * SIDE * SIDE * GROUP))
            pick = jnp.where(lane == 64 * j + row, 1.0, 0.0).astype(F32)
            part = jnp.dot(block, pick, precision=lax.Precision.HIGHEST, preferred_element_type=F32)
            whole = part if whole is None else whole + part
        cor[...] = whole
        for i in range(SIDE):
            cor_own[l, i] = cor[2 * i : 2 * i + 2, :]
        for slot, col, row in plane:
            x, y = (col // 2) % 4, col // 8
            pltpu.make_async_remote_copy(
                src_ref=cor_own.at[l, y * 4 + x],
                dst_ref=cor_a.at[l, slot],
                send_sem=csend.at[l],
                recv_sem=crecv.at[l],
                device_id={"cols": col, "rows": row},
                device_id_type=MESH,
            ).start()

    def correlate_b(l):
        phase_wait(cor_a.at[l], crecv.at[l])
        cor_b[l, 0] = cor_own[l, place] + jnp.sum(cor_a[l, 1:SIDE], axis=0)
        phase_start(cor_b.at[l], column, csend.at[l + 3], crecv.at[l + 3])

    def correlate_c(l):
        phase_wait(cor_b.at[l], crecv.at[l + 3])
        cor_c[l, place] = jnp.sum(cor_b[l], axis=0)
        for slot, col, row in plane:
            pltpu.make_async_remote_copy(
                src_ref=cor_c.at[l, place],
                dst_ref=cor_c.at[l, place],
                send_sem=csend.at[l + 6],
                recv_sem=crecv.at[l + 6],
                device_id={"cols": col, "rows": row},
                device_id_type=MESH,
            ).start()

    def expand(l):
        phase_wait(cor_c.at[l], crecv.at[l + 6])
        for i in range(SIDE):
            cor[2 * i : 2 * i + 2, :] = cor_c[l, i]
        whole = cor[...]
        high = whole.astype(BF16)
        low = (whole - high.astype(F32)).astype(BF16)
        group = lax.broadcasted_iota(jnp.int32, (32, C), 1) // GROUP
        spread = jnp.where(lax.broadcasted_iota(jnp.int32, (32, C), 0) == group, 1.0, 0.0).astype(BF16)
        lane = lax.broadcasted_iota(jnp.int32, (128, 2 * C), 0)
        channel = lax.broadcasted_iota(jnp.int32, (128, 2 * C), 1) // GROUP
        for j in range(2):
            pick = jnp.where(lane == 64 * j + channel, 1.0, 0.0).astype(BF16)
            for part, value in enumerate((high, low)):
                block = jnp.dot(value, pick, preferred_element_type=F32).astype(BF16)
                block = lax.dot_general(spread, block, (((0,), (0,)), ((), ())), preferred_element_type=F32)
                expanded[part, j * C : (j + 1) * C, :] = block.astype(BF16)

    lane = lax.broadcasted_iota(jnp.int32, (1, 128), 1) & 7

    def chips_moments(k):
        parts = buf_a[k]
        total_row = jnp.sum(parts, axis=0, keepdims=True)
        mean = total_row * (1.0 / CHIPS)
        delta = parts - mean
        square = jnp.sum(delta * delta, axis=0, keepdims=True) * float(PIXELS * GROUP)
        return jnp.where(lane < 2, mean, jnp.where(lane < 4, total_row + pltpu.roll(square, 2, 1), 0.0))

    def finish_moments(k):
        mine, theirs = buf_b[k, 0, 0:1], buf_b[k, 1, 0:1]
        delta = mine - theirs
        square = delta * delta * float(PIXELS * GROUP * CHIPS // 2)
        both = jnp.where(lane < 2, (mine + theirs) * 0.5, mine + theirs + pltpu.roll(square, 2, 1))
        rows = unpacked(both)
        mean = rows[0:2]
        inv = lax.rsqrt(rows[2:4] * (1.0 / (PIXELS * GROUP * CHIPS * 2)) + EPS)
        mean, inv = wide(mean), wide(inv)
        stats[k, 0:1, :] = mean.reshape(1, C)
        stats[k, 1:2, :] = inv.reshape(1, C)
        return mean, inv

    def forward(k, carry):
        @pl.when(k > 0)
        def _():
            start_a(k)
            for copy in wide_copies(k - 1):
                copy.wait_recv()
            slope(k - 1, 1, RT - 1)

        @pl.when((k == 3) | (k == 5))
        def _():
            correlate_c(k // 2 - 1)

        @pl.when(k % 2 == 1)
        def _():
            correlate(k // 2)

        @pl.when((k == 2) | (k == 4))
        def _():
            correlate_b(k // 2 - 1)

        @pl.when(k == 2)
        def _():
            boxes()
            upper()

        @pl.when(k == 4)
        def _():
            weight_copy(5).wait()
            for copy in total_copies():
                copy.wait()
            lift(5)

        @pl.when(k < 5)
        def _():
            weight_copy(k).wait()

        wait_all(k, recv_a)
        swap_cores(k, chips_moments(k))
        for copy in ring_copies(k):
            copy.wait_recv()
        core_copy(k).wait_recv()
        mean, inv = finish_moments(k)

        @pl.when(k < 5)
        def _():
            def active(first, rows):
                n = (fields[k, first : first + rows] - mean) * inv
                return n * sigmoid(n)

            put_taps(active, T - 1, T + H + 1, W)
            y = conv(k)
            keep = jnp.where(k % 2 == 1, 1.0, 0.0).astype(F32)
            y = y + keep * fields[jnp.maximum(k - 1, 0), tile_rows, tile_columns, :]
            fields[k + 1, tile_rows, tile_columns, :] = y
            put_moments(k + 1, y)

        return carry

    lax.fori_loop(0, 6, forward, 0)
    slope(5, T - 1, T + H + 1)

    def drain(k, carry):
        wait_all(k, send_a)
        core_copy(k).wait_send()
        for copy in ring_copies(k) + wide_copies(k):
            copy.wait_send()
        return carry

    def drain_layer(l):
        wait_all(8 - l, send_a)
        core_copy(8 - l).wait_send()
        phase_wait(cor_a.at[l], csend.at[l])
        phase_wait(cor_b.at[l], csend.at[l + 3])
        phase_wait(cor_c.at[l], csend.at[l + 6])
        for copy in grad_copies(l, l == 0):
            copy.wait_send()

    def layer(l, last):
        k = 2 * l
        mean1, inv1 = load_stats(k)
        mean2, inv2 = load_stats(k + 1)
        t = 8 - l
        grads[l, tile_rows, tile_columns, :] = (
            pre[1 : H + 1, 0:W] * slopes[k + 1, T - 1 : T - 1 + H, 0:W]
        )
        grads_out[l] = grads[l, tile_rows, tile_columns, :].astype(BF16)
        put_sums(0, grads[l, tile_rows, tile_columns, :], normed(k + 1, tile_rows, tile_columns))

        def unprojected(first, rows):
            at = first - T + 1
            return inv2 * (pre[at : at + rows] * slopes[k + 1, first - 1 : first - 1 + rows])

        put_taps(unprojected, T - 1, T + H + 1, W)
        d = tap_conv_back(k, H, W) * slopes[k, T - 1 : T - 1 + H, 0:W]
        put_sums(4, d, normed(k, tile_rows, tile_columns))
        pack_sums(t)

        def middle():
            @pl.when(l == 2)
            def _():
                correlate_b(l)

        send_all(t, grad_copies(l, last), [], None if last else middle)

        if last:
            expand(l)
            drain_layer(2)
            drain_layer(1)
            for copy in fine_copies():
                copy.wait_send()
        else:

            @pl.when(l == 2)
            def _():
                for copy in wide_copies(5):
                    copy.wait_recv()
                correlate_c(l)

            @pl.when(l == 1)
            def _():
                expand(l)
                lax.fori_loop(0, 6, drain, 0)

        wait_all(t, recv_a)
        swap_cores(t, jnp.sum(buf_a[t], axis=0, keepdims=True) * (1.0 / CHIPS))
        for copy in grad_copies(l, last):
            copy.wait_recv()
        far = 1 if last else 3
        grads[l, T - far : T, tile_columns, :] = grads_in[l, 0, 3 - far : 3].astype(F32)
        grads[l, T + H : T + H + far, tile_columns, :] = grads_in[l, 1, 0:far].astype(F32)
        core_copy(t).wait_recv()
        sums = unpacked((buf_b[t, 0, 0:1] + buf_b[t, 1, 0:1]) * 0.5)
        first2, second2, first1_raw, second1_raw = (wide(sums[i : i + 2]) for i in (0, 2, 4, 6))
        def second_sums():
            scaled = inv2 * second2
            source = jnp.concatenate([inv2 * scaled, inv2 * (first2 - mean2 * scaled)], axis=-1).reshape(1, 2 * C)
            source = jnp.broadcast_to(source * (1.0 / GROUP), (16, 2 * C))
            high = source.astype(BF16)
            low = (source - high.astype(F32)).astype(BF16)
            moved = (
                jnp.dot(high, expanded[0], preferred_element_type=F32)
                + jnp.dot(low, expanded[0], preferred_element_type=F32)
                + jnp.dot(high, expanded[1], preferred_element_type=F32)
            )
            first1_left = first1_raw - moved[0:1, 0:C].reshape(1, 1, C)
            second1_left = second1_raw - moved[0:1, C : 2 * C].reshape(1, 1, C)
            return first1_left, second1_left

        def back(first, rows):
            at = slice(first, first + rows)
            return inv2 * (grads[l, at] - first2 - normed(k + 1, at) * second2)

        if last:
            put_taps(back, T - 1, T + H + 1, W)
            d = tap_conv_back(k, H, W) * slopes[k, T - 1 : T - 1 + H, 0:W]
            n = normed(k, tile_rows, tile_columns)
            first1, second1 = second_sums()
            out[...] = total[tile_rows, tile_columns, :] + inv1 * (d - first1 - n * second1)
        else:
            put_taps(back, 0, RT, WB)
            d = tap_conv_back(k, H + 4, WB)[:, 0:WT] * slopes[k]
            rows = slice(T - 2, T + H + 2)

            @pl.when(l == 2)
            def _():
                expand(l)

            first1, second1 = second_sums()
            total[rows] += inv1 * (d - first1 - normed(k, rows) * second1)
            lift(k - 1)

    def backward(j, carry):
        layer(2 - j, False)
        return carry

    lax.fori_loop(0, 2, backward, 0)
    layer(0, True)

    drain_layer(0)


def per_device(latent, cotangent, pixel_mask, res_kernels, up_kernel):
    vmem = pl.BlockSpec(memory_space=pltpu.VMEM)
    hbm = pl.BlockSpec(memory_space=pl.ANY)
    dma = pltpu.SemaphoreType.DMA
    return pl.pallas_call(
        kernel,
        out_shape=jax.ShapeDtypeStruct((H, W, C), F32),
        in_specs=[vmem, hbm, hbm, hbm, hbm],
        out_specs=vmem,
        scratch_shapes=[
            pltpu.VMEM((H, W, C), BF16),
            pltpu.VMEM((FH, FW, C), BF16),
            pltpu.VMEM((7, 9, C, C), BF16),
            pltpu.VMEM((6, RT, WT, C), F32),
            pltpu.VMEM((3, RT, WT, C), F32),
            pltpu.VMEM((3, H, W, C), BF16),
            pltpu.VMEM((3, 2, 3, W, C), BF16),
            pltpu.VMEM((RT, WT, C), F32),
            pltpu.VMEM((H + 2, WT, C), F32),
            pltpu.VMEM((2, FH + 2, FWT, 128), F32),
            pltpu.VMEM((2, FW, C), BF16),
            pltpu.VMEM((2, FW, C), BF16),
            pltpu.VMEM((6, RT - 2, WT, C), F32),
            pltpu.VMEM((6, 8, C), F32),
            pltpu.VMEM((RT, WB, 3 * C), BF16),
            pltpu.VMEM((H + 2, W, 3 * C), BF16),
            pltpu.VMEM((H + 1, W, 3 * C), BF16),
            pltpu.VMEM((H, W, 3 * C), BF16),
            pltpu.VMEM((9, CHIPS, 128), F32),
            pltpu.VMEM((9, 2, 8, 128), F32),
            pltpu.VMEM((8, 128), F32),
            pltpu.VMEM((6, 8, C), F32),
            pltpu.VMEM((3, SIDE, 2, 128), F32),
            pltpu.VMEM((3, SIDE, 2, 128), F32),
            pltpu.VMEM((3, SIDE, 2, 128), F32),
            pltpu.VMEM((3, SIDE, 2, 128), F32),
            pltpu.VMEM((32, 128), F32),
            pltpu.VMEM((2, 2 * C, 2 * C), BF16),
            dma((9,)),
            dma((9,)),
            dma((9,)),
            dma((9,)),
            dma((9,)),
            dma((9,)),
            dma((9,)),
            dma((17, 8)),
            dma((17, 8)),
        ],
        compiler_params=pltpu.CompilerParams(
            collective_id=0, has_side_effects=True, vmem_limit_bytes=56 * 2**20
        ),
    )(
        pixel_mask,
        latent,
        cotangent,
        res_kernels.reshape(6, 9, C, C),
        up_kernel.reshape(9, C, C),
    )


def solution(mesh):
    in_specs = (P("rows", "cols", None), P("rows", "cols", None), P("rows", "cols"), P(), P())
    out_specs = P("rows", "cols", None)
    return jax.shard_map(
        per_device, mesh=mesh, in_specs=in_specs, out_specs=out_specs, check_vma=False
    )
```

```python
import functools

import jax
import jax.numpy as jnp
from jax import lax
from jax.experimental import pallas as pl
from jax.experimental.pallas import tpu as pltpu
from jax.sharding import PartitionSpec as P

LAYERS = 3
EPS = 1e-06
MESH = pl.DeviceIdType.MESH
F32 = jnp.float32
BF16 = jnp.bfloat16

H, W, C = 8, 64, 256
T = 3
RT = H + 2 * T
WT = W + 8
WB = W + 16
FH, FW = 2 * H, 2 * W
FWT = FW + 16
SIDE = 16
CHIPS = 128
PIXELS = H * W
GROUP = 8


def position():
    c = lax.axis_index("cols")
    r = lax.axis_index("rows")
    core = c % 2
    chip = c // 2
    return c, r, core, chip % 4, chip // 4


def plane_peers():
    c, r, core, x, y = position()
    out = []
    for dy in range(4):
        for dx in range(4):
            if dx or dy:
                far = min(dx, 4 - dx) + min(dy, 4 - dy)
                out.append((far, dy * 4 + dx, (((y + dy) % 4) * 4 + (x + dx) % 4) * 2 + core, r))
    return [p[1:] for p in sorted(out, key=lambda p: -p[0])]


def column_peers():
    c, r, core, x, y = position()
    out = []
    for dz in range(8):
        for dc in range(2):
            if dz or dc:
                far = min(dz, 8 - dz)
                out.append((far, dz * 2 + dc, c - core + (core + dc) % 2, (r + dz) % 8))
    return [p[1:] for p in sorted(out, key=lambda p: -p[0])]


def other_core():
    c, r, core, x, y = position()
    return c - core + (core + 1) % 2, r


def chip_peers(visit, middle=None):
    c, r, core, x, y = position()
    plane = [(0, c, r)] + plane_peers()[::-1]

    def level(i, carry):
        dz = jnp.where(i % 2 == 0, 4 + i // 2, 4 - (i + 1) // 2)
        row = (r + dz) % 8
        for slot, col, _ in plane[::-1]:
            visit(dz * SIDE + slot, col, row)
        return carry

    lax.fori_loop(0, 4, level, 0)
    if middle is not None:
        middle()
    lax.fori_loop(4, 7, level, 0)


def neighbours():
    c, r, core, x, y = position()
    out = []
    for dr in (-1, 0, 1):
        for dc in (-1, 0, 1):
            if dr or dc:
                out.append((dr, dc, (c + dc + 32) % 32, (r + dr + 8) % 8))
    return out


def halo_copies(field, rows, columns, corners, send, recv, top=T, height=H, width=W, total=WT):
    def spans(step, first, size, end, near, far):
        n = far - near + 1
        if step < 0:
            return pl.ds(first + near - 1, n), pl.ds(first + size + near - 1, n)
        if step > 0:
            return pl.ds(first + size - far, n), pl.ds(end - far, n)
        return pl.ds(first, size), pl.ds(first, size)

    copies = []
    for dr, dc, col, row in neighbours():
        band = corners if dr and dc else (rows if dr else columns)
        if band is None:
            continue
        src_r, dst_r = spans(dr, top, height, top, *band)
        src_c, dst_c = spans(dc, 0, width, total, *band)
        src, dst = (src_r, src_c, slice(None)), (dst_r, dst_c, slice(None))
        if len(field.shape) == 4:
            src, dst = (slice(None),) + src, (slice(None),) + dst
        copies.append(
            pltpu.make_async_remote_copy(
                src_ref=field.at[src],
                dst_ref=field.at[dst],
                send_sem=send.at[len(copies)],
                recv_sem=recv.at[len(copies)],
                device_id={"cols": col, "rows": row},
                device_id_type=MESH,
            )
        )
    return copies


def phase_start(buf, peers, send, recv):
    for slot, col, row in peers:
        pltpu.make_async_remote_copy(
            src_ref=buf.at[0],
            dst_ref=buf.at[slot],
            send_sem=send,
            recv_sem=recv,
            device_id={"cols": col, "rows": row},
            device_id_type=MESH,
        ).start()


def phase_wait(buf, sem):
    pltpu.make_async_copy(buf.at[pl.ds(1, SIDE - 1)], buf.at[pl.ds(1, SIDE - 1)], sem).wait()


def lane_swap(value, step):
    lane = lax.broadcasted_iota(jnp.int32, value.shape, 1)
    return jnp.where((lane & step) != 0, pltpu.roll(value, step, 1), pltpu.roll(value, 128 - step, 1))


def own_lanes():
    lane = lax.broadcasted_iota(jnp.int32, (8, 128), 1)
    return (lane & 7) == lax.broadcasted_iota(jnp.int32, (8, 128), 0)


def packed(rows):
    return jnp.sum(jnp.where(own_lanes(), rows, 0.0), axis=0, keepdims=True)


def unpacked(row):
    rows = jnp.where(own_lanes(), jnp.broadcast_to(row, (8, 128)), 0.0)
    for step in (1, 2, 4):
        rows = rows + lane_swap(rows, step)
    return rows


def wide(value):
    return jnp.concatenate([value[0:1], value[1:2]], axis=1).reshape(1, 1, C)


def sigmoid(v):
    return 1.0 / (1.0 + jnp.exp(-v))


def kernel(
    mask_hbm, latent_hbm, cot_hbm, res_hbm, up_hbm, out_hbm,
    mask, out, latent, cot, weights, fields, grads, grads_out, grads_in, total, pre, fine, rows_out, rows_in, slopes, stats, taps, taps_n, box_a, box_b,
    buf_a, buf_b, lines, means, cor_own, cor_a, cor_b, cor_c, cor, expanded,
    load_sem, send_a, send_b, recv_a, recv_b, csend, crecv, hsend, hrecv,
):
    c, r, _, px, py = position()
    place = py * 4 + px
    top = jnp.where(r == 0, 0.0, 1.0).astype(F32)
    bottom = jnp.where(r == 7, 0.0, 1.0).astype(F32)
    left = jnp.where(c == 0, 0.0, 1.0).astype(F32)
    right = jnp.where(c == 31, 0.0, 1.0).astype(F32)
    side = lax.broadcasted_iota(jnp.int32, (1, 8, C), 1)
    edge = jnp.where(side < 4, right, left)

    def weight_copy(k):
        return pltpu.make_async_copy(res_hbm.at[k], weights.at[k], load_sem.at[k])

    up_copy = pltpu.make_async_copy(up_hbm, weights.at[6], load_sem.at[6])
    cot_copy = pltpu.make_async_copy(cot_hbm, cot, load_sem.at[7])
    mask_copy = pltpu.make_async_copy(mask_hbm, mask, load_sem.at[9])
    out_copy = pltpu.make_async_copy(out, out_hbm, load_sem.at[10])
    latent_copy = pltpu.make_async_copy(latent_hbm, latent, load_sem.at[8])
    latent_copy.start()
    barrier = pltpu.get_barrier_semaphore()
    plane, column = plane_peers(), column_peers()

    def greet(slot, col, row):
        pl.semaphore_signal(barrier, inc=1, device_id={"cols": col, "rows": row}, device_id_type=MESH)

    chip_peers(greet)
    greeted = plane + [p for p in column if p[0] % 2 == 1] + [(0,) + p[2:] for p in neighbours()]
    for peer in greeted:
        greet(*peer)

    mask_copy.start()
    cot_copy.start()
    weight_copy(0).start()
    up_copy.start()
    for k in range(1, 6):
        weight_copy(k).start()

    def load_stats(k):
        return stats[k, 0:1, :].reshape(1, 1, C), stats[k, 1:2, :].reshape(1, 1, C)

    def normed(k, rows, columns=slice(0, WT)):
        mean, inv = load_stats(k)
        return (fields[k, rows, columns, :] - mean) * inv

    tile_rows, tile_columns = slice(T, T + H), slice(0, W)

    def put_rows(buf, at, first, second):
        buf[at : at + 1, :] = first[:, 0:128]
        buf[at + 1 : at + 2, :] = first[:, 128:256]
        buf[at + 2 : at + 3, :] = second[:, 0:128]
        buf[at + 3 : at + 4, :] = second[:, 128:256]

    def put_moments(k, x):
        mean = jnp.sum(x, axis=(0, 1)).reshape(1, C) * (1.0 / PIXELS)
        delta = x - mean.reshape(1, 1, C)
        square = jnp.sum(delta * delta, axis=(0, 1)).reshape(1, C)
        means[k, 0:1, :] = mean
        put_rows(lines, 0, mean, square)
        mean, square = lines[0:2], lines[2:4]
        count = float(PIXELS)
        for step in (1, 2, 4):
            other, squares = lane_swap(mean, step), lane_swap(square, step)
            delta = mean - other
            mean = (mean + other) * 0.5
            square = square + squares + delta * delta * (count * 0.5)
            count *= 2.0
        lines[0:2] = mean
        lines[2:4] = square
        lines[4:8] = jnp.zeros((4, 128), F32)
        buf_a[k, 0:1, :] = packed(lines[...])

    def put_sums(at, d, n):
        first = jnp.sum(d, axis=(0, 1)).reshape(1, C) * (1.0 / PIXELS)
        second = jnp.sum(d * n, axis=(0, 1)).reshape(1, C) * (1.0 / PIXELS)
        put_rows(lines, at, first, second)

    def pack_sums(t):
        rows = lines[...]
        for step in (1, 2, 4):
            rows = rows + lane_swap(rows, step)
        buf_a[t, 0:1, :] = packed(rows * (1.0 / GROUP))

    def send_all(t, first, then, middle=None):
        def send(slot, col, row):
            pltpu.make_async_remote_copy(
                src_ref=buf_a.at[t, pl.ds(0, 1)],
                dst_ref=buf_a.at[t, pl.ds(slot, 1)],
                send_sem=send_a.at[t],
                recv_sem=recv_a.at[t],
                device_id={"cols": col, "rows": row},
                device_id_type=MESH,
            ).start()

        chip_peers(send, middle)
        for copy in first:
            copy.start()
        for peer in plane:
            send(*peer)
        for copy in then:
            copy.start()

    def wait_all(t, sem):
        part = buf_a.at[t, pl.ds(1, CHIPS - 1)]
        pltpu.make_async_copy(part, part, sem.at[t]).wait()

    def core_copy(t):
        col, row = other_core()
        return pltpu.make_async_remote_copy(
            src_ref=buf_b.at[t, 0],
            dst_ref=buf_b.at[t, 1],
            send_sem=send_b.at[t],
            recv_sem=recv_b.at[t],
            device_id={"cols": col, "rows": row},
            device_id_type=MESH,
        )

    def swap_cores(t, row):
        buf_b[t, 0] = jnp.broadcast_to(row, (8, 128))
        core_copy(t).start()

    def ring_copies(k):
        return halo_copies(fields.at[k], (1, 1), (1, 3), (1, 3), hsend.at[k], hrecv.at[k])

    def wide_copies(k):
        return halo_copies(fields.at[k], (2, 3), None, None, hsend.at[k + 6], hrecv.at[k + 6])

    def grad_copies(l, last):
        far = 1 if last else 3
        copies = halo_copies(grads.at[l], None, (1, far), (1, far), hsend.at[l + 12], hrecv.at[l + 12])
        c, r, _, _, _ = position()
        for i, (first, dst_first) in enumerate(((0, 0), (H - far, 3 - far))):
            copies.append(
                pltpu.make_async_remote_copy(
                    src_ref=grads_out.at[l, pl.ds(first, far)],
                    dst_ref=grads_in.at[l, 1 - i, pl.ds(dst_first, far)],
                    send_sem=hsend.at[l + 12, 6 + i],
                    recv_sem=hrecv.at[l + 12, 6 + i],
                    device_id={"cols": c, "rows": (r + 2 * i + 7) % 8},
                    device_id_type=MESH,
                )
            )
        return copies

    def total_copies():
        return halo_copies(total, (1, 2), (1, 2), (1, 2), hsend.at[15], hrecv.at[15])

    def fine_copies():
        copies = []
        for i, (dr, dc, col, row) in enumerate(neighbours()):
            if dc == 0:
                src, dst = rows_out.at[max(dr, 0)], rows_in.at[max(-dr, 0)]
            else:
                src_r = pl.ds(1, FH) if dr == 0 else (pl.ds(1, 1) if dr < 0 else pl.ds(FH, 1))
                dst_r = pl.ds(1, FH) if dr == 0 else (pl.ds(FH + 1, 1) if dr < 0 else pl.ds(0, 1))
                src = fine.at[:, src_r, pl.ds(0 if dc < 0 else FW - 1, 1), :]
                dst = fine.at[:, dst_r, pl.ds(FW if dc < 0 else FWT - 1, 1), :]
            copies.append(
                pltpu.make_async_remote_copy(
                    src_ref=src,
                    dst_ref=dst,
                    send_sem=hsend.at[16, i],
                    recv_sem=hrecv.at[16, i],
                    device_id={"cols": col, "rows": row},
                    device_id_type=MESH,
                )
            )
        return copies

    def put_taps(make, first, last, columns, dst=taps):
        parts = ((first, T, top), (T, T + H, None), (T + H, last, bottom))
        for begin, end, scale in parts:
            u = make(begin, end - begin)
            if scale is not None:
                u = u * scale
            u = jnp.concatenate([u[:, 0:W], u[:, W:WT] * edge], axis=1)
            at = slice(begin - first, end - first)
            for b, v in enumerate((pltpu.roll(u, 1, 1), u, pltpu.roll(u, WT - 1, 1))):
                if columns > WT:
                    v = jnp.concatenate([v, jnp.zeros((end - begin, columns - WT, C), F32)], axis=1)
                dst[at, 0:columns, b * C : (b + 1) * C] = v[:, 0:columns].astype(BF16)

    def conv(k):
        rows = [taps[a : a + H, 0:W].reshape(PIXELS, 3 * C) for a in range(3)]
        y = jnp.dot(jnp.concatenate(rows, axis=-1), weights[k].reshape(9 * C, C), preferred_element_type=F32)
        return y.reshape(H, W, C)

    def conv_back(piece, k, rows, columns):
        y = None
        for a in range(3):
            for b in range(3):
                d = lax.dot_general(
                    piece(a, b), weights[k, 8 - 3 * a - b], (((1,), (1,)), ((), ())), preferred_element_type=F32
                )
                y = d if y is None else y + d
        return y.reshape(rows, columns, C)

    def tap_conv_back(k, rows, columns):
        parts = []
        chunks = 1 if rows * columns <= PIXELS else 2
        height = rows // chunks
        for begin in range(0, rows, height):

            def piece(a, b):
                at = slice(begin + a, begin + a + height)
                return taps[at, 0:columns, b * C : (b + 1) * C].reshape(height * columns, C)

            parts.append(conv_back(piece, k, height, columns))
        return parts[0] if chunks == 1 else jnp.concatenate(parts, axis=0)

    latent_copy.wait()
    fields[0, tile_rows, tile_columns, :] = latent[...].astype(F32)
    put_moments(0, latent[...].astype(F32))

    def start_a(k):
        send_all(k, ring_copies(k), wide_copies(k))

    pl.semaphore_wait(barrier, CHIPS - SIDE + len(greeted))
    send_all(0, ring_copies(0), wide_copies(0))
    mask_copy.wait()
    cot_copy.wait()

    def mask_row(i, carry):
        row = jnp.broadcast_to(mask[pl.ds(i, 1), :].astype(F32), (FW, FW)).T
        fine[0, i + 1, 0:FW, :] = cot[i, :, 0:128].astype(F32) * row
        fine[1, i + 1, 0:FW, :] = cot[i, :, 128:256].astype(F32) * row
        return carry

    lax.fori_loop(0, FH, mask_row, 0)
    for i, at in enumerate((1, FH)):
        rows_out[i] = jnp.concatenate([fine[0, at, 0:FW, :], fine[1, at, 0:FW, :]], axis=1).astype(BF16)
    for copy in fine_copies():
        copy.start()

    def slope(k, first, last):
        n = normed(k, slice(first, last))
        s = sigmoid(n)
        slopes[k, first - 1 : last - 1] = s * (1.0 + n * (1.0 - s))

    def boxes():
        for copy in fine_copies():
            copy.wait_recv()
        for i, (at, scale) in enumerate(((0, top), (FH + 1, bottom))):
            edge_row = rows_in[i].astype(F32) * scale
            fine[0, at, 0:FW, :] = edge_row[:, 0:128]
            fine[1, at, 0:FW, :] = edge_row[:, 128:256]
            fine[:, at, FW:FWT, :] = fine[:, at, FW:FWT, :] * scale
        fine[:, :, FW : FW + 8, :] = fine[:, :, FW : FW + 8, :] * right
        fine[:, :, FWT - 8 : FWT, :] = fine[:, :, FWT - 8 : FWT, :] * left

        def pair(i, dst, at):
            even, odd = (
                jnp.concatenate(
                    [fine[h, i, pl.ds(q, WT, 2), :] + fine[h, i + 1, pl.ds(q, WT, 2), :] for h in (0, 1)], axis=1
                )
                for q in (0, 1)
            )
            dst[at, :, 0:C] = (pltpu.roll(odd, 1, 0) + even)[0:W].astype(BF16)
            dst[at, :, C : 2 * C] = (even + odd)[0:W].astype(BF16)
            dst[at, :, 2 * C : 3 * C] = (odd + pltpu.roll(even, WT - 1, 0))[0:W].astype(BF16)

        def body(i, carry):
            pair(2 * i, box_a, i)
            pair(2 * i + 1, box_b, i)
            return carry

        lax.fori_loop(0, H, body, 0)
        pair(2 * H, box_a, H)

    def upper():
        up_copy.wait()

        def piece(a, b):
            at = slice(b * C, (b + 1) * C)
            if a == 1:
                return box_b[:, :, at].reshape(PIXELS, C)
            return box_a[a // 2 : a // 2 + H, :, at].reshape(PIXELS, C)

        total[tile_rows, tile_columns, :] = conv_back(piece, 6, H, W)
        for copy in total_copies():
            copy.start()

    def lift(k):
        put_taps(lambda first, rows: total[first : first + rows], T - 2, T + H + 2, WB)
        pre[...] = tap_conv_back(k, H + 2, WB)[:, 0:WT]

    def correlate(l):
        k = 2 * l
        mean = means[k + 1, 0:1, :]

        def plain_slope(first, rows):
            return slopes[k, first - 1 : first - 1 + rows]

        def normed_slope(first, rows):
            return slopes[k, first - 1 : first - 1 + rows] * normed(k, slice(first, first + rows))

        put_taps(plain_slope, T - 1, T + H + 1, W)
        put_taps(normed_slope, T - 1, T + H + 1, W, taps_n)
        x = (fields[k + 1, tile_rows, tile_columns, :] - mean.reshape(1, 1, C)).reshape(PIXELS, C).astype(BF16)
        raw = plain = None
        for b in range(3):
            at = slice(b * C, (b + 1) * C)
            sums = [jnp.sum(src[0 : H + 2, 0:W, at].astype(F32), axis=1) for src in (taps, taps_n)]
            for a in range(3):
                weight = weights[k, 3 * a + b].astype(F32).T
                weight = jnp.concatenate([weight, weight], axis=1)
                q = jnp.concatenate(
                    [src[a : a + H, 0:W, at].reshape(PIXELS, C) for src in (taps, taps_n)], axis=1
                )
                first = lax.dot_general(x, q, (((0,), (0,)), ((), ())), preferred_element_type=F32) * weight
                total_q = jnp.concatenate([jnp.sum(v[a : a + H], axis=0, keepdims=True) for v in sums], axis=1)
                second = total_q * weight
                raw = first if raw is None else raw + first
                plain = second if plain is None else plain + second
        shift = jnp.broadcast_to(mean, (8, C)).T[:, 0:1]
        raw = raw + plain * shift
        row = lax.broadcasted_iota(jnp.int32, (2 * C, 128), 0) // GROUP
        lane = lax.broadcasted_iota(jnp.int32, (2 * C, 128), 1)
        whole = None
        for j, block in enumerate((raw, plain)):
            block = jnp.sum(block.reshape(C // GROUP, GROUP, 2 * C), axis=1) * (1.0 / (PIXELS * SIDE * SIDE * GROUP))
            pick = jnp.where(lane == 64 * j + row, 1.0, 0.0).astype(F32)
            part = jnp.dot(block, pick, precision=lax.Precision.HIGHEST, preferred_element_type=F32)
            whole = part if whole is None else whole + part
        cor[...] = whole
        for i in range(SIDE):
            cor_own[l, i] = cor[2 * i : 2 * i + 2, :]
        for slot, col, row in plane:
            x, y = (col // 2) % 4, col // 8
            pltpu.make_async_remote_copy(
                src_ref=cor_own.at[l, y * 4 + x],
                dst_ref=cor_a.at[l, slot],
                send_sem=csend.at[l],
                recv_sem=crecv.at[l],
                device_id={"cols": col, "rows": row},
                device_id_type=MESH,
            ).start()

    def correlate_b(l):
        phase_wait(cor_a.at[l], crecv.at[l])
        cor_b[l, 0] = cor_own[l, place] + jnp.sum(cor_a[l, 1:SIDE], axis=0)
        phase_start(cor_b.at[l], column, csend.at[l + 3], crecv.at[l + 3])

    def correlate_c(l):
        phase_wait(cor_b.at[l], crecv.at[l + 3])
        cor_c[l, place] = jnp.sum(cor_b[l], axis=0)
        for slot, col, row in plane:
            pltpu.make_async_remote_copy(
                src_ref=cor_c.at[l, place],
                dst_ref=cor_c.at[l, place],
                send_sem=csend.at[l + 6],
                recv_sem=crecv.at[l + 6],
                device_id={"cols": col, "rows": row},
                device_id_type=MESH,
            ).start()

    def expand(l):
        phase_wait(cor_c.at[l], crecv.at[l + 6])
        for i in range(SIDE):
            cor[2 * i : 2 * i + 2, :] = cor_c[l, i]
        whole = cor[...]
        high = whole.astype(BF16)
        low = (whole - high.astype(F32)).astype(BF16)
        group = lax.broadcasted_iota(jnp.int32, (32, C), 1) // GROUP
        spread = jnp.where(lax.broadcasted_iota(jnp.int32, (32, C), 0) == group, 1.0, 0.0).astype(BF16)
        lane = lax.broadcasted_iota(jnp.int32, (128, 2 * C), 0)
        channel = lax.broadcasted_iota(jnp.int32, (128, 2 * C), 1) // GROUP
        for j in range(2):
            pick = jnp.where(lane == 64 * j + channel, 1.0, 0.0).astype(BF16)
            for part, value in enumerate((high, low)):
                block = jnp.dot(value, pick, preferred_element_type=F32).astype(BF16)
                block = lax.dot_general(spread, block, (((0,), (0,)), ((), ())), preferred_element_type=F32)
                expanded[part, j * C : (j + 1) * C, :] = block.astype(BF16)

    lane = lax.broadcasted_iota(jnp.int32, (1, 128), 1) & 7

    def chips_moments(k):
        parts = buf_a[k]
        total_row = jnp.sum(parts, axis=0, keepdims=True)
        mean = total_row * (1.0 / CHIPS)
        delta = parts - mean
        square = jnp.sum(delta * delta, axis=0, keepdims=True) * float(PIXELS * GROUP)
        return jnp.where(lane < 2, mean, jnp.where(lane < 4, total_row + pltpu.roll(square, 2, 1), 0.0))

    def finish_moments(k):
        mine, theirs = buf_b[k, 0, 0:1], buf_b[k, 1, 0:1]
        delta = mine - theirs
        square = delta * delta * float(PIXELS * GROUP * CHIPS // 2)
        both = jnp.where(lane < 2, (mine + theirs) * 0.5, mine + theirs + pltpu.roll(square, 2, 1))
        rows = unpacked(both)
        mean = rows[0:2]
        inv = lax.rsqrt(rows[2:4] * (1.0 / (PIXELS * GROUP * CHIPS * 2)) + EPS)
        mean, inv = wide(mean), wide(inv)
        stats[k, 0:1, :] = mean.reshape(1, C)
        stats[k, 1:2, :] = inv.reshape(1, C)
        return mean, inv

    def forward(k, carry):
        @pl.when(k > 0)
        def _():
            start_a(k)
            for copy in wide_copies(k - 1):
                copy.wait_recv()
            slope(k - 1, 1, RT - 1)

        @pl.when((k == 3) | (k == 5))
        def _():
            correlate_c(k // 2 - 1)

        @pl.when(k % 2 == 1)
        def _():
            correlate(k // 2)

        @pl.when((k == 2) | (k == 4))
        def _():
            correlate_b(k // 2 - 1)

        @pl.when(k == 2)
        def _():
            boxes()
            upper()

        @pl.when(k == 4)
        def _():
            weight_copy(5).wait()
            for copy in total_copies():
                copy.wait()
            lift(5)

        @pl.when(k < 5)
        def _():
            weight_copy(k).wait()

        wait_all(k, recv_a)
        swap_cores(k, chips_moments(k))
        for copy in ring_copies(k):
            copy.wait_recv()
        core_copy(k).wait_recv()
        mean, inv = finish_moments(k)

        @pl.when(k < 5)
        def _():
            def active(first, rows):
                n = (fields[k, first : first + rows] - mean) * inv
                return n * sigmoid(n)

            put_taps(active, T - 1, T + H + 1, W)
            y = conv(k)
            keep = jnp.where(k % 2 == 1, 1.0, 0.0).astype(F32)
            y = y + keep * fields[jnp.maximum(k - 1, 0), tile_rows, tile_columns, :]
            fields[k + 1, tile_rows, tile_columns, :] = y
            put_moments(k + 1, y)

        return carry

    lax.fori_loop(0, 6, forward, 0)
    slope(5, T - 1, T + H + 1)

    def drain(k, carry):
        wait_all(k, send_a)
        core_copy(k).wait_send()
        for copy in ring_copies(k) + wide_copies(k):
            copy.wait_send()
        return carry

    def drain_layer(l):
        wait_all(8 - l, send_a)
        core_copy(8 - l).wait_send()
        phase_wait(cor_a.at[l], csend.at[l])
        phase_wait(cor_b.at[l], csend.at[l + 3])
        phase_wait(cor_c.at[l], csend.at[l + 6])
        for copy in grad_copies(l, l == 0):
            copy.wait_send()

    def layer(l, last):
        k = 2 * l
        mean1, inv1 = load_stats(k)
        mean2, inv2 = load_stats(k + 1)
        t = 8 - l
        grads[l, tile_rows, tile_columns, :] = (
            pre[1 : H + 1, 0:W] * slopes[k + 1, T - 1 : T - 1 + H, 0:W]
        )
        grads_out[l] = grads[l, tile_rows, tile_columns, :].astype(BF16)
        put_sums(0, grads[l, tile_rows, tile_columns, :], normed(k + 1, tile_rows, tile_columns))

        def unprojected(first, rows):
            at = first - T + 1
            return inv2 * (pre[at : at + rows] * slopes[k + 1, first - 1 : first - 1 + rows])

        put_taps(unprojected, T - 1, T + H + 1, W)
        d = tap_conv_back(k, H, W) * slopes[k, T - 1 : T - 1 + H, 0:W]
        put_sums(4, d, normed(k, tile_rows, tile_columns))
        pack_sums(t)

        def middle():
            @pl.when(l == 2)
            def _():
                correlate_b(l)

        send_all(t, grad_copies(l, last), [], None if last else middle)

        if last:
            expand(l)
            drain_layer(2)
            drain_layer(1)
            for copy in fine_copies():
                copy.wait_send()
        else:

            @pl.when(l == 2)
            def _():
                for copy in wide_copies(5):
                    copy.wait_recv()
                correlate_c(l)

            @pl.when(l == 1)
            def _():
                expand(l)
                lax.fori_loop(0, 6, drain, 0)

        wait_all(t, recv_a)
        swap_cores(t, jnp.sum(buf_a[t], axis=0, keepdims=True) * (1.0 / CHIPS))
        for copy in grad_copies(l, last):
            copy.wait_recv()
        far = 1 if last else 3
        grads[l, T - far : T, tile_columns, :] = grads_in[l, 0, 3 - far : 3].astype(F32)
        grads[l, T + H : T + H + far, tile_columns, :] = grads_in[l, 1, 0:far].astype(F32)
        core_copy(t).wait_recv()
        sums = unpacked((buf_b[t, 0, 0:1] + buf_b[t, 1, 0:1]) * 0.5)
        first2, second2, first1_raw, second1_raw = (wide(sums[i : i + 2]) for i in (0, 2, 4, 6))
        def second_sums():
            scaled = inv2 * second2
            source = jnp.concatenate([inv2 * scaled, inv2 * (first2 - mean2 * scaled)], axis=-1).reshape(1, 2 * C)
            source = jnp.broadcast_to(source * (1.0 / GROUP), (16, 2 * C))
            high = source.astype(BF16)
            low = (source - high.astype(F32)).astype(BF16)
            moved = (
                jnp.dot(high, expanded[0], preferred_element_type=F32)
                + jnp.dot(low, expanded[0], preferred_element_type=F32)
                + jnp.dot(high, expanded[1], preferred_element_type=F32)
            )
            first1_left = first1_raw - moved[0:1, 0:C].reshape(1, 1, C)
            second1_left = second1_raw - moved[0:1, C : 2 * C].reshape(1, 1, C)
            return first1_left, second1_left

        def back(first, rows):
            at = slice(first, first + rows)
            return inv2 * (grads[l, at] - first2 - normed(k + 1, at) * second2)

        if last:
            put_taps(back, T - 1, T + H + 1, W)
            d = tap_conv_back(k, H, W) * slopes[k, T - 1 : T - 1 + H, 0:W]
            n = normed(k, tile_rows, tile_columns)
            first1, second1 = second_sums()
            out[...] = total[tile_rows, tile_columns, :] + inv1 * (d - first1 - n * second1)
        else:
            put_taps(back, 0, RT, WB)
            d = tap_conv_back(k, H + 4, WB)[:, 0:WT] * slopes[k]
            rows = slice(T - 2, T + H + 2)

            @pl.when(l == 2)
            def _():
                expand(l)

            first1, second1 = second_sums()
            total[rows] += inv1 * (d - first1 - normed(k, rows) * second1)
            lift(k - 1)

    def backward(j, carry):
        layer(2 - j, False)
        return carry

    lax.fori_loop(0, 2, backward, 0)
    layer(0, True)

    out_copy.start()
    drain_layer(0)
    out_copy.wait()


def per_device(latent, cotangent, pixel_mask, res_kernels, up_kernel):
    hbm = pl.BlockSpec(memory_space=pl.ANY)
    dma = pltpu.SemaphoreType.DMA
    return pl.pallas_call(
        kernel,
        out_shape=jax.ShapeDtypeStruct((H, W, C), F32),
        in_specs=[hbm, hbm, hbm, hbm, hbm],
        out_specs=hbm,
        scratch_shapes=[
            pltpu.VMEM((FH, FW), jnp.int32),
            pltpu.VMEM((H, W, C), F32),
            pltpu.VMEM((H, W, C), BF16),
            pltpu.VMEM((FH, FW, C), BF16),
            pltpu.VMEM((7, 9, C, C), BF16),
            pltpu.VMEM((6, RT, WT, C), F32),
            pltpu.VMEM((3, RT, WT, C), F32),
            pltpu.VMEM((3, H, W, C), BF16),
            pltpu.VMEM((3, 2, 3, W, C), BF16),
            pltpu.VMEM((RT, WT, C), F32),
            pltpu.VMEM((H + 2, WT, C), F32),
            pltpu.VMEM((2, FH + 2, FWT, 128), F32),
            pltpu.VMEM((2, FW, C), BF16),
            pltpu.VMEM((2, FW, C), BF16),
            pltpu.VMEM((6, RT - 2, WT, C), F32),
            pltpu.VMEM((6, 8, C), F32),
            pltpu.VMEM((RT, WB, 3 * C), BF16),
            pltpu.VMEM((H + 2, W, 3 * C), BF16),
            pltpu.VMEM((H + 1, W, 3 * C), BF16),
            pltpu.VMEM((H, W, 3 * C), BF16),
            pltpu.VMEM((9, CHIPS, 128), F32),
            pltpu.VMEM((9, 2, 8, 128), F32),
            pltpu.VMEM((8, 128), F32),
            pltpu.VMEM((6, 8, C), F32),
            pltpu.VMEM((3, SIDE, 2, 128), F32),
            pltpu.VMEM((3, SIDE, 2, 128), F32),
            pltpu.VMEM((3, SIDE, 2, 128), F32),
            pltpu.VMEM((3, SIDE, 2, 128), F32),
            pltpu.VMEM((32, 128), F32),
            pltpu.VMEM((2, 2 * C, 2 * C), BF16),
            dma((11,)),
            dma((9,)),
            dma((9,)),
            dma((9,)),
            dma((9,)),
            dma((9,)),
            dma((9,)),
            dma((17, 8)),
            dma((17, 8)),
        ],
        compiler_params=pltpu.CompilerParams(
            collective_id=0, has_side_effects=True, vmem_limit_bytes=56 * 2**20
        ),
    )(
        pixel_mask,
        latent,
        cotangent,
        res_kernels.reshape(6, 9, C, C),
        up_kernel.reshape(9, C, C),
    )


def solution(mesh):
    in_specs = (P("rows", "cols", None), P("rows", "cols", None), P("rows", "cols"), P(), P())
    out_specs = P("rows", "cols", None)
    return jax.shard_map(
        per_device, mesh=mesh, in_specs=in_specs, out_specs=out_specs, check_vma=False
    )
```
